32 devices in a mesh: dp: 2 (over core), heads: 4 (over y, x), tensor: 4 (over z).
Axes of the slice: x: 2, y: 2, z: 4, core: 2. Of those that a mesh axis runs over, the one named last changes fastest.
Arguments:
- images_in: bfloat16 [3152, 512], P(('dp', 'tensor')), may hold values from -6 to 6
- attn_weights: float32 [4, 512, 512], P('tensor', 'dp', 'heads')
- attn_momentum: float32 [4, 512, 512], P('tensor', 'dp', 'heads'), may hold values from -192 to 192
- router_weight: float32 [512, 32], P(('dp', 'tensor')), may hold values from -0.1875 to 0.1875
- router_first: float32 [512, 32], P(('dp', 'tensor')), may hold values from -48 to 48
- router_second: float32 [512, 32], P(('dp', 'tensor')), may hold values from 4.9 to 19.6
- expert_weights: float32 [64, 512, 2048], P(('heads', 'dp'), None, 'tensor')
- expert_momentum: float32 [64, 512, 2048], P(('heads', 'dp'), None, 'tensor'), may hold values from -16 to 16
- norm_params: float32 [4, 512], P(None, ('dp', 'tensor'))
- norm_first: float32 [4, 512], P(None, ('dp', 'tensor')), may hold values from -40 to 40
- norm_second: float32 [4, 512], P(None, ('dp', 'tensor')), may hold values from 3.152 to 12.608
- expert_ids: int32 [3152, 2], P('dp'), may hold values from 0 to 31, all different within a row; in each aligned block of 1576 rows (0 to 1575, 1576 to 3151, ...) at most 147 rows name the same one
- cotangent: bfloat16 [3152, 512], P(('dp', 'tensor')), may hold values from -6 to 6
Outputs:
- block_out: float32 [3152, 512], P(('dp', 'tensor'))
- input_grad: float32 [3152, 512], P(('dp', 'tensor'))
- attn_momentum_new: float32 [4, 512, 512], P('tensor', 'dp', 'heads')
- attn_weights_new: float32 [4, 512, 512], P('tensor', 'dp', 'heads')
- router_first_new: float32 [512, 32], P(('dp', 'tensor'))
- router_second_new: float32 [512, 32], P(('dp', 'tensor'))
- router_new: float32 [512, 32], P(('dp', 'tensor'))
- expert_momentum_new: float32 [64, 512, 2048], P(('heads', 'dp'), None, 'tensor')
- expert_weights_new: float32 [64, 512, 2048], P(('heads', 'dp'), None, 'tensor')
- norm_first_new: float32 [4, 512], P(None, ('dp', 'tensor'))
- norm_second_new: float32 [4, 512], P(None, ('dp', 'tensor'))
- norm_new: float32 [4, 512], P(None, ('dp', 'tensor'))
The draws below stay inside these ranges and needn't reach their ends.
Inputs may be any that keep to these rules, and one draw needn't show every extreme that they name: `expert_ids`: each token names 2 different experts; among the 1576 tokens of one index of dp no expert is named more than 147 times.
All inputs are finite; a program needn't handle non-finite values.
Results may differ from the reference program's by a relative error of at most 0.012.
The reference program's roundings to bfloat16 on the way count: a program that leaves them out, or rounds other values in their place, can miss the bound.
Values may be sent and summed in bfloat16 or wider, within the bound.
A program may use at most 192 MiB of HBM per device.

```python
import math
import jax
import jax.numpy as jnp
import numpy as np
from jax import lax

D = 512
FF = 2048
HEADS = 8
EXPERTS = 32
SEQ = 197
TOP = 2
ITERS = 5
STEP = 5
HEAD_DIM = 64
GROUP_TOK = 1576
TOKENS = 3152
CAP = 147
MATS = 64
N_DP = 2


def draw_attn_weights(key, part):
    key = jax.random.fold_in(key, 5)
    sample = jnp.clip(jax.random.normal(key, (4, D, D), jnp.float32), -6.0, 6.0)
    factors = jnp.array([1.4, 1.4, 1.0, 3.0], jnp.float32) * D ** (-0.5)
    return sample * factors[:, None, None]


def draw_expert_weights(key, part):
    key = jax.random.fold_in(key, 7)
    sample = jnp.clip(jax.random.normal(key, (2 * EXPERTS, D, FF), jnp.float32), -6.0, 6.0)
    matrix_kind = jnp.arange(2 * EXPERTS) % 2
    factors = jnp.where(matrix_kind == 0, D ** (-0.5), 1.5 * FF ** (-0.5)).astype(jnp.float32)
    return sample * factors[:, None, None]


def draw_norm_params(key, part):
    key = jax.random.fold_in(key, 9)
    sample = jnp.clip(jax.random.normal(key, (4, D), jnp.float32), -4.0, 4.0) * 0.1
    centre = jnp.array([1.0, 0.0, 1.0, 0.0], jnp.float32)
    return centre[:, None] + sample


def levels(own_key, dims, cuts, least, top_value):
    def one(dim, blocks):
        steps = jax.random.uniform(jax.random.fold_in(jax.random.fold_in(own_key, 6), dim), (blocks,), jnp.float32, least / len(cuts), top_value / len(cuts))
        return jnp.repeat(jnp.exp(steps), dims[dim] // blocks).reshape((-1,) + (1,) * (len(dims) - dim - 1))

    level = one(*cuts[0])
    for cut in cuts[1:]:
        level = level * one(*cut)
    return level


def routed_block(stream_key, own, number, rows, number_of, top, most, lean):
    sequence = jax.random.permutation(stream_key, number_of)
    heavy_load, ordinary = shares(number_of, rows * top, most, lean, True), shares(number_of, rows * top, most, lean, False)
    places = jnp.arange(number_of)

    def named(tallies, turn):
        used = int((tallies > 0).sum())
        fixed = max(1, used // 4)
        shifted = fixed + (places - fixed + turn * (used - fixed)) % max(1, number_of - fixed)
        return jnp.zeros((number_of,), jnp.int32).at[sequence[jnp.where(places < fixed, places, shifted)]].set(jnp.asarray(tallies, jnp.int32))

    tallies = jnp.where(number % 4 == 0, named(heavy_load, number // 4), named(ordinary, number - number // 4 - 1))
    mixed = jax.random.permutation(jax.random.fold_in(own, 3), number_of)
    source_of, taker = mixed[0:number_of // 2 * 2:2], mixed[1:number_of // 2 * 2:2]
    room = jnp.minimum(tallies[source_of] - 1, most - tallies[taker]) // 2
    room = jnp.where((source_of == sequence[0]) | (taker == sequence[0]) | (tallies[taker] == 0), 0, jnp.maximum(room, 0))
    shifted = jax.random.randint(jax.random.fold_in(own, 4), (number_of // 2,), 0, 1 << 20) % (room + 1)
    tallies = tallies.at[source_of].add(-shifted).at[taker].add(shifted)
    members = jnp.searchsorted(jnp.cumsum(tallies), jnp.arange(rows * top), side="right").astype(jnp.int32)
    table = members.reshape(top, rows).T
    table = table[jax.random.permutation(jax.random.fold_in(own, 1), rows)]
    turn = jax.random.randint(jax.random.fold_in(own, 2), (rows, 1), 0, top)
    return jnp.take_along_axis(table, (jnp.arange(top)[None, :] + turn) % top, axis=1)


def shares(amount, total, bound, skew, full):
    weights = [(1 << 20) // math.isqrt(rank ** skew) + 1 for rank in range(1, amount + 1)]
    largest = bound if full else min(bound, max(-(-total // amount), total * weights[0] // sum(weights)))
    least = 1 if total - largest >= amount - 1 else 0
    holding, spare = [largest] + [least] * (amount - 1), total - largest - least * (amount - 1)
    while spare > 0:
        candidates = [i for i in range(1, amount) if holding[i] < largest] or [i for i in range(1, amount) if holding[i] < bound]
        whole, remaining = sum([weights[i] for i in candidates]), spare
        for i in candidates:
            more = min(bound - holding[i], max(1, remaining * weights[i] // whole), spare)
            holding[i] = holding[i] + more
            spare = spare - more
    return np.array(holding)


def scatter_about(key, dims, width, limit, pieces=(), held_as=jnp.bfloat16):
    entries = jax.random.normal(key, dims, jnp.float32) * width
    if len(pieces) > 0:
        entries = levels(key, dims, pieces, -0.22, 0.18) * entries
    return jnp.clip(entries, min=-limit, max=limit).astype(held_as)


def setup_inputs(seed: int = 0) -> dict:
    streams_of = jax.random.split(jax.random.key(seed), 14)
    images_in = scatter_about(streams_of[0], (TOKENS, D), 1.0, 6.0, ((0, 8),))
    attn_weights = draw_attn_weights(jax.random.fold_in(streams_of[13], 71), 0)
    attn_momentum = scatter_about(streams_of[2], (4, D, D), (0.6 * TOKENS ** 0.5), 192.0, ((0, 4), (1, 2), (2, 4)), jnp.float32)
    router_weight = scatter_about(streams_of[3], (D, EXPERTS), (2 * D) ** -0.5, 0.1875, ((0, 8),), jnp.float32)
    router_first = scatter_about(streams_of[4], (D, EXPERTS), (0.55 * (2 * (TOKENS // EXPERTS)) ** 0.5), 48.0, ((0, 8),), jnp.float32)
    router_second = jnp.clip(jnp.exp(math.log(19.6) - 1.3862944 * jax.random.uniform(streams_of[5], (D, EXPERTS), jnp.float32) ** levels(streams_of[5], (D, EXPERTS), ((0, 8),), -0.2, 0.2)), 4.9, 19.6)
    expert_weights = draw_expert_weights(jax.random.fold_in(streams_of[13], 71), 0)
    expert_momentum = scatter_about(streams_of[7], (MATS, D, FF), (0.2 * (2 * (TOKENS // EXPERTS)) ** 0.5), 16.0, ((0, 8), (2, 4)), jnp.float32)
    norm_params = draw_norm_params(jax.random.fold_in(streams_of[13], 71), 0)
    norm_first = scatter_about(streams_of[9], (4, D), (0.11 * TOKENS ** 0.5), 40.0, ((1, 8),), jnp.float32)
    norm_second = jnp.clip(jnp.exp(math.log(12.608) - 1.3862944 * jax.random.uniform(streams_of[10], (4, D), jnp.float32) ** levels(streams_of[10], (4, D), ((1, 8),), -0.2, 0.2)), 3.152, 12.608)
    expert_ids_keys = jax.random.split(jax.random.fold_in(streams_of[11], 1), TOKENS // GROUP_TOK)
    expert_ids_turns = jax.random.permutation(jax.random.fold_in(streams_of[11], 3), TOKENS // GROUP_TOK)
    expert_ids = jax.vmap(lambda own, number: routed_block(jax.random.fold_in(streams_of[11], 2), own, number, GROUP_TOK, EXPERTS, TOP, CAP, 1))(expert_ids_keys, expert_ids_turns).reshape((TOKENS, TOP))
    cotangent = scatter_about(streams_of[12], (TOKENS, D), 1.0, 6.0, ((0, 8),))
    return dict(images_in=images_in, attn_weights=attn_weights, attn_momentum=attn_momentum, router_weight=router_weight, router_first=router_first, router_second=router_second, expert_weights=expert_weights, expert_momentum=expert_momentum, norm_params=norm_params, norm_first=norm_first, norm_second=norm_second, expert_ids=expert_ids, cotangent=cotangent)


@jax.custom_vjp
def low(v):
    return lax.optimization_barrier(v.astype(jnp.bfloat16)).astype(jnp.float32)

@jax.custom_vjp
def low_back(v):
    return v

def low_keep(v):
    return (low(v), None)

def low_pass(kept, grad):
    return (grad,)

def back_keep(v):
    return (v, None)

def back_low(kept, grad):
    return (low(grad),)
low.defvjp(low_keep, low_pass)
low_back.defvjp(back_keep, back_low)
norm_epsilon = 1e-06
coef_first = 3.4445
coef_second = -4.775
coef_third = 2.0315
momentum_decay = 0.95
muon_rate = 0.2
muon_decay = 0.1
adam_first = 0.9
adam_second = 0.999
adam_epsilon = 1e-08
router_rate = 0.03
router_decay = 0.01
gains_rate = 0.1
highest = lax.Precision.HIGHEST

def norm_apply(values, gain, shift):
    center = lax.optimization_barrier(jnp.mean(values, axis=-1, keepdims=True))
    centred = values - center
    return centred * lax.rsqrt(lax.optimization_barrier(jnp.mean(centred * centred, axis=-1, keepdims=True)) + norm_epsilon) * gain + shift

def exact_gelu(values):
    return jax.nn.gelu(values, approximate=False)

def batch_gram(values):
    return jnp.einsum('mij,mkj->mik', values, values, precision=highest)

def batch_product(left, right):
    return jnp.einsum('mij,mjk->mik', left, right, precision=highest)

def polish_step(values, gram):
    poly = coef_second * gram + coef_third * batch_product(gram, gram)
    return coef_first * values + batch_product(poly, values)

def muon_scale(rows, cols):
    return muon_rate * 0.2 * math.sqrt(max(rows, cols))

def adamw_update(values, first, second, grad, rate, decay):
    first_new = adam_first * first + (1.0 - adam_first) * grad
    second_new = adam_second * second + (1.0 - adam_second) * grad * grad
    first_hat = first_new / (1.0 - adam_first ** STEP)
    second_hat = second_new / (1.0 - adam_second ** STEP)
    values_new = values * (1.0 - rate * decay) - rate * first_hat / (jnp.sqrt(second_hat) + adam_epsilon)
    return (first_new, second_new, values_new)

def route_slots(ids):
    routes = ids.reshape(-1).astype(jnp.int32)
    route_count = routes.shape[0]
    order = jnp.argsort(routes * route_count + jnp.arange(route_count, dtype=jnp.int32)).astype(jnp.int32)
    labels = jnp.arange(EXPERTS, dtype=jnp.int32)
    counts = lax.optimization_barrier(jnp.sum((routes[None, :] == labels[:, None]).astype(jnp.int32), axis=1)).astype(jnp.int32)
    starts = lax.optimization_barrier(jnp.sum((routes[None, :] < labels[:, None]).astype(jnp.int32), axis=1)).astype(jnp.int32)
    slot_index = jnp.arange(CAP, dtype=jnp.int32)
    picked = order[jnp.minimum(starts[:, None] + slot_index[None, :], route_count - 1)]
    filled = (slot_index[None, :] < counts[:, None]).astype(jnp.float32)
    return (picked // TOP, picked % TOP, filled)

def group_forward(tokens, ids, attn, router, pairs, gains):
    normed_a = low(norm_apply(tokens, gains[0], gains[1]))
    qkv = jnp.einsum('td,mdc->mtc', normed_a, attn[:3], precision=highest)
    qkv = low_back(low(qkv))
    images = tokens.shape[0] // SEQ
    split = qkv.reshape(3, images, SEQ, HEADS, HEAD_DIM)
    scores = jnp.einsum('ishd,ithd->ihst', split[0], split[1], precision=highest) * HEAD_DIM ** (-0.5)
    probs = low(jax.nn.softmax(low_back(scores), axis=-1))
    mixed = jnp.einsum('ihst,ithd->ishd', probs, split[2], precision=highest).reshape(tokens.shape[0], D)
    mixed = low_back(low(mixed))
    attended = low_back(jnp.einsum('tc,dc->td', mixed, attn[3], precision=highest))
    first = tokens + attended
    normed_b = low(norm_apply(first, gains[2], gains[3]))
    logits = low_back(jnp.dot(normed_b, router, precision=highest))
    gates = jax.nn.softmax(jnp.take_along_axis(logits, ids, axis=1), axis=-1)
    token_rows, pick_cols, filled = route_slots(ids)
    slot_gate = gates[token_rows, pick_cols] * filled
    slot_in = normed_b[token_rows]
    hidden = low_back(jnp.einsum('ecd,edf->ecf', slot_in, pairs[:, 0], precision=highest))
    active = low(exact_gelu(hidden))
    expert_out = low_back(jnp.einsum('ecf,edf->ecd', active, pairs[:, 1], precision=highest))
    weighted = (expert_out * slot_gate[:, :, None]).reshape(-1, D)
    combined = jnp.zeros_like(first).at[token_rows.reshape(-1)].add(weighted)
    return first + combined

def orthogonal(matrix):
    values = matrix / (jnp.sqrt(jnp.sum(matrix * matrix)) + 1e-07)
    values = values[None]
    for iteration in range(ITERS):
        values = polish_step(values, batch_gram(values))
    return values[0]

def reference(images_in, attn_weights, attn_momentum, router_weight, router_first, router_second, expert_weights, expert_momentum, norm_params, norm_first, norm_second, expert_ids, cotangent):
    tokens = images_in.astype(jnp.float32)
    ids_groups = expert_ids.reshape(N_DP, GROUP_TOK, TOP)

    def forward(tokens, attn, router, experts, gains):
        attn_low = low(attn)
        router_low = low(router)
        pairs = low(experts).reshape(EXPERTS, 2, D, FF)
        gains_low = low(gains)

        def one_group(items):
            return group_forward(items[0], items[1], attn_low, router_low, pairs, gains_low)
        outputs = lax.map(jax.checkpoint(one_group), (tokens.reshape(N_DP, GROUP_TOK, D), ids_groups))
        return outputs.reshape(TOKENS, D)
    block_out, pullback = jax.vjp(forward, tokens, attn_weights, router_weight, expert_weights, norm_params)
    input_grad, attn_grad, router_grad, expert_grad, norm_grad = pullback(cotangent.astype(jnp.float32))
    attn_mom = momentum_decay * attn_momentum + attn_grad
    attn_ortho = lax.map(orthogonal, attn_grad + momentum_decay * attn_mom)
    attn_new = attn_weights * (1.0 - muon_rate * muon_decay) - muon_scale(D, D) * attn_ortho
    expert_mom = momentum_decay * expert_momentum + expert_grad
    expert_ortho = lax.map(orthogonal, expert_grad + momentum_decay * expert_mom)
    expert_new = expert_weights * (1.0 - muon_rate * muon_decay) - muon_scale(D, FF) * expert_ortho
    router_first_new, router_second_new, router_new = adamw_update(router_weight, router_first, router_second, router_grad, router_rate, router_decay)
    norm_first_new, norm_second_new, norm_new = adamw_update(norm_params, norm_first, norm_second, norm_grad, gains_rate, 0.0)
    return (block_out, input_grad, attn_mom, attn_new, router_first_new, router_second_new, router_new, expert_mom, expert_new, norm_first_new, norm_second_new, norm_new)
```

```python
import math

import jax
import jax.numpy as jnp
from jax import lax
from jax.experimental import pallas as pl
from jax.experimental.pallas import tpu as pltpu
from jax.sharding import PartitionSpec as P

EXPERTS = 32
SEQ = 197
TOP = 2
ITERS = 5
STEP = 5
HEAD_DIM = 64


norm_epsilon = 1e-06
coef_first = 3.4445
coef_second = -4.775
coef_third = 2.0315
momentum_decay = 0.95
muon_rate = 0.2
muon_decay = 0.1
adam_first = 0.9
adam_second = 0.999
adam_epsilon = 1e-08
router_rate = 0.03
router_decay = 0.01
gains_rate = 0.1
TILE = 128
VMEM_LIMIT = 56 * 1024 * 1024


def norm_forward(values, gain, shift):
    center = jnp.mean(values, axis=-1, keepdims=True)
    centred = values - center
    inverse = lax.rsqrt(jnp.mean(centred * centred, axis=-1, keepdims=True) + norm_epsilon)
    scaled = centred * inverse
    return (scaled * gain + shift, scaled, inverse)


def norm_backward(grad_normed, scaled, inverse, gain):
    grad_scaled = grad_normed * gain
    inner = grad_scaled - jnp.mean(grad_scaled, axis=-1, keepdims=True)
    inner = inner - scaled * jnp.mean(grad_scaled * scaled, axis=-1, keepdims=True)
    return inner * inverse


def exact_gelu(values):
    return jax.nn.gelu(values, approximate=False)


def batch_gram(values):
    return jnp.einsum("mij,mkj->mik", values, values, precision=lax.Precision.HIGHEST)


def batch_product(left, right):
    return jnp.einsum("mij,mjk->mik", left, right, precision=lax.Precision.HIGHEST)


def polish_step(values, gram):
    poly = coef_second * gram + coef_third * batch_product(gram, gram)
    return coef_first * values + batch_product(poly, values)


def muon_scale(rows, cols):
    return muon_rate * 0.2 * math.sqrt(max(rows, cols))


def adamw_update(values, first, second, grad, rate, decay):
    first_new = adam_first * first + (1.0 - adam_first) * grad
    second_new = adam_second * second + (1.0 - adam_second) * grad * grad
    first_hat = first_new / (1.0 - adam_first**STEP)
    second_hat = second_new / (1.0 - adam_second**STEP)
    values_new = values * (1.0 - rate * decay) - rate * first_hat / (
        jnp.sqrt(second_hat) + adam_epsilon
    )
    return (first_new, second_new, values_new)


def shards_general(
    images_in,
    attn_weights,
    attn_momentum,
    router_weight,
    router_first,
    router_second,
    expert_weights,
    expert_momentum,
    norm_params,
    norm_first,
    norm_second,
    expert_ids,
    cotangent,
):
    local_rows, width = images_in.shape
    dp_count = lax.axis_size("dp")
    head_count = lax.axis_size("heads")
    tensor_count = lax.axis_size("tensor")
    mats_here = attn_weights.shape[0]
    row_shard = attn_weights.shape[1]
    head_cols = attn_weights.shape[2]
    hidden_cols = expert_weights.shape[2]
    group_rows = expert_ids.shape[0]
    capacity = 3 * TOP * group_rows // (2 * EXPERTS)
    experts_here = EXPERTS // head_count
    heads_here = head_cols // HEAD_DIM
    images = local_rows // SEQ
    score_scale = HEAD_DIM ** (-0.5)
    head_index = lax.axis_index("heads")
    tensor_index = lax.axis_index("tensor")
    dp_index = lax.axis_index("dp")
    attn_low, router_low, norms_low = (
        lax.all_gather(attn_weights.astype(jnp.bfloat16), ("dp", "tensor"), axis=0, tiled=True),
        lax.all_gather(router_weight.astype(jnp.bfloat16), ("dp", "tensor"), axis=0, tiled=True),
        lax.all_gather(norm_params.astype(jnp.bfloat16), ("dp", "tensor"), axis=1, tiled=True),
    )
    attn_low = attn_low.reshape(dp_count, tensor_count * mats_here, row_shard, head_cols)
    attn_low = jnp.transpose(attn_low, (1, 0, 2, 3)).reshape(
        tensor_count * mats_here, width, head_cols
    )
    gains = norms_low.astype(jnp.float32)
    qkv_weight = jnp.transpose(attn_low[:3], (1, 0, 2)).reshape(width, 3 * head_cols)
    out_weight = attn_low[3]
    tokens = images_in.astype(jnp.float32)
    normed_a, scaled_a, inverse_a = norm_forward(tokens, gains[0], gains[1])
    normed_a = normed_a.astype(jnp.bfloat16)
    qkv = jnp.dot(normed_a, qkv_weight, preferred_element_type=jnp.float32).astype(jnp.bfloat16)
    split = qkv.reshape(images, SEQ, 3, heads_here, HEAD_DIM)
    query = split[:, :, 0]
    keys = split[:, :, 1]
    values = split[:, :, 2]
    scores = (
        jnp.einsum("ishd,ithd->ihst", query, keys, preferred_element_type=jnp.float32) * score_scale
    )
    peak = jnp.max(scores, axis=-1, keepdims=True)
    logsum = peak + jnp.log(jnp.sum(jnp.exp(scores - peak), axis=-1, keepdims=True))
    probs_low = jnp.exp(scores - logsum).astype(jnp.bfloat16)
    mixed = jnp.einsum("ihst,ithd->ishd", probs_low, values, preferred_element_type=jnp.float32)
    mixed = mixed.reshape(local_rows, head_cols).astype(jnp.bfloat16)
    partial_out = jnp.einsum("tc,dc->td", mixed, out_weight, preferred_element_type=jnp.float32)
    attended = lax.psum(partial_out, "heads")
    first = tokens + attended
    normed_b, scaled_b, inverse_b = norm_forward(first, gains[2], gains[3])
    normed_b = normed_b.astype(jnp.bfloat16)
    group_in, group_cot = (
        lax.all_gather(normed_b, "tensor", axis=0, tiled=True),
        lax.all_gather(cotangent, "tensor", axis=0, tiled=True),
    )
    logits = jnp.dot(group_in, router_low, preferred_element_type=jnp.float32)
    chosen = jnp.take_along_axis(logits, expert_ids, axis=1)
    raised = jnp.exp(chosen - jnp.max(chosen, axis=1, keepdims=True))
    gates = raised / jnp.sum(raised, axis=1, keepdims=True)
    routes = expert_ids.reshape(-1)
    route_count = routes.shape[0]
    order = jnp.argsort(routes * route_count + jnp.arange(route_count, dtype=jnp.int32))
    labels = head_index * experts_here + jnp.arange(experts_here, dtype=jnp.int32)
    counts = jnp.sum((routes[None, :] == labels[:, None]).astype(jnp.int32), axis=1)
    starts = jnp.sum((routes[None, :] < labels[:, None]).astype(jnp.int32), axis=1)
    slot_index = jnp.arange(capacity, dtype=jnp.int32)
    picked = order[jnp.minimum(starts[:, None] + slot_index[None, :], route_count - 1)]
    filled = (slot_index[None, :] < counts[:, None]).astype(jnp.float32)
    token_rows = (picked // TOP).reshape(-1)
    pick_cols = (picked % TOP).reshape(-1)
    slot_gate = gates[token_rows, pick_cols].reshape(experts_here, capacity) * filled
    slot_in = group_in[token_rows].reshape(experts_here, capacity, width)
    pair = lax.all_gather(expert_weights.astype(jnp.bfloat16), "dp", axis=0, tiled=True).reshape(
        experts_here, 2, width, hidden_cols
    )
    hidden = jnp.einsum("ecd,edf->ecf", slot_in, pair[:, 0], preferred_element_type=jnp.float32)
    active, gelu_pull = jax.vjp(exact_gelu, hidden)
    active = active.astype(jnp.bfloat16)
    expert_out = jnp.einsum("ecf,edf->ecd", active, pair[:, 1], preferred_element_type=jnp.float32)
    weighted = (expert_out * slot_gate[:, :, None]).reshape(-1, width)
    spread = jnp.zeros((group_rows, width), jnp.float32).at[token_rows].add(weighted)
    own_sum = lax.psum_scatter(spread, "tensor", scatter_dimension=0, tiled=True)
    moe_out = lax.psum(own_sum, "heads")
    block_out = first + moe_out
    grad_out = cotangent.astype(jnp.float32)
    slot_cot = group_cot[token_rows].reshape(experts_here, capacity, width).astype(jnp.float32)
    gate_grad = jnp.sum(slot_cot * expert_out, axis=-1) * filled
    out_grad = (slot_cot * slot_gate[:, :, None]).astype(jnp.bfloat16)
    pair_back = lax.all_gather(
        expert_weights.astype(jnp.bfloat16), "dp", axis=0, tiled=True
    ).reshape(experts_here, 2, width, hidden_cols)
    active_grad = jnp.einsum(
        "ecd,edf->ecf", out_grad, pair_back[:, 1], preferred_element_type=jnp.float32
    )
    hidden_grad = gelu_pull(active_grad)[0].astype(jnp.bfloat16)
    down_grad = jnp.einsum("ecd,ecf->edf", out_grad, active, preferred_element_type=jnp.float32)
    up_grad = jnp.einsum("ecd,ecf->edf", slot_in, hidden_grad, preferred_element_type=jnp.float32)
    slot_in_grad = jnp.einsum(
        "ecf,edf->ecd", hidden_grad, pair_back[:, 0], preferred_element_type=jnp.float32
    ).reshape(-1, width)
    back_spread = jnp.zeros((group_rows, width), jnp.float32).at[token_rows].add(slot_in_grad)
    gate_spread = (
        jnp.zeros((group_rows, TOP), jnp.float32)
        .at[token_rows, pick_cols]
        .add(gate_grad.reshape(-1))
    )
    own_back, own_gate = (
        lax.psum_scatter(back_spread, "tensor", scatter_dimension=0, tiled=True),
        lax.psum_scatter(gate_spread, "tensor", scatter_dimension=0, tiled=True),
    )
    normed_b_grad, gate_total = lax.psum((own_back, own_gate), "heads")
    matrix_grads = jnp.stack((up_grad, down_grad), axis=1).reshape(
        2 * experts_here, width, hidden_cols
    )
    expert_grad = lax.psum_scatter(matrix_grads, "dp", scatter_dimension=0, tiled=True)
    own_ids = lax.dynamic_slice_in_dim(expert_ids, tensor_index * local_rows, local_rows, 0)
    own_gates = lax.dynamic_slice_in_dim(gates, tensor_index * local_rows, local_rows, 0)
    blend = jnp.sum(own_gates * gate_total, axis=1, keepdims=True)
    chosen_grad = own_gates * (gate_total - blend)
    expert_labels = jnp.arange(EXPERTS, dtype=jnp.int32)
    matches = (own_ids[:, :, None] == expert_labels[None, None, :]).astype(jnp.float32)
    logit_grad = jnp.sum(matches * chosen_grad[:, :, None], axis=1).astype(jnp.bfloat16)
    normed_b_grad = normed_b_grad + jnp.einsum(
        "te,de->td", logit_grad, router_low, preferred_element_type=jnp.float32
    )
    router_grad = jnp.einsum("td,te->de", normed_b, logit_grad, preferred_element_type=jnp.float32)
    gain_b_grad = jnp.sum(normed_b_grad * scaled_b, axis=0)
    shift_b_grad = jnp.sum(normed_b_grad, axis=0)
    first_grad = grad_out + norm_backward(normed_b_grad, scaled_b, inverse_b, gains[2])
    branch_grad = first_grad.astype(jnp.bfloat16)
    out_weight_grad = jnp.einsum(
        "td,tc->dc", branch_grad, mixed, preferred_element_type=jnp.float32
    )
    mixed_grad = jnp.einsum(
        "td,dc->tc", branch_grad, out_weight, preferred_element_type=jnp.float32
    ).astype(jnp.bfloat16)
    mixed_grad = mixed_grad.reshape(images, SEQ, heads_here, HEAD_DIM)
    scores_again = (
        jnp.einsum("ishd,ithd->ihst", query, keys, preferred_element_type=jnp.float32) * score_scale
    )
    probs_again = jnp.exp(scores_again - logsum)
    prob_grad = jnp.einsum(
        "ishd,ithd->ihst", mixed_grad, values, preferred_element_type=jnp.float32
    )
    value_grad = jnp.einsum(
        "ihst,ishd->ithd",
        probs_again.astype(jnp.bfloat16),
        mixed_grad,
        preferred_element_type=jnp.float32,
    )
    score_grad = (
        probs_again * (prob_grad - jnp.sum(probs_again * prob_grad, axis=-1, keepdims=True))
    ).astype(jnp.bfloat16)
    query_grad = (
        jnp.einsum("ihst,ithd->ishd", score_grad, keys, preferred_element_type=jnp.float32)
        * score_scale
    )
    key_grad = (
        jnp.einsum("ihst,ishd->ithd", score_grad, query, preferred_element_type=jnp.float32)
        * score_scale
    )
    qkv_grad = (
        jnp.stack((query_grad, key_grad, value_grad), axis=2)
        .reshape(local_rows, 3 * head_cols)
        .astype(jnp.bfloat16)
    )
    normed_a_part = jnp.einsum(
        "tc,dc->td", qkv_grad, qkv_weight, preferred_element_type=jnp.float32
    )
    qkv_weight_grad = jnp.einsum(
        "td,tc->dc", normed_a, qkv_grad, preferred_element_type=jnp.float32
    )
    normed_a_grad = lax.psum(normed_a_part, "heads")
    gain_a_grad = jnp.sum(normed_a_grad * scaled_a, axis=0)
    shift_a_grad = jnp.sum(normed_a_grad, axis=0)
    input_grad = first_grad + norm_backward(normed_a_grad, scaled_a, inverse_a, gains[0])
    attn_grad = jnp.concatenate(
        (
            jnp.transpose(qkv_weight_grad.reshape(width, 3, head_cols), (1, 0, 2)),
            out_weight_grad[None],
        ),
        axis=0,
    )
    arranged = attn_grad.reshape(tensor_count, mats_here, dp_count, row_shard, head_cols)
    arranged = jnp.transpose(arranged, (2, 0, 1, 3, 4)).reshape(
        dp_count * tensor_count * mats_here, row_shard, head_cols
    )
    norm_grad = jnp.stack((gain_a_grad, shift_a_grad, gain_b_grad, shift_b_grad))
    attn_sum, router_sum, norm_sum = (
        lax.psum_scatter(arranged, ("dp", "tensor"), scatter_dimension=0, tiled=True),
        lax.psum_scatter(router_grad, ("dp", "tensor"), scatter_dimension=0, tiled=True),
        lax.psum_scatter(norm_grad, ("dp", "tensor"), scatter_dimension=1, tiled=True),
    )
    attn_mom = momentum_decay * attn_momentum + attn_sum
    attn_dir = attn_sum + momentum_decay * attn_mom
    whole = lax.all_gather(attn_dir, ("dp", "heads"), axis=1, tiled=True)
    whole = whole.reshape(mats_here, dp_count, head_count, row_shard, head_cols)
    whole = jnp.transpose(whole, (0, 1, 3, 2, 4)).reshape(mats_here, width, head_count * head_cols)
    whole = whole / (jnp.sqrt(jnp.sum(whole * whole, axis=(1, 2), keepdims=True)) + 1e-07)
    for iteration in range(ITERS):
        whole = polish_step(whole, batch_gram(whole))
    own_part = lax.dynamic_slice(
        whole, (0, dp_index * row_shard, head_index * head_cols), (mats_here, row_shard, head_cols)
    )
    attn_new = (
        attn_weights * (1.0 - muon_rate * muon_decay)
        - muon_scale(width, head_count * head_cols) * own_part
    )
    expert_mom = momentum_decay * expert_momentum + expert_grad
    current = expert_grad + momentum_decay * expert_mom
    for iteration in range(ITERS):
        gram = lax.psum(batch_gram(current), "tensor")
        if iteration == 0:
            factor = 1.0 / (jnp.sqrt(jnp.trace(gram, axis1=1, axis2=2)) + 1e-07)
            factor = factor[:, None, None]
            current = current * factor
            gram = gram * (factor * factor)
        current = polish_step(current, gram)
    expert_new = (
        expert_weights * (1.0 - muon_rate * muon_decay)
        - muon_scale(width, hidden_cols * tensor_count) * current
    )
    router_first_new, router_second_new, router_new = adamw_update(
        router_weight, router_first, router_second, router_sum, router_rate, router_decay
    )
    norm_first_new, norm_second_new, norm_new = adamw_update(
        norm_params, norm_first, norm_second, norm_sum, gains_rate, 0.0
    )
    return (
        block_out,
        input_grad,
        attn_mom,
        attn_new,
        router_first_new,
        router_second_new,
        router_new,
        expert_mom,
        expert_new,
        norm_first_new,
        norm_second_new,
        norm_new,
    )


def ceil_to(value, step):
    return -(-value // step) * step


def dot_exact(left, right):
    return jnp.dot(
        left, right, precision=lax.Precision.HIGH, preferred_element_type=jnp.float32
    )


def dot_low(left, right, contract=((1,), (0,))):
    return lax.dot_general(
        left, right, (contract, ((), ())), preferred_element_type=jnp.float32
    )


def block_pairs(width):
    tiles = width // TILE
    return [(i, j) for i in range(tiles) for j in range(i, tiles)]


def pack_upper(matrix, out_ref):
    for place, (i, j) in enumerate(block_pairs(matrix.shape[0])):
        out_ref[place * TILE : (place + 1) * TILE, :] = matrix[
            i * TILE : (i + 1) * TILE, j * TILE : (j + 1) * TILE
        ]


def unpack_upper(packed_ref, out_ref, factor=None):
    for place, (i, j) in enumerate(block_pairs(out_ref.shape[0])):
        block = packed_ref[place * TILE : (place + 1) * TILE, :]
        if factor is not None:
            block = block * factor
        out_ref[i * TILE : (i + 1) * TILE, j * TILE : (j + 1) * TILE] = block
        if i != j:
            out_ref[j * TILE : (j + 1) * TILE, i * TILE : (i + 1) * TILE] = block.T


def gram_packed(values, out_ref):
    rows = values.shape[0]
    half = rows // 2
    contract = (((1,), (1,)), ((), ()))
    upper = lax.dot_general(
        values[:half], values, contract,
        precision=lax.Precision.HIGH, preferred_element_type=jnp.float32,
    )
    lower = lax.dot_general(
        values[half:], values[half:], contract,
        precision=lax.Precision.HIGH, preferred_element_type=jnp.float32,
    )
    for place, (i, j) in enumerate(block_pairs(rows)):
        top = i * TILE
        if top < half:
            block = upper[top : top + TILE, j * TILE : (j + 1) * TILE]
        else:
            block = lower[top - half : top - half + TILE, j * TILE - half : (j + 1) * TILE - half]
        out_ref[place * TILE : (place + 1) * TILE, :] = block


def expert_kernel(
    label_ref, rank_ref, tokens_ref, cot_ref, member_ref, router_ref, weight_ref, momentum_ref,
    momentum_out, back_out, gate_out, ahead_out, dir_out, gram_out,
):
    groups = tokens_ref.shape[0]
    slots = back_out.shape[1] // groups
    label = label_ref[pl.program_id(0)]
    ins, cots, members = [], [], []
    for group in range(groups):
        rank = rank_ref[0, group : group + 1, :]
        place = lax.broadcasted_iota(jnp.int32, (slots, rank.shape[1]), 0)
        pick = jnp.where(rank == place, 1.0, 0.0).astype(jnp.bfloat16)
        ins.append(dot_low(pick, tokens_ref[group]).astype(jnp.bfloat16))
        cots.append(dot_low(pick, cot_ref[group]))
        members.append(dot_low(pick, member_ref[group]))
    slot_in = jnp.concatenate(ins, axis=0)
    slot_cot = jnp.concatenate(cots, axis=0)
    member = jnp.concatenate(members, axis=0)
    logits = dot_low(slot_in, router_ref[...])
    lanes = lax.broadcasted_iota(jnp.int32, logits.shape, 1)
    own = jnp.where(lanes == label, 1.0, 0.0)
    filled = jnp.sum(member * own, axis=1, keepdims=True)
    logit_own = jnp.sum(logits * own, axis=1, keepdims=True)
    logit_other = jnp.sum(logits * (member - own), axis=1, keepdims=True)
    peak = jnp.maximum(logit_own, logit_other)
    raised = jnp.exp(logit_own - peak)
    gate = filled * raised / (raised + jnp.exp(logit_other - peak))
    up = weight_ref[0].astype(jnp.bfloat16)
    down = weight_ref[1].astype(jnp.bfloat16)
    hidden = dot_low(slot_in, up)
    cdf = 0.5 * (1.0 + lax.erf(hidden * math.sqrt(0.5)))
    active = (hidden * cdf).astype(jnp.bfloat16)
    slope = cdf + hidden * jnp.exp(-0.5 * hidden * hidden) * (1.0 / math.sqrt(2.0 * math.pi))
    expert_out = dot_low(active, down, ((1,), (1,)))
    gate_grad = jnp.sum(slot_cot * expert_out, axis=1, keepdims=True) * filled
    ahead_out[0] = (expert_out * gate).astype(jnp.bfloat16)
    out_grad = (slot_cot * gate).astype(jnp.bfloat16)
    hidden_grad = (dot_low(out_grad, down) * slope).astype(jnp.bfloat16)
    back_out[0] = dot_low(hidden_grad, up, ((1,), (1,))).astype(jnp.bfloat16)
    wide = lax.broadcasted_iota(jnp.int32, (gate_grad.shape[0], TILE), 1)
    high = gate_grad.astype(jnp.bfloat16).astype(jnp.float32)
    spread = jnp.where(wide == label, high, 0.0)
    spread = jnp.where(wide == label + EXPERTS, gate_grad - high, spread)
    gate_out[0] = spread.astype(jnp.bfloat16)
    for which, grad in enumerate(
        (
            dot_low(slot_in, hidden_grad, ((0,), (0,))),
            dot_low(out_grad, active, ((0,), (0,))),
        )
    ):
        momentum = momentum_decay * momentum_ref[which] + grad
        momentum_out[which] = momentum
        direction = grad + momentum_decay * momentum
        dir_out[which] = direction
        gram_packed(direction, gram_out.at[which])


def run_experts(first, count, slots, labels, ranks, tokens, cot, member, router, weights, momentum, earlier):
    groups, padded, width = tokens.shape
    mats, _, hidden = weights.shape
    pairs = len(block_pairs(width))
    whole = (
        jax.ShapeDtypeStruct((mats, width, hidden), jnp.float32),
        jax.ShapeDtypeStruct((mats // 2, groups * slots, width), jnp.bfloat16),
        jax.ShapeDtypeStruct((mats // 2, groups * slots, TILE), jnp.bfloat16),
        jax.ShapeDtypeStruct((mats // 2, groups * slots, width), jnp.bfloat16),
    )
    part = (
        jax.ShapeDtypeStruct((2 * count, width, hidden), jnp.float32),
        jax.ShapeDtypeStruct((2 * count, pairs * TILE, TILE), jnp.float32),
    )

    def shifted(e):
        return (first + e, 0, 0)

    def here(e):
        return (e, 0, 0)

    def kernel(*refs):
        expert_kernel(*refs[:8], *refs[8 + len(earlier) :])

    return pl.pallas_call(
        kernel,
        grid=(count,),
        in_specs=[
            pl.BlockSpec(memory_space=pltpu.SMEM),
            pl.BlockSpec((1, groups, padded), shifted),
            pl.BlockSpec((groups, padded, width), lambda e: (0, 0, 0)),
            pl.BlockSpec((groups, padded, width), lambda e: (0, 0, 0)),
            pl.BlockSpec((groups, padded, EXPERTS), lambda e: (0, 0, 0)),
            pl.BlockSpec((width, EXPERTS), lambda e: (0, 0)),
            pl.BlockSpec((2, width, hidden), shifted),
            pl.BlockSpec((2, width, hidden), shifted),
        ]
        + [pl.BlockSpec(memory_space=pl.ANY)] * len(earlier),
        out_specs=[
            pl.BlockSpec((2, width, hidden), shifted),
            pl.BlockSpec((1, groups * slots, width), shifted),
            pl.BlockSpec((1, groups * slots, TILE), shifted),
            pl.BlockSpec((1, groups * slots, width), shifted),
            pl.BlockSpec((2, width, hidden), here),
            pl.BlockSpec((2, pairs * TILE, TILE), here),
        ],
        out_shape=whole + part,
        input_output_aliases={8 + place: place for place in range(len(earlier))},
        compiler_params=pltpu.CompilerParams(vmem_limit_bytes=VMEM_LIMIT),
        name="expert_pair",
    )(labels[first : first + count], ranks, tokens, cot, member, router, weights, momentum, *earlier)


def polish_kernel(packed_ref, out_ref, gram, poly, product):
    width = gram.shape[0]
    half = width // 2
    trace = jnp.zeros((1, 1), jnp.float32)
    rows = lax.broadcasted_iota(jnp.int32, (TILE, TILE), 0)
    lanes = lax.broadcasted_iota(jnp.int32, (TILE, TILE), 1)
    for place, (i, j) in enumerate(block_pairs(width)):
        if i == j:
            block = packed_ref[0, place * TILE : (place + 1) * TILE, :]
            trace += jnp.sum(jnp.where(rows == lanes, block, 0.0), keepdims=True)
    factor = 1.0 / (jnp.sqrt(trace) + 1e-07)
    unpack_upper(packed_ref.at[0], gram, factor * factor)

    def symmetric(left, right):
        upper = dot_exact(left[:half, :], right[...])
        corner = dot_exact(left[half:, :], right[:, half:])
        return upper, corner

    def store(ref, upper, corner):
        ref[:half, :] = upper
        ref[half:, half:] = corner
        ref[half:, :half] = upper[:, half:].T

    def eye(offset, count):
        here = lax.broadcasted_iota(jnp.int32, (half, count), 0)
        there = lax.broadcasted_iota(jnp.int32, (half, count), 1)
        return jnp.where(here == there, coef_first, 0.0)

    for step in range(ITERS):
        upper, corner = symmetric(gram, gram)
        upper = eye(0, width) + coef_second * gram[:half, :] + coef_third * upper
        corner = eye(0, half) + coef_second * gram[half:, half:] + coef_third * corner
        store(poly, upper, corner)
        if step == 0:
            store(product, upper, corner)
        else:
            store(product, *symmetric(poly, product))
        if step < ITERS - 1:
            store(poly, *symmetric(poly, poly))
            store(gram, *symmetric(gram, poly))
    pack_upper(product[...] * factor, out_ref.at[0])


def run_polish(packed, width):
    return pl.pallas_call(
        polish_kernel,
        grid=(packed.shape[0],),
        in_specs=[pl.BlockSpec((1,) + packed.shape[1:], lambda m: (m, 0, 0))],
        out_specs=pl.BlockSpec((1,) + packed.shape[1:], lambda m: (m, 0, 0)),
        out_shape=jax.ShapeDtypeStruct(packed.shape, jnp.float32),
        scratch_shapes=[pltpu.VMEM((width, width), jnp.float32)] * 3,
        compiler_params=pltpu.CompilerParams(vmem_limit_bytes=VMEM_LIMIT),
        name="polish",
    )(packed)


def apply_kernel(scale, packed_ref, dir_ref, weight_ref, out_ref, whole):
    unpack_upper(packed_ref.at[0], whole)
    ortho = dot_exact(whole[...], dir_ref[0])
    out_ref[0] = weight_ref[0] * (1.0 - muon_rate * muon_decay) - scale * ortho


def run_apply(first, scale, packed, direction, weights, earlier):
    count, width, hidden = direction.shape

    def kernel(packed_ref, dir_ref, weight_ref, *refs):
        apply_kernel(scale, packed_ref, dir_ref, weight_ref, *refs[len(earlier) :])

    return pl.pallas_call(
        kernel,
        grid=(count,),
        in_specs=[
            pl.BlockSpec((1,) + packed.shape[1:], lambda m: (m, 0, 0)),
            pl.BlockSpec((1, width, hidden), lambda m: (m, 0, 0)),
            pl.BlockSpec((1, width, hidden), lambda m: (first + m, 0, 0)),
        ]
        + [pl.BlockSpec(memory_space=pl.ANY)] * len(earlier),
        out_specs=pl.BlockSpec((1, width, hidden), lambda m: (first + m, 0, 0)),
        out_shape=jax.ShapeDtypeStruct(weights.shape, jnp.float32),
        input_output_aliases={3 + place: place for place in range(len(earlier))},
        scratch_shapes=[pltpu.VMEM((width, width), jnp.float32)],
        compiler_params=pltpu.CompilerParams(vmem_limit_bytes=VMEM_LIMIT),
        name="apply",
    )(packed, direction, weights, *earlier)


def spread_kernel(slots, code_ref, back_ref, gate_ref, ahead_ref, back_out, ahead_out):
    experts = back_ref.shape[0]
    total = experts * slots
    place = lax.broadcasted_iota(jnp.int32, (code_ref.shape[1], total), 1)
    hit = (code_ref[0, :, 0:1] == place) | (code_ref[0, :, 1:2] == place)
    pick = jnp.where(hit, 1.0, 0.0).astype(jnp.bfloat16)
    width = back_ref.shape[2]
    back_out[0, :, :width] = dot_low(pick, back_ref[...].reshape(total, width)).astype(jnp.bfloat16)
    back_out[0, :, width:] = dot_low(pick, gate_ref[...].reshape(total, TILE)).astype(jnp.bfloat16)
    ahead_out[0] = dot_low(pick, ahead_ref[...].reshape(total, width)).astype(jnp.bfloat16)


def run_spread(slots, codes, back, gate, ahead):
    groups, padded, _ = codes.shape
    experts, _, width = back.shape

    def at_group(g):
        return (g, 0, 0)

    def slot_rows(g):
        return (0, g, 0)

    return pl.pallas_call(
        lambda *refs: spread_kernel(slots, *refs),
        grid=(groups,),
        in_specs=[
            pl.BlockSpec((1, padded, TOP), at_group),
            pl.BlockSpec((experts, slots, width), slot_rows),
            pl.BlockSpec((experts, slots, TILE), slot_rows),
            pl.BlockSpec((experts, slots, width), slot_rows),
        ],
        out_specs=[
            pl.BlockSpec((1, padded, width + TILE), at_group),
            pl.BlockSpec((1, padded, width), at_group),
        ],
        out_shape=[
            jax.ShapeDtypeStruct((groups, padded, width + TILE), jnp.bfloat16),
            jax.ShapeDtypeStruct((groups, padded, width), jnp.bfloat16),
        ],
        compiler_params=pltpu.CompilerParams(vmem_limit_bytes=VMEM_LIMIT),
        name="spread",
    )(codes, back, gate, ahead)


def gather_all(values):
    return lax.all_gather(values, ("dp", "tensor", "heads"), axis=0, tiled=False)


def total_rows(spread, rows):
    groups, padded, width = spread.shape
    own = lax.psum_scatter(spread, "dp", scatter_dimension=0, tiled=True)
    heads, tensor = lax.axis_size("heads"), lax.axis_size("tensor")
    own = own.reshape(tensor, heads, padded // (tensor * heads), width)
    own = lax.psum_scatter(own, "heads", scatter_dimension=1, tiled=True)
    own = lax.psum_scatter(own, "tensor", scatter_dimension=0, tiled=True)
    whole = lax.all_gather(own.reshape(-1, width), "heads", axis=0, tiled=True)
    return whole[:rows].astype(jnp.float32)


def slot_places(ids, labels, padded_rows, slots):
    groups, padded, _ = ids.shape
    own = ids[:, :, :, None] == labels[None, None, None, :]
    mine = jnp.any(own, axis=2)
    marks = mine.astype(jnp.bfloat16).reshape(groups, padded // TILE, TILE, -1)
    steps = jnp.arange(TILE)
    earlier = (steps[:, None] > steps[None, :]).astype(jnp.bfloat16)
    within = jnp.einsum("st,gbte->gbse", earlier, marks, preferred_element_type=jnp.float32)
    sums = jnp.sum(marks.astype(jnp.float32), axis=2)
    before = jnp.cumsum(sums, axis=1) - sums
    rank = (within + before[:, :, None, :]).astype(jnp.int32).reshape(groups, padded, -1)
    rank = jnp.where(mine, rank, -1)
    codes = rank + slots * jnp.arange(labels.shape[0], dtype=jnp.int32)
    codes = jnp.max(jnp.where(own, codes[:, :, None, :], -1), axis=3)
    return jnp.transpose(rank, (2, 0, 1)), codes


def shards_fast(
    images_in,
    attn_weights,
    attn_momentum,
    router_weight,
    router_first,
    router_second,
    expert_weights,
    expert_momentum,
    norm_params,
    norm_first,
    norm_second,
    expert_ids,
    cotangent,
):
    rows, width = images_in.shape
    dp_count = lax.axis_size("dp")
    head_count = lax.axis_size("heads")
    tensor_count = lax.axis_size("tensor")
    mats_here, row_shard, head_cols = attn_weights.shape
    mats = expert_weights.shape[0]
    hidden_cols = expert_weights.shape[2]
    group_rows = expert_ids.shape[0]
    capacity = 3 * TOP * group_rows // (2 * EXPERTS)
    slots = ceil_to(capacity, 16)
    quarter = ceil_to(-(-rows // head_count), 16)
    padded_rows = quarter * head_count
    images = rows // SEQ
    heads = width // HEAD_DIM
    score_scale = HEAD_DIM ** (-0.5)
    head_index = lax.axis_index("heads")
    tensor_index = lax.axis_index("tensor")
    dp_index = lax.axis_index("dp")
    bf16, f32 = jnp.bfloat16, jnp.float32

    def pad_rows(values):
        return jnp.pad(values, ((0, padded_rows - rows),) + ((0, 0),) * (values.ndim - 1))

    def own_quarter(values):
        return lax.dynamic_slice_in_dim(pad_rows(values), head_index * quarter, quarter, 0)

    router_rows = router_weight.size // TILE
    norm_rows = norm_params.size // TILE
    attn_rows = attn_weights.size // TILE
    flat = jnp.concatenate(
        (
            attn_weights.astype(bf16).reshape(attn_rows, TILE),
            router_weight.astype(bf16).reshape(router_rows, TILE),
            norm_params.astype(bf16).reshape(norm_rows, TILE),
        ),
        axis=0,
    )
    filled_rows = flat.shape[0]
    flat = jnp.pad(flat, ((0, ceil_to(filled_rows, 16) - filled_rows), (0, 0)))
    low = gather_all(flat).reshape(dp_count, tensor_count, head_count, -1, TILE)
    attn_low = low[:, :, :, :attn_rows].reshape(
        dp_count, tensor_count, head_count, mats_here, row_shard, head_cols
    )
    attn_low = jnp.transpose(attn_low, (1, 3, 0, 4, 2, 5)).reshape(4, width, width)
    router_low = low[:, :, 0, attn_rows : attn_rows + router_rows].reshape(width, EXPERTS)
    gains = low[:, :, 0, attn_rows + router_rows : filled_rows].reshape(
        dp_count * tensor_count, 4, -1
    )
    gains = jnp.transpose(gains, (1, 0, 2)).reshape(4, width).astype(f32)
    qkv_weight = jnp.transpose(attn_low[:3], (1, 0, 2)).reshape(width, 3 * width)
    out_weight = attn_low[3]

    all_cot = gather_all(own_quarter(cotangent)).reshape(dp_count, -1, width)
    all_ids = lax.all_gather(expert_ids, "dp", axis=0)
    all_ids = all_ids.reshape(dp_count * tensor_count, rows, TOP)
    all_ids = jnp.pad(all_ids, ((0, 0), (0, padded_rows - rows), (0, 0)), constant_values=-1)
    all_ids = all_ids.reshape(dp_count, tensor_count * padded_rows, TOP)
    experts_own = mats // 2
    labels = (head_index * dp_count + dp_index) * experts_own + jnp.arange(
        experts_own, dtype=jnp.int32
    )
    expert_labels = jnp.arange(EXPERTS, dtype=jnp.int32)
    member = jnp.any(all_ids[:, :, :, None] == expert_labels, axis=2).astype(bf16)
    ranks, codes = slot_places(all_ids, labels, padded_rows, slots)

    tokens = images_in.astype(f32)
    normed_a, scaled_a, inverse_a = norm_forward(tokens, gains[0], gains[1])
    normed_a = normed_a.astype(bf16)
    qkv = jnp.dot(normed_a, qkv_weight, preferred_element_type=f32).astype(bf16)
    split = qkv.reshape(images, SEQ, 3, heads, HEAD_DIM)
    query = split[:, :, 0]
    keys = split[:, :, 1]
    values = split[:, :, 2]
    scores = jnp.einsum("ishd,ithd->ihst", query, keys, preferred_element_type=f32) * score_scale
    peak = jnp.max(scores, axis=-1, keepdims=True)
    logsum = peak + jnp.log(jnp.sum(jnp.exp(scores - peak), axis=-1, keepdims=True))
    probs = jnp.exp(scores - logsum)
    probs_low = probs.astype(bf16)
    mixed = jnp.einsum("ihst,ithd->ishd", probs_low, values, preferred_element_type=f32)
    mixed = mixed.reshape(rows, width).astype(bf16)
    first = tokens + jnp.einsum("tc,dc->td", mixed, out_weight, preferred_element_type=f32)
    normed_b, scaled_b, inverse_b = norm_forward(first, gains[2], gains[3])
    normed_b = normed_b.astype(bf16)
    all_normed = gather_all(own_quarter(normed_b)).reshape(dp_count, -1, width)

    step = tensor_count // 2
    earlier = ()
    directions, packed = [], []
    for start in range(0, experts_own, step):
        *earlier, direction, gram = run_experts(
            start, step, slots, labels, ranks, all_normed, all_cot, member, router_low,
            expert_weights, expert_momentum, tuple(earlier),
        )
        directions.append(direction)
        packed.append(lax.psum_scatter(gram, "tensor", scatter_dimension=0, tiled=True))
    expert_mom, back, gate_back, ahead = earlier
    back_spread, ahead_spread = run_spread(slots, codes, back, gate_back, ahead)
    back_total = total_rows(back_spread, rows)
    block_out = first + total_rows(ahead_spread, rows)

    expert_new = ()
    scale = muon_scale(width, hidden_cols * tensor_count)
    for place, (direction, gram) in enumerate(zip(directions, packed)):
        product = lax.all_gather(run_polish(gram, width), "tensor", axis=0, tiled=True)
        expert_new = (
            run_apply(place * tensor_count, scale, product, direction, expert_weights, expert_new),
        )
    expert_new = expert_new[0]

    normed_b_grad = back_total[:, :width]
    gate_total = (
        back_total[:, width : width + EXPERTS] + back_total[:, width + EXPERTS : width + 2 * EXPERTS]
    )
    own_ids = lax.dynamic_slice_in_dim(expert_ids, tensor_index * rows, rows, 0)
    chosen = jnp.any(own_ids[:, :, None] == expert_labels, axis=1)
    logits = jnp.dot(normed_b, router_low, preferred_element_type=f32)
    raised = jnp.where(chosen, logits, -jnp.inf)
    raised = jnp.exp(raised - jnp.max(raised, axis=1, keepdims=True))
    own_gates = raised / jnp.sum(raised, axis=1, keepdims=True)
    blend = jnp.sum(own_gates * gate_total, axis=1, keepdims=True)
    logit_grad = (own_gates * (gate_total - blend)).astype(bf16)
    normed_b_grad = normed_b_grad + jnp.einsum(
        "te,de->td", logit_grad, router_low, preferred_element_type=f32
    )
    router_grad = jnp.einsum("td,te->de", normed_b, logit_grad, preferred_element_type=f32)
    gain_b_grad = jnp.sum(normed_b_grad * scaled_b, axis=0)
    shift_b_grad = jnp.sum(normed_b_grad, axis=0)
    first_grad = cotangent.astype(f32) + norm_backward(
        normed_b_grad, scaled_b, inverse_b, gains[2]
    )

    branch_grad = first_grad.astype(bf16)
    mixed_grad = jnp.einsum(
        "td,dc->tc", branch_grad, out_weight, preferred_element_type=f32
    ).astype(bf16)
    mixed_grad = mixed_grad.reshape(images, SEQ, heads, HEAD_DIM)
    prob_grad = jnp.einsum("ishd,ithd->ihst", mixed_grad, values, preferred_element_type=f32)
    value_grad = jnp.einsum("ihst,ishd->ithd", probs_low, mixed_grad, preferred_element_type=f32)
    score_grad = (
        probs * (prob_grad - jnp.sum(probs * prob_grad, axis=-1, keepdims=True))
    ).astype(bf16)
    query_grad = (
        jnp.einsum("ihst,ithd->ishd", score_grad, keys, preferred_element_type=f32) * score_scale
    )
    key_grad = (
        jnp.einsum("ihst,ishd->ithd", score_grad, query, preferred_element_type=f32) * score_scale
    )
    qkv_grad = (
        jnp.stack((query_grad, key_grad, value_grad), axis=2)
        .reshape(rows, 3, width)
        .astype(bf16)
    )
    normed_a_grad = jnp.einsum(
        "tc,dc->td", qkv_grad.reshape(rows, 3 * width), qkv_weight, preferred_element_type=f32
    )
    gain_a_grad = jnp.sum(normed_a_grad * scaled_a, axis=0)
    shift_a_grad = jnp.sum(normed_a_grad, axis=0)
    input_grad = first_grad + norm_backward(normed_a_grad, scaled_a, inverse_a, gains[0])

    own_qkv_grad = lax.dynamic_slice_in_dim(qkv_grad, head_index * head_cols, head_cols, 2)
    own_mixed = lax.dynamic_slice_in_dim(mixed, head_index * head_cols, head_cols, 1)
    qkv_weight_grad = jnp.einsum("td,tmc->mdc", normed_a, own_qkv_grad, preferred_element_type=f32)
    out_weight_grad = jnp.einsum("td,tc->dc", branch_grad, own_mixed, preferred_element_type=f32)
    attn_grad = jnp.concatenate((qkv_weight_grad, out_weight_grad[None]), axis=0)
    arranged = attn_grad.reshape(tensor_count, mats_here, dp_count, row_shard, head_cols)
    arranged = jnp.transpose(arranged, (2, 0, 1, 3, 4)).reshape(
        dp_count * tensor_count, attn_rows, TILE
    )
    norm_grad = jnp.stack((gain_a_grad, shift_a_grad, gain_b_grad, shift_b_grad))
    norm_grad = norm_grad.reshape(4, dp_count * tensor_count, -1)
    norm_grad = jnp.transpose(norm_grad, (1, 0, 2)).reshape(dp_count * tensor_count, norm_rows, TILE)
    arranged = jnp.concatenate(
        (arranged, router_grad.reshape(dp_count * tensor_count, router_rows, TILE), norm_grad),
        axis=1,
    )
    extra = ceil_to(filled_rows, 16) - filled_rows
    arranged = jnp.pad(arranged, ((0, 0), (0, extra), (0, 0)))
    sums = lax.psum_scatter(arranged, ("dp", "tensor"), scatter_dimension=0, tiled=True)[0]
    attn_sum = sums[:attn_rows].reshape(mats_here, row_shard, head_cols)
    router_sum = sums[attn_rows : attn_rows + router_rows].reshape(router_weight.shape)
    norm_sum = sums[attn_rows + router_rows : filled_rows].reshape(norm_params.shape)

    attn_mom = momentum_decay * attn_momentum + attn_sum
    attn_dir = attn_sum + momentum_decay * attn_mom
    whole = lax.all_gather(attn_dir, ("dp", "heads"), axis=1, tiled=True)
    whole = whole.reshape(mats_here, dp_count, head_count, row_shard, head_cols)
    whole = jnp.transpose(whole, (0, 1, 3, 2, 4)).reshape(mats_here, width, head_count * head_cols)
    whole = whole / (jnp.sqrt(jnp.sum(whole * whole, axis=(1, 2), keepdims=True)) + 1e-07)
    high = lax.Precision.HIGH
    for iteration in range(ITERS):
        gram = jnp.einsum("mij,mkj->mik", whole, whole, precision=high)
        poly = coef_second * gram + coef_third * jnp.einsum(
            "mij,mjk->mik", gram, gram, precision=high
        )
        whole = coef_first * whole + jnp.einsum("mij,mjk->mik", poly, whole, precision=high)
    own_part = lax.dynamic_slice(
        whole, (0, dp_index * row_shard, head_index * head_cols), (mats_here, row_shard, head_cols)
    )
    attn_new = (
        attn_weights * (1.0 - muon_rate * muon_decay)
        - muon_scale(width, head_count * head_cols) * own_part
    )
    router_first_new, router_second_new, router_new = adamw_update(
        router_weight, router_first, router_second, router_sum, router_rate, router_decay
    )
    norm_first_new, norm_second_new, norm_new = adamw_update(
        norm_params, norm_first, norm_second, norm_sum, gains_rate, 0.0
    )
    return (
        block_out,
        input_grad,
        attn_mom,
        attn_new,
        router_first_new,
        router_second_new,
        router_new,
        expert_mom,
        expert_new,
        norm_first_new,
        norm_second_new,
        norm_new,
    )


def solution(mesh):
    in_specs = (
        P(("dp", "tensor"), None),
        P("tensor", "dp", "heads"),
        P("tensor", "dp", "heads"),
        P(("dp", "tensor"), None),
        P(("dp", "tensor"), None),
        P(("dp", "tensor"), None),
        P(("heads", "dp"), None, "tensor"),
        P(("heads", "dp"), None, "tensor"),
        P(None, ("dp", "tensor")),
        P(None, ("dp", "tensor")),
        P(None, ("dp", "tensor")),
        P("dp", None),
        P(("dp", "tensor"), None),
    )
    out_specs = (
        P(("dp", "tensor"), None),
        P(("dp", "tensor"), None),
        P("tensor", "dp", "heads"),
        P("tensor", "dp", "heads"),
        P(("dp", "tensor"), None),
        P(("dp", "tensor"), None),
        P(("dp", "tensor"), None),
        P(("heads", "dp"), None, "tensor"),
        P(("heads", "dp"), None, "tensor"),
        P(None, ("dp", "tensor")),
        P(None, ("dp", "tensor")),
        P(None, ("dp", "tensor")),
    )
    shape = dict(mesh.shape)
    step = EXPERTS * 2 // (shape["heads"] * shape["dp"])
    fits = shape["dp"] == 2 and step % (2 * shape["tensor"]) == 0
    fits = fits and shape["tensor"] % 2 == 0
    shards = shards_fast if fits else shards_general
    return jax.shard_map(shards, mesh=mesh, in_specs=in_specs, out_specs=out_specs, check_vma=False)
```

```python
import functools
import math

import jax
import jax.numpy as jnp
from jax import lax
from jax.experimental import pallas as pl
from jax.experimental.pallas import tpu as pltpu
from jax.sharding import PartitionSpec as P

EXPERTS = 32
SEQ = 197
TOP = 2
ITERS = 5
STEP = 5
HEAD_DIM = 64


norm_epsilon = 1e-06
coef_first = 3.4445
coef_second = -4.775
coef_third = 2.0315
momentum_decay = 0.95
muon_rate = 0.2
muon_decay = 0.1
adam_first = 0.9
adam_second = 0.999
adam_epsilon = 1e-08
router_rate = 0.03
router_decay = 0.01
gains_rate = 0.1
TILE = 128
DP, HEADS, TENSOR = "dp", "heads", "tensor"
TO_ALL, OWN_HEAD, TO_CORE = range(3)
VMEM_LIMIT = 56 * 1024 * 1024


def norm_forward(values, gain, shift):
    center = jnp.mean(values, axis=-1, keepdims=True)
    centred = values - center
    inverse = lax.rsqrt(jnp.mean(centred * centred, axis=-1, keepdims=True) + norm_epsilon)
    scaled = centred * inverse
    return (scaled * gain + shift, scaled, inverse)


def norm_backward(grad_normed, scaled, inverse, gain):
    grad_scaled = grad_normed * gain
    inner = grad_scaled - jnp.mean(grad_scaled, axis=-1, keepdims=True)
    inner = inner - scaled * jnp.mean(grad_scaled * scaled, axis=-1, keepdims=True)
    return inner * inverse


def exact_gelu(values):
    return jax.nn.gelu(values, approximate=False)


def batch_gram(values):
    return jnp.einsum("mij,mkj->mik", values, values, precision=lax.Precision.HIGHEST)


def batch_product(left, right):
    return jnp.einsum("mij,mjk->mik", left, right, precision=lax.Precision.HIGHEST)


def polish_step(values, gram):
    poly = coef_second * gram + coef_third * batch_product(gram, gram)
    return coef_first * values + batch_product(poly, values)


def muon_scale(rows, cols):
    return muon_rate * 0.2 * math.sqrt(max(rows, cols))


def adamw_update(values, first, second, grad, rate, decay):
    first_new = adam_first * first + (1.0 - adam_first) * grad
    second_new = adam_second * second + (1.0 - adam_second) * grad * grad
    first_hat = first_new / (1.0 - adam_first**STEP)
    second_hat = second_new / (1.0 - adam_second**STEP)
    values_new = values * (1.0 - rate * decay) - rate * first_hat / (
        jnp.sqrt(second_hat) + adam_epsilon
    )
    return (first_new, second_new, values_new)


def shards_general(
    images_in,
    attn_weights,
    attn_momentum,
    router_weight,
    router_first,
    router_second,
    expert_weights,
    expert_momentum,
    norm_params,
    norm_first,
    norm_second,
    expert_ids,
    cotangent,
):
    local_rows, width = images_in.shape
    dp_count = lax.axis_size(DP)
    head_count = lax.axis_size(HEADS)
    tensor_count = lax.axis_size(TENSOR)
    mats_here = attn_weights.shape[0]
    row_shard = attn_weights.shape[1]
    head_cols = attn_weights.shape[2]
    hidden_cols = expert_weights.shape[2]
    group_rows = expert_ids.shape[0]
    capacity = 3 * TOP * group_rows // (2 * EXPERTS)
    experts_here = EXPERTS // head_count
    heads_here = head_cols // HEAD_DIM
    images = local_rows // SEQ
    score_scale = HEAD_DIM ** (-0.5)
    head_index = lax.axis_index(HEADS)
    tensor_index = lax.axis_index(TENSOR)
    dp_index = lax.axis_index(DP)
    attn_low, router_low, norms_low = (
        lax.all_gather(attn_weights.astype(jnp.bfloat16), (DP, TENSOR), axis=0, tiled=True),
        lax.all_gather(router_weight.astype(jnp.bfloat16), (DP, TENSOR), axis=0, tiled=True),
        lax.all_gather(norm_params.astype(jnp.bfloat16), (DP, TENSOR), axis=1, tiled=True),
    )
    attn_low = attn_low.reshape(dp_count, tensor_count * mats_here, row_shard, head_cols)
    attn_low = jnp.transpose(attn_low, (1, 0, 2, 3)).reshape(
        tensor_count * mats_here, width, head_cols
    )
    gains = norms_low.astype(jnp.float32)
    qkv_weight = jnp.transpose(attn_low[:3], (1, 0, 2)).reshape(width, 3 * head_cols)
    out_weight = attn_low[3]
    tokens = images_in.astype(jnp.float32)
    normed_a, scaled_a, inverse_a = norm_forward(tokens, gains[0], gains[1])
    normed_a = normed_a.astype(jnp.bfloat16)
    qkv = jnp.dot(normed_a, qkv_weight, preferred_element_type=jnp.float32).astype(jnp.bfloat16)
    split = qkv.reshape(images, SEQ, 3, heads_here, HEAD_DIM)
    query = split[:, :, 0]
    keys = split[:, :, 1]
    values = split[:, :, 2]
    scores = (
        jnp.einsum("ishd,ithd->ihst", query, keys, preferred_element_type=jnp.float32) * score_scale
    )
    peak = jnp.max(scores, axis=-1, keepdims=True)
    logsum = peak + jnp.log(jnp.sum(jnp.exp(scores - peak), axis=-1, keepdims=True))
    probs_low = jnp.exp(scores - logsum).astype(jnp.bfloat16)
    mixed = jnp.einsum("ihst,ithd->ishd", probs_low, values, preferred_element_type=jnp.float32)
    mixed = mixed.reshape(local_rows, head_cols).astype(jnp.bfloat16)
    partial_out = jnp.einsum("tc,dc->td", mixed, out_weight, preferred_element_type=jnp.float32)
    attended = lax.psum(partial_out, HEADS)
    first = tokens + attended
    normed_b, scaled_b, inverse_b = norm_forward(first, gains[2], gains[3])
    normed_b = normed_b.astype(jnp.bfloat16)
    group_in, group_cot = (
        lax.all_gather(normed_b, TENSOR, axis=0, tiled=True),
        lax.all_gather(cotangent, TENSOR, axis=0, tiled=True),
    )
    logits = jnp.dot(group_in, router_low, preferred_element_type=jnp.float32)
    chosen = jnp.take_along_axis(logits, expert_ids, axis=1)
    raised = jnp.exp(chosen - jnp.max(chosen, axis=1, keepdims=True))
    gates = raised / jnp.sum(raised, axis=1, keepdims=True)
    routes = expert_ids.reshape(-1)
    route_count = routes.shape[0]
    order = jnp.argsort(routes * route_count + jnp.arange(route_count, dtype=jnp.int32))
    labels = head_index * experts_here + jnp.arange(experts_here, dtype=jnp.int32)
    counts = jnp.sum((routes[None, :] == labels[:, None]).astype(jnp.int32), axis=1)
    starts = jnp.sum((routes[None, :] < labels[:, None]).astype(jnp.int32), axis=1)
    slot_index = jnp.arange(capacity, dtype=jnp.int32)
    picked = order[jnp.minimum(starts[:, None] + slot_index[None, :], route_count - 1)]
    filled = (slot_index[None, :] < counts[:, None]).astype(jnp.float32)
    token_rows = (picked // TOP).reshape(-1)
    pick_cols = (picked % TOP).reshape(-1)
    slot_gate = gates[token_rows, pick_cols].reshape(experts_here, capacity) * filled
    slot_in = group_in[token_rows].reshape(experts_here, capacity, width)
    pair = lax.all_gather(expert_weights.astype(jnp.bfloat16), DP, axis=0, tiled=True).reshape(
        experts_here, 2, width, hidden_cols
    )
    hidden = jnp.einsum("ecd,edf->ecf", slot_in, pair[:, 0], preferred_element_type=jnp.float32)
    active, gelu_pull = jax.vjp(exact_gelu, hidden)
    active = active.astype(jnp.bfloat16)
    expert_out = jnp.einsum("ecf,edf->ecd", active, pair[:, 1], preferred_element_type=jnp.float32)
    weighted = (expert_out * slot_gate[:, :, None]).reshape(-1, width)
    spread = jnp.zeros((group_rows, width), jnp.float32).at[token_rows].add(weighted)
    own_sum = lax.psum_scatter(spread, TENSOR, scatter_dimension=0, tiled=True)
    moe_out = lax.psum(own_sum, HEADS)
    block_out = first + moe_out
    grad_out = cotangent.astype(jnp.float32)
    slot_cot = group_cot[token_rows].reshape(experts_here, capacity, width).astype(jnp.float32)
    gate_grad = jnp.sum(slot_cot * expert_out, axis=-1) * filled
    out_grad = (slot_cot * slot_gate[:, :, None]).astype(jnp.bfloat16)
    pair_back = lax.all_gather(
        expert_weights.astype(jnp.bfloat16), DP, axis=0, tiled=True
    ).reshape(experts_here, 2, width, hidden_cols)
    active_grad = jnp.einsum(
        "ecd,edf->ecf", out_grad, pair_back[:, 1], preferred_element_type=jnp.float32
    )
    hidden_grad = gelu_pull(active_grad)[0].astype(jnp.bfloat16)
    down_grad = jnp.einsum("ecd,ecf->edf", out_grad, active, preferred_element_type=jnp.float32)
    up_grad = jnp.einsum("ecd,ecf->edf", slot_in, hidden_grad, preferred_element_type=jnp.float32)
    slot_in_grad = jnp.einsum(
        "ecf,edf->ecd", hidden_grad, pair_back[:, 0], preferred_element_type=jnp.float32
    ).reshape(-1, width)
    back_spread = jnp.zeros((group_rows, width), jnp.float32).at[token_rows].add(slot_in_grad)
    gate_spread = (
        jnp.zeros((group_rows, TOP), jnp.float32)
        .at[token_rows, pick_cols]
        .add(gate_grad.reshape(-1))
    )
    own_back, own_gate = (
        lax.psum_scatter(back_spread, TENSOR, scatter_dimension=0, tiled=True),
        lax.psum_scatter(gate_spread, TENSOR, scatter_dimension=0, tiled=True),
    )
    normed_b_grad, gate_total = lax.psum((own_back, own_gate), HEADS)
    matrix_grads = jnp.stack((up_grad, down_grad), axis=1).reshape(
        2 * experts_here, width, hidden_cols
    )
    expert_grad = lax.psum_scatter(matrix_grads, DP, scatter_dimension=0, tiled=True)
    own_ids = lax.dynamic_slice_in_dim(expert_ids, tensor_index * local_rows, local_rows, 0)
    own_gates = lax.dynamic_slice_in_dim(gates, tensor_index * local_rows, local_rows, 0)
    blend = jnp.sum(own_gates * gate_total, axis=1, keepdims=True)
    chosen_grad = own_gates * (gate_total - blend)
    expert_labels = jnp.arange(EXPERTS, dtype=jnp.int32)
    matches = (own_ids[:, :, None] == expert_labels[None, None, :]).astype(jnp.float32)
    logit_grad = jnp.sum(matches * chosen_grad[:, :, None], axis=1).astype(jnp.bfloat16)
    normed_b_grad = normed_b_grad + jnp.einsum(
        "te,de->td", logit_grad, router_low, preferred_element_type=jnp.float32
    )
    router_grad = jnp.einsum("td,te->de", normed_b, logit_grad, preferred_element_type=jnp.float32)
    gain_b_grad = jnp.sum(normed_b_grad * scaled_b, axis=0)
    shift_b_grad = jnp.sum(normed_b_grad, axis=0)
    first_grad = grad_out + norm_backward(normed_b_grad, scaled_b, inverse_b, gains[2])
    branch_grad = first_grad.astype(jnp.bfloat16)
    out_weight_grad = jnp.einsum(
        "td,tc->dc", branch_grad, mixed, preferred_element_type=jnp.float32
    )
    mixed_grad = jnp.einsum(
        "td,dc->tc", branch_grad, out_weight, preferred_element_type=jnp.float32
    ).astype(jnp.bfloat16)
    mixed_grad = mixed_grad.reshape(images, SEQ, heads_here, HEAD_DIM)
    scores_again = (
        jnp.einsum("ishd,ithd->ihst", query, keys, preferred_element_type=jnp.float32) * score_scale
    )
    probs_again = jnp.exp(scores_again - logsum)
    prob_grad = jnp.einsum(
        "ishd,ithd->ihst", mixed_grad, values, preferred_element_type=jnp.float32
    )
    value_grad = jnp.einsum(
        "ihst,ishd->ithd",
        probs_again.astype(jnp.bfloat16),
        mixed_grad,
        preferred_element_type=jnp.float32,
    )
    score_grad = (
        probs_again * (prob_grad - jnp.sum(probs_again * prob_grad, axis=-1, keepdims=True))
    ).astype(jnp.bfloat16)
    query_grad = (
        jnp.einsum("ihst,ithd->ishd", score_grad, keys, preferred_element_type=jnp.float32)
        * score_scale
    )
    key_grad = (
        jnp.einsum("ihst,ishd->ithd", score_grad, query, preferred_element_type=jnp.float32)
        * score_scale
    )
    qkv_grad = (
        jnp.stack((query_grad, key_grad, value_grad), axis=2)
        .reshape(local_rows, 3 * head_cols)
        .astype(jnp.bfloat16)
    )
    normed_a_part = jnp.einsum(
        "tc,dc->td", qkv_grad, qkv_weight, preferred_element_type=jnp.float32
    )
    qkv_weight_grad = jnp.einsum(
        "td,tc->dc", normed_a, qkv_grad, preferred_element_type=jnp.float32
    )
    normed_a_grad = lax.psum(normed_a_part, HEADS)
    gain_a_grad = jnp.sum(normed_a_grad * scaled_a, axis=0)
    shift_a_grad = jnp.sum(normed_a_grad, axis=0)
    input_grad = first_grad + norm_backward(normed_a_grad, scaled_a, inverse_a, gains[0])
    attn_grad = jnp.concatenate(
        (
            jnp.transpose(qkv_weight_grad.reshape(width, 3, head_cols), (1, 0, 2)),
            out_weight_grad[None],
        ),
        axis=0,
    )
    arranged = attn_grad.reshape(tensor_count, mats_here, dp_count, row_shard, head_cols)
    arranged = jnp.transpose(arranged, (2, 0, 1, 3, 4)).reshape(
        dp_count * tensor_count * mats_here, row_shard, head_cols
    )
    norm_grad = jnp.stack((gain_a_grad, shift_a_grad, gain_b_grad, shift_b_grad))
    attn_sum, router_sum, norm_sum = (
        lax.psum_scatter(arranged, (DP, TENSOR), scatter_dimension=0, tiled=True),
        lax.psum_scatter(router_grad, (DP, TENSOR), scatter_dimension=0, tiled=True),
        lax.psum_scatter(norm_grad, (DP, TENSOR), scatter_dimension=1, tiled=True),
    )
    attn_mom = momentum_decay * attn_momentum + attn_sum
    attn_dir = attn_sum + momentum_decay * attn_mom
    whole = lax.all_gather(attn_dir, (DP, HEADS), axis=1, tiled=True)
    whole = whole.reshape(mats_here, dp_count, head_count, row_shard, head_cols)
    whole = jnp.transpose(whole, (0, 1, 3, 2, 4)).reshape(mats_here, width, head_count * head_cols)
    whole = whole / (jnp.sqrt(jnp.sum(whole * whole, axis=(1, 2), keepdims=True)) + 1e-07)
    for iteration in range(ITERS):
        whole = polish_step(whole, batch_gram(whole))
    own_part = lax.dynamic_slice(
        whole, (0, dp_index * row_shard, head_index * head_cols), (mats_here, row_shard, head_cols)
    )
    attn_new = (
        attn_weights * (1.0 - muon_rate * muon_decay)
        - muon_scale(width, head_count * head_cols) * own_part
    )
    expert_mom = momentum_decay * expert_momentum + expert_grad
    current = expert_grad + momentum_decay * expert_mom
    for iteration in range(ITERS):
        gram = lax.psum(batch_gram(current), TENSOR)
        if iteration == 0:
            factor = 1.0 / (jnp.sqrt(jnp.trace(gram, axis1=1, axis2=2)) + 1e-07)
            factor = factor[:, None, None]
            current = current * factor
            gram = gram * (factor * factor)
        current = polish_step(current, gram)
    expert_new = (
        expert_weights * (1.0 - muon_rate * muon_decay)
        - muon_scale(width, hidden_cols * tensor_count) * current
    )
    router_first_new, router_second_new, router_new = adamw_update(
        router_weight, router_first, router_second, router_sum, router_rate, router_decay
    )
    norm_first_new, norm_second_new, norm_new = adamw_update(
        norm_params, norm_first, norm_second, norm_sum, gains_rate, 0.0
    )
    return (
        block_out,
        input_grad,
        attn_mom,
        attn_new,
        router_first_new,
        router_second_new,
        router_new,
        expert_mom,
        expert_new,
        norm_first_new,
        norm_second_new,
        norm_new,
    )


def ceil_to(value, step):
    return -(-value // step) * step


def dot_exact(left, right):
    return jnp.dot(
        left, right, precision=lax.Precision.HIGH, preferred_element_type=jnp.float32
    )


def dot_low(left, right, contract=((1,), (0,))):
    return lax.dot_general(
        left, right, (contract, ((), ())), preferred_element_type=jnp.float32
    )


def block_pairs(width):
    tiles = width // TILE
    return [(i, j) for i in range(tiles) for j in range(i + 1, tiles)]


def packed_rows(width):
    tiles = width // TILE
    return (len(block_pairs(width)) + tiles // 2) * TILE + ceil_to(tiles // 2, 8)


def tile_places():
    rows = lax.broadcasted_iota(jnp.int32, (TILE, TILE), 0)
    lanes = lax.broadcasted_iota(jnp.int32, (TILE, TILE), 1)
    return rows, lanes


def pack_upper(block, width, out_ref):
    rows, lanes = tile_places()
    start = 0
    for i, j in block_pairs(width):
        out_ref[start : start + TILE, :] = block(i, j)
        start += TILE
    diagonals = []
    for i in range(0, width // TILE, 2):
        second = block(i + 1, i + 1)
        out_ref[start : start + TILE, :] = jnp.where(rows <= lanes, block(i, i), second)
        diagonals.append(
            jnp.sum(jnp.where(rows == lanes, second, 0.0), axis=0, keepdims=True)
        )
        start += TILE
    rest = out_ref.shape[0] - start - len(diagonals)
    if rest:
        diagonals.append(jnp.zeros((rest, TILE), jnp.float32))
    out_ref[start:, :] = jnp.concatenate(diagonals, axis=0)


def packed_trace(packed_ref, width):
    rows, lanes = tile_places()
    start = len(block_pairs(width)) * TILE
    total = jnp.zeros((1, 1), jnp.float32)
    pairs = width // TILE // 2
    for pair in range(pairs):
        block = packed_ref[start + pair * TILE : start + (pair + 1) * TILE, :]
        total = total + jnp.sum(jnp.where(rows == lanes, block, 0.0), keepdims=True)
    return total + jnp.sum(packed_ref[start + pairs * TILE :, :], keepdims=True)


def unpack_upper(packed_ref, out_ref, factor=None):
    rows, lanes = tile_places()
    width = out_ref.shape[0]

    def load(start, count):
        values = packed_ref[start : start + count, :]
        return values if factor is None else values * factor

    start = 0
    for i, j in block_pairs(width):
        block = load(start, TILE)
        out_ref[i * TILE : (i + 1) * TILE, j * TILE : (j + 1) * TILE] = block
        out_ref[j * TILE : (j + 1) * TILE, i * TILE : (i + 1) * TILE] = block.T
        start += TILE
    diagonals = load(start + width // 2, 8)
    for i in range(0, width // TILE, 2):
        block = load(start, TILE)
        turned = block.T
        first = jnp.where(rows <= lanes, block, turned)
        second = jnp.where(rows > lanes, block, turned)
        second = jnp.where(rows == lanes, diagonals[i // 2 : i // 2 + 1], second)
        out_ref[i * TILE : (i + 1) * TILE, i * TILE : (i + 1) * TILE] = first
        i += 1
        out_ref[i * TILE : (i + 1) * TILE, i * TILE : (i + 1) * TILE] = second
        start += TILE


def gram_packed(values, out_ref):
    rows = values.shape[0]
    half = rows // 2
    contract = (((1,), (1,)), ((), ()))
    upper = lax.dot_general(
        values[:half], values, contract,
        precision=lax.Precision.HIGH, preferred_element_type=jnp.float32,
    )
    lower = lax.dot_general(
        values[half:], values[half:], contract,
        precision=lax.Precision.HIGH, preferred_element_type=jnp.float32,
    )

    def block(i, j):
        top, left = i * TILE, j * TILE
        if top < half:
            return upper[top : top + TILE, left : left + TILE]
        return lower[top - half : top - half + TILE, left - half : left - half + TILE]

    pack_upper(block, rows, out_ref)


def own_label(experts, number):
    shard = lax.axis_index(HEADS) * lax.axis_size(DP) + lax.axis_index(DP)
    return shard * experts + number


def expert_kernel(
    first, slot_in_ref, slot_cot_ref, member_ref, router_ref, weight_ref, momentum_ref,
    momentum_out, back_out, gate_out, ahead_out, dir_out, gram_out,
):
    experts = EXPERTS // (lax.axis_size(HEADS) * lax.axis_size(DP))
    label = own_label(experts, first + pl.program_id(0))
    rows = slot_in_ref.shape[1] * slot_in_ref.shape[2]
    slot_in = slot_in_ref[0].reshape(rows, -1)
    slot_cot = slot_cot_ref[0].reshape(rows, -1).astype(jnp.float32)
    member = member_ref[0].reshape(rows, EXPERTS)
    logits = dot_low(slot_in, router_ref[...], ((1,), (1,)))
    lanes = lax.broadcasted_iota(jnp.int32, logits.shape, 1)
    own = jnp.where(lanes == label, 1.0, 0.0)
    filled = jnp.sum(member * own, axis=1, keepdims=True)
    logit_own = jnp.sum(logits * own, axis=1, keepdims=True)
    logit_other = jnp.sum(logits * (member - own), axis=1, keepdims=True)
    peak = jnp.maximum(logit_own, logit_other)
    raised = jnp.exp(logit_own - peak)
    gate = filled * raised / (raised + jnp.exp(logit_other - peak))
    up = weight_ref[0].astype(jnp.bfloat16)
    down = weight_ref[1].astype(jnp.bfloat16)
    hidden = dot_low(slot_in, up)
    cdf = 0.5 * (1.0 + lax.erf(hidden * math.sqrt(0.5)))
    active = (hidden * cdf).astype(jnp.bfloat16)
    slope = cdf + hidden * jnp.exp(-0.5 * hidden * hidden) * (1.0 / math.sqrt(2.0 * math.pi))
    expert_out = dot_low(active, down, ((1,), (1,)))
    gate_grad = jnp.sum(slot_cot * expert_out, axis=1, keepdims=True) * filled
    ahead_out[0] = (expert_out * gate).astype(jnp.bfloat16)
    out_grad = (slot_cot * gate).astype(jnp.bfloat16)
    hidden_grad = (dot_low(out_grad, down) * slope).astype(jnp.bfloat16)
    back_out[0] = dot_low(hidden_grad, up, ((1,), (1,))).astype(jnp.bfloat16)
    wide = lax.broadcasted_iota(jnp.int32, (gate_grad.shape[0], TILE), 1)
    high = gate_grad.astype(jnp.bfloat16).astype(jnp.float32)
    spread = jnp.where(wide == label, high, 0.0)
    spread = jnp.where(wide == label + EXPERTS, gate_grad - high, spread)
    gate_out[0] = spread.astype(jnp.bfloat16)
    for which, grad in enumerate(
        (
            dot_low(slot_in, hidden_grad, ((0,), (0,))),
            dot_low(out_grad, active, ((0,), (0,))),
        )
    ):
        momentum = momentum_decay * momentum_ref[which] + grad
        momentum_out[which] = momentum
        direction = grad + momentum_decay * momentum
        dir_out[which] = direction
        gram_packed(direction, gram_out.at[which])


def run_experts(first, count, slot_in, slot_cot, member, router, weights, momentum, earlier):
    _, groups, slots, width = slot_in.shape
    mats, _, hidden = weights.shape
    packed = packed_rows(width)
    shape = jax.ShapeDtypeStruct
    whole = (
        shape((mats, width, hidden), jnp.float32),
        shape((mats // 2, groups * slots, width), jnp.bfloat16),
        shape((mats // 2, groups * slots, TILE), jnp.bfloat16),
        shape((mats // 2, groups * slots, width), jnp.bfloat16),
    )
    part = (
        shape((2 * count, width, hidden), jnp.float32),
        shape((2 * count, packed, TILE), jnp.float32),
    )

    def shifted(e):
        return (first + e, 0, 0)

    def here(e):
        return (e, 0, 0)

    def slotted(e):
        return (first + e, 0, 0, 0)

    def kernel(*refs):
        expert_kernel(first, *refs[:6], *refs[6 + len(earlier) :])

    return pl.pallas_call(
        kernel,
        grid=(count,),
        in_specs=[
            pl.BlockSpec((1, groups, slots, width), slotted),
            pl.BlockSpec((1, groups, slots, width), slotted),
            pl.BlockSpec((1, groups, slots, EXPERTS), slotted),
            pl.BlockSpec(router.shape, lambda e: (0, 0)),
            pl.BlockSpec((2, width, hidden), shifted),
            pl.BlockSpec((2, width, hidden), shifted),
        ]
        + [pl.BlockSpec(memory_space=pl.ANY)] * len(earlier),
        out_specs=[
            pl.BlockSpec((2, width, hidden), shifted),
            pl.BlockSpec((1, groups * slots, width), shifted),
            pl.BlockSpec((1, groups * slots, TILE), shifted),
            pl.BlockSpec((1, groups * slots, width), shifted),
            pl.BlockSpec((2, width, hidden), here),
            pl.BlockSpec((2, packed, TILE), here),
        ],
        out_shape=whole + part,
        input_output_aliases={6 + place: place for place in range(len(earlier))},
        compiler_params=pltpu.CompilerParams(vmem_limit_bytes=VMEM_LIMIT),
        name="experts",
    )(slot_in, slot_cot, member, router, weights, momentum, *earlier)


def polish_kernel(packed_ref, out_ref, gram, poly, product):
    width = gram.shape[0]
    half = width // 2
    trace = packed_trace(packed_ref.at[0], width)
    factor = 1.0 / (jnp.sqrt(trace) + 1e-07)
    unpack_upper(packed_ref.at[0], gram, factor * factor)

    def symmetric(left, right):
        upper = dot_exact(left[:half, :], right[...])
        corner = dot_exact(left[half:, :], right[:, half:])
        return upper, corner

    def store(ref, upper, corner):
        ref[:half, :] = upper
        ref[half:, half:] = corner
        ref[half:, :half] = upper[:, half:].T

    def eye(offset, count):
        here = lax.broadcasted_iota(jnp.int32, (half, count), 0)
        there = lax.broadcasted_iota(jnp.int32, (half, count), 1)
        return jnp.where(here == there, coef_first, 0.0)

    for step in range(ITERS):
        upper, corner = symmetric(gram, gram)
        upper = eye(0, width) + coef_second * gram[:half, :] + coef_third * upper
        corner = eye(0, half) + coef_second * gram[half:, half:] + coef_third * corner
        store(poly, upper, corner)
        if step == 0:
            store(product, upper, corner)
        else:
            store(product, *symmetric(poly, product))
        if step < ITERS - 1:
            store(poly, *symmetric(poly, poly))
            store(gram, *symmetric(gram, poly))

    def block(i, j):
        return product[i * TILE : (i + 1) * TILE, j * TILE : (j + 1) * TILE] * factor

    pack_upper(block, width, out_ref.at[0])


def run_polish(packed, width):
    return pl.pallas_call(
        polish_kernel,
        grid=(packed.shape[0],),
        in_specs=[pl.BlockSpec((1,) + packed.shape[1:], lambda m: (m, 0, 0))],
        out_specs=pl.BlockSpec((1,) + packed.shape[1:], lambda m: (m, 0, 0)),
        out_shape=jax.ShapeDtypeStruct(packed.shape, jnp.float32),
        scratch_shapes=[pltpu.VMEM((width, width), jnp.float32)] * 3,
        compiler_params=pltpu.CompilerParams(vmem_limit_bytes=VMEM_LIMIT),
        name="polish",
    )(packed)


def apply_kernel(scale, packed_ref, dir_ref, weight_ref, out_ref, whole):
    unpack_upper(packed_ref.at[0], whole)
    ortho = dot_exact(whole[...], dir_ref[0])
    out_ref[0] = weight_ref[0] * (1.0 - muon_rate * muon_decay) - scale * ortho


def run_apply(first, scale, packed, direction, weights, earlier):
    count, width, hidden = direction.shape

    def kernel(packed_ref, dir_ref, weight_ref, *refs):
        apply_kernel(scale, packed_ref, dir_ref, weight_ref, *refs[len(earlier) :])

    return pl.pallas_call(
        kernel,
        grid=(count,),
        in_specs=[
            pl.BlockSpec((1,) + packed.shape[1:], lambda m: (m, 0, 0)),
            pl.BlockSpec((1, width, hidden), lambda m: (m, 0, 0)),
            pl.BlockSpec((1, width, hidden), lambda m: (first + m, 0, 0)),
        ]
        + [pl.BlockSpec(memory_space=pl.ANY)] * len(earlier),
        out_specs=pl.BlockSpec((1, width, hidden), lambda m: (first + m, 0, 0)),
        out_shape=jax.ShapeDtypeStruct(weights.shape, jnp.float32),
        input_output_aliases={3 + place: place for place in range(len(earlier))},
        scratch_shapes=[pltpu.VMEM((width, width), jnp.float32)],
        compiler_params=pltpu.CompilerParams(vmem_limit_bytes=VMEM_LIMIT),
        name="apply",
    )(packed, direction, weights, *earlier)


def neighbours(index, count):
    return [lax.rem(index + step, count) for step in range(1, count)]


def square_peers(index):
    return [3 - index, index + 1 - 2 * lax.rem(index, 2), lax.rem(index + 2, 4)]


def enter(peers):
    barrier = pltpu.get_barrier_semaphore()
    for peer in peers:
        pl.semaphore_signal(barrier, inc=1, device_id=peer, device_id_type=pl.DeviceIdType.MESH)
    pl.semaphore_wait(barrier, len(peers))


def send(source, target, send_sem, recv_sem, peer):
    copy = pltpu.make_async_remote_copy(
        src_ref=source,
        dst_ref=target,
        send_sem=send_sem,
        recv_sem=recv_sem,
        device_id=peer,
        device_id_type=pl.DeviceIdType.MESH,
    )
    copy.start()
    return copy


class Sharing:
    def __init__(self, values, out, sems):
        self.values, self.out, self.sems = values, out, sems
        self.core, self.tensor = lax.axis_index(DP), lax.axis_index(TENSOR)
        self.head, self.places = lax.axis_index(HEADS), lax.axis_size(TENSOR)
        self.along = neighbours(self.tensor, self.places)
        self.diagonal, self.beside, self.above = square_peers(self.head)
        self.origins = [self.tensor] + [
            lax.rem(self.tensor + self.places - step, self.places)
            for step in range(1, self.places)
        ]
        self.here = out.at[self.core, self.tensor, self.head]
        self.started = []

    def start(self):
        self.home = pltpu.make_async_copy(self.values, self.here, self.sems[0])
        self.home.start()
        for step, peer in enumerate(self.along):
            self.started.append(
                send(
                    self.values, self.here, self.sems[1].at[step], self.sems[2].at[step],
                    {TENSOR: peer},
                )
            )

    def to_partner(self, block, source, number):
        self.started.append(
            send(
                source, block, self.sems[5].at[number], self.sems[6].at[number],
                {DP: 1 - self.core},
            )
        )

    def to_sides(self, block, source, place):
        for step, peer in enumerate((self.beside, self.above)):
            number = 4 * place + step
            self.started.append(
                send(
                    source, block, self.sems[3].at[number], self.sems[4].at[number],
                    {HEADS: peer},
                )
            )

    def cut(self, block):
        rows = block.shape[0]
        middle = ceil_to(rows // 2, 16)
        return block.at[pl.ds(0, middle)], block.at[pl.ds(middle, rows - middle)]

    def pass_to_sides(self):
        self.to_sides(self.here, self.values, 0)
        self.to_partner(self.here, self.values, 0)
        for place in range(1, self.places):
            block = self.out.at[self.core, self.origins[place], self.head]
            wait_for(block, self.sems[2].at[place - 1])
            self.to_sides(block, block, place)
            self.to_partner(block, block, 4 * place)

    def pass_round(self):
        ways = ((self.beside, self.above), (self.above, self.beside))
        for place in range(self.places):
            for step, (peer, other) in enumerate(ways):
                block = self.out.at[self.core, self.origins[place], peer]
                wait_for(block, self.sems[4].at[4 * place + step])
                half = self.cut(block)[step]
                number = 4 * place + 2 + step
                self.started.append(
                    send(
                        half, half, self.sems[3].at[number], self.sems[4].at[number],
                        {HEADS: other},
                    )
                )
                self.to_partner(block, block, 4 * place + 1 + step)

    def own_group(self):
        for place in range(self.places):
            block = self.out.at[self.core, self.origins[place], self.diagonal]
            for step, half in enumerate(self.cut(block)):
                wait_for(half, self.sems[4].at[4 * place + 2 + step])
            self.to_partner(block, block, 4 * place + 3)
        self.home.wait()

    def other_group(self):
        corners = (self.head, self.beside, self.above, self.diagonal)
        for place in range(self.places):
            for step, peer in enumerate(corners):
                block = self.out.at[1 - self.core, self.origins[place], peer]
                wait_for(block, self.sems[6].at[4 * place + step])

    def finish(self):
        for copy in self.started:
            copy.wait_send()


def sharing_sems(places, corners):
    dma = pltpu.SemaphoreType.DMA
    blocks = places * corners
    return [dma(()), dma((places - 1,)), dma((places - 1,))] + [dma((blocks,))] * 4


def wait_for(block, sem):
    pltpu.make_async_copy(block, block, sem).wait()


def attn_kernel(
    grads, momentum, sums_out, whole,
    own, from_core, merged, low, from_z, from_z_small, sums, direction,
    own_sem, core_send, core_recv, z_send, z_recv, xy_send, xy_recv, pass_send, pass_recv,
):
    core = lax.axis_index(DP)
    tensor = lax.axis_index(TENSOR)
    head = lax.axis_index(HEADS)
    count = lax.axis_size(TENSOR)
    along = neighbours(tensor, count)
    across = square_peers(head)
    partner = 1 - core
    enter(
        [{TENSOR: peer} for peer in along]
        + [{HEADS: peer} for peer in across]
        + [{DP: partner}]
    )
    started = [
        send(grads.at[partner], from_core, core_send, core_recv, {DP: partner})
    ]
    load = pltpu.make_async_copy(grads.at[core], own, own_sem.at[0])
    load.start()
    load.wait()
    wait_for(from_core, core_recv)
    rows = momentum.shape[0]
    for place in range(count):
        both = own[place] + from_core[place]
        merged[place] = both
        low[place] = both[:rows].astype(low.dtype)
    for step, peer in enumerate(along):
        started.append(
            send(
                low.at[peer], from_z.at[step], z_send.at[step], z_recv.at[step], {TENSOR: peer}
            )
        )
    others = len(along)
    for step, peer in enumerate(along):
        started.append(
            send(
                merged.at[peer, pl.ds(rows, from_z_small.shape[1])], from_z_small.at[step],
                z_send.at[others + step], z_recv.at[others + step], {TENSOR: peer},
            )
        )
    grad = merged[tensor, :rows, :]
    small = merged[tensor, rows:, :]
    for step in range(others):
        wait_for(from_z.at[step], z_recv.at[step])
        grad = grad + from_z[step].astype(jnp.float32)
        wait_for(from_z_small.at[step], z_recv.at[others + step])
        small = small + from_z_small[step]
    sums[:rows, :] = grad
    sums[rows:, :] = small
    direction[...] = grad + momentum_decay * (momentum_decay * momentum[...] + grad)
    here = whole.at[core, head]
    homes = [
        pltpu.make_async_copy(sums, sums_out, own_sem.at[1]),
        pltpu.make_async_copy(direction, here, own_sem.at[2]),
    ]
    for copy in homes:
        copy.start()
    for step, peer in enumerate(across):
        started.append(
            send(direction, here, xy_send.at[step], xy_recv.at[step], {HEADS: peer})
        )
    started.append(send(direction, here, pass_send.at[0], pass_recv.at[0], {DP: partner}))
    for step, peer in enumerate(across):
        block = whole.at[core, peer]
        wait_for(block, xy_recv.at[step])
        started.append(
            send(block, block, pass_send.at[step + 1], pass_recv.at[step + 1], {DP: partner})
        )
    for step, peer in enumerate([head] + across):
        wait_for(whole.at[partner, peer], pass_recv.at[step])
    for copy in homes:
        copy.wait()
    for copy in started:
        copy.wait_send()


def attn_exchange(grads, momentum, number):
    _, _, rows, lanes = grads.shape
    dp_count, head_count = lax.axis_size(DP), lax.axis_size(HEADS)
    tensor_count = lax.axis_size(TENSOR)
    others = head_count - 1
    f32 = jnp.float32
    dma = pltpu.SemaphoreType.DMA
    return pl.pallas_call(
        attn_kernel,
        in_specs=[
            pl.BlockSpec(memory_space=pl.ANY),
            pl.BlockSpec(memory_space=pltpu.VMEM),
        ],
        out_specs=[pl.BlockSpec(memory_space=pl.ANY)] * 2,
        out_shape=[
            jax.ShapeDtypeStruct((rows, lanes), f32),
            jax.ShapeDtypeStruct((dp_count, head_count) + momentum.shape, f32),
        ],
        scratch_shapes=[
            pltpu.VMEM((tensor_count, rows, lanes), f32),
            pltpu.VMEM((tensor_count, rows, lanes), f32),
            pltpu.VMEM((tensor_count, rows, lanes), f32),
            pltpu.VMEM((tensor_count,) + momentum.shape, jnp.bfloat16),
            pltpu.VMEM((tensor_count - 1,) + momentum.shape, jnp.bfloat16),
            pltpu.VMEM((tensor_count - 1, rows - momentum.shape[0], lanes), f32),
            pltpu.VMEM((rows, lanes), f32),
            pltpu.VMEM(momentum.shape, f32),
            dma((3,)),
            dma(()),
            dma(()),
            dma((2 * (tensor_count - 1),)),
            dma((2 * (tensor_count - 1),)),
            dma((others,)),
            dma((others,)),
            dma((head_count,)),
            dma((head_count,)),
        ],
        compiler_params=pltpu.CompilerParams(
            collective_id=number, has_side_effects=True, vmem_limit_bytes=VMEM_LIMIT
        ),
        name="attn_exchange",
    )(grads, momentum)


class Combining:
    def __init__(self, payloads, out, exact_out, scratch, sems):
        self.payloads, self.out, self.exact_out = payloads, out, exact_out
        self.widths = [payload.shape[3] for payload in payloads]
        (
            self.stage, self.own, self.from_core, self.merged, self.from_side, self.relay,
            self.from_next, self.low, self.from_z, self.done, *self.exact,
        ) = scratch
        (
            self.home_sem, self.core_send, self.core_recv, self.xy_send, self.xy_recv,
            self.z_send, self.z_recv, self.back_send, self.back_recv,
        ) = sems
        self.core, self.tensor = lax.axis_index(DP), lax.axis_index(TENSOR)
        self.head, self.places = lax.axis_index(HEADS), lax.axis_size(TENSOR)
        self.across = square_peers(self.head)
        self.order = neighbours(self.tensor, self.places) + [self.tensor]
        self.quarter = self.done.shape[0]
        self.started, self.homes = [], []
        self.result = None

    def send(self, *args):
        self.started.append(send(*args))

    def write(self, ref, number, pick, group):
        start = 0
        for payload, width in zip(self.payloads, self.widths):
            slots = payload[:, group].reshape(-1, width)
            ref[number, :, start : start + width] = dot_low(pick, slots).astype(ref.dtype)
            start += width

    def spread(self, number, picks):
        self.write(self.stage, number, picks[1], 1 - self.core)
        self.send(
            self.stage.at[number], self.from_core.at[number], self.core_send.at[number],
            self.core_recv.at[number], {DP: 1 - self.core},
        )
        self.write(self.own, number, picks[0], self.core)

    def sides(self, number):
        _, beside, above = self.across
        return (beside, above) if number % 2 == 0 else (above, beside)

    def rows(self, corner):
        return pl.ds(pl.multiple_of(corner * self.quarter, 16), self.quarter)

    def exchange(self, number):
        wait_for(self.from_core.at[number], self.core_recv.at[number])
        both = self.own[number] + self.from_core[number].astype(jnp.float32)
        self.own[number] = both
        self.merged[number] = both.astype(jnp.bfloat16)
        side = self.sides(number)[0]
        for step, corner in enumerate((self.across[0], side)):
            place = 3 * number + step
            self.send(
                self.merged.at[number, self.rows(corner)], self.from_side.at[number, step],
                self.xy_send.at[place], self.xy_recv.at[place], {HEADS: side},
            )

    def pass_on(self, number):
        following = self.sides(number)[1]
        place = 3 * number
        wait_for(self.from_side.at[number, 0], self.xy_recv.at[place])
        both = self.own[number, self.rows(following), :]
        both = both + self.from_side[number, 0].astype(jnp.float32)
        self.relay[number] = both.astype(jnp.bfloat16)
        self.send(
            self.relay.at[number], self.from_next.at[number], self.xy_send.at[place + 2],
            self.xy_recv.at[place + 2], {HEADS: following},
        )

    def reduce(self, number):
        wait_for(self.from_side.at[number, 1], self.xy_recv.at[3 * number + 1])
        wait_for(self.from_next.at[number], self.xy_recv.at[3 * number + 2])
        both = self.own[number, self.rows(self.head), :]
        both = both + self.from_side[number, 1].astype(jnp.float32)
        both = both + self.from_next[number].astype(jnp.float32)
        if number == self.places - 1:
            self.result = both
            return
        self.low[number] = both.astype(jnp.bfloat16)
        self.send(
            self.low.at[number], self.from_z.at[number], self.z_send.at[number],
            self.z_recv.at[number], {TENSOR: self.order[number]},
        )

    def share(self):
        result = self.result
        for number in range(self.places - 1):
            wait_for(self.from_z.at[number], self.z_recv.at[number])
            result = result + self.from_z[number].astype(jnp.float32)
        main = self.done.shape[1]
        self.done[...] = result[:, :main].astype(jnp.bfloat16)
        parts = [(self.done, self.out)]
        if self.exact:
            self.exact[0][...] = result[:, main:]
            parts.append((self.exact[0], self.exact_out))
        for which, (source, out) in enumerate(parts):
            here = out.at[self.head]
            home = pltpu.make_async_copy(source, here, self.home_sem.at[which])
            home.start()
            self.homes.append(home)
            for step, peer in enumerate(self.across):
                number = which * len(self.across) + step
                self.send(
                    source, here, self.back_send.at[number], self.back_recv.at[number],
                    {HEADS: peer},
                )

    def finish(self):
        outs = [self.out] + ([self.exact_out] if self.exact else [])
        for which, out in enumerate(outs):
            for step, peer in enumerate(self.across):
                number = which * len(self.across) + step
                wait_for(out.at[peer], self.back_recv.at[number])
        for home in self.homes:
            home.wait()
        for copy in self.started:
            copy.wait_send()


def combining_scratch(places, rows, quarter, widths, exact):
    wide = sum(widths)
    main = wide - (widths[-1] if exact else 0)
    f32, bf16 = jnp.float32, jnp.bfloat16
    dma = pltpu.SemaphoreType.DMA
    scratch = [
        pltpu.VMEM((places, rows, wide), bf16),
        pltpu.VMEM((places, rows, wide), f32),
        pltpu.VMEM((places, rows, wide), bf16),
        pltpu.VMEM((places, rows, wide), bf16),
        pltpu.VMEM((places, 2, quarter, wide), bf16),
        pltpu.VMEM((places, quarter, wide), bf16),
        pltpu.VMEM((places, quarter, wide), bf16),
        pltpu.VMEM((places - 1, quarter, wide), bf16),
        pltpu.VMEM((places - 1, quarter, wide), bf16),
        pltpu.VMEM((quarter, main), bf16),
    ]
    if exact:
        scratch.append(pltpu.VMEM((quarter, wide - main), f32))
    sems = [
        dma((2,)),
        dma((places,)),
        dma((places,)),
        dma((places * 3,)),
        dma((places * 3,)),
        dma((places - 1,)),
        dma((places - 1,)),
        dma((6,)),
        dma((6,)),
    ]
    return scratch, sems


def combine_kernel(
    columns, back, gates, ahead, back_out, gates_out, ahead_out, picks, *refs
):
    core = lax.axis_index(DP)
    places, rows, _ = columns.shape
    first = Combining((back, gates), back_out, gates_out, refs[:11], refs[21:30])
    second = Combining((ahead,), ahead_out, None, refs[11:21], refs[30:39])
    enter(
        [{TENSOR: peer} for peer in first.order[:-1]]
        + [{HEADS: peer} for peer in first.across]
        + [{DP: 1 - core}]
    )
    total = picks.shape[3]

    def pick(group, place):
        table = columns[place]
        lanes = lax.broadcasted_iota(jnp.int32, (rows, total), 1)
        hit = None
        for k in range(TOP):
            code = jnp.where(group == 0, table[:, k : k + 1], table[:, TOP + k : TOP + k + 1])
            here = code == lanes
            hit = here if hit is None else hit | here
        return jnp.where(hit, 1.0, 0.0).astype(jnp.bfloat16)

    last = places - 1
    for number, place in enumerate(first.order):
        picks[number, 1] = pick(1 - core, place)
        picks[number, 0] = pick(core, place)
        first.spread(number, picks[number])
        if number > 0:
            first.exchange(number - 1)
        if number > 1:
            first.pass_on(number - 2)
    first.exchange(last)
    for number in range(places):
        second.spread(number, picks[number])
        if number < 2:
            first.pass_on(last - 1 + number)
        else:
            first.reduce(number - 2)
        if number > 0:
            second.exchange(number - 1)
    second.exchange(last)
    for number in range(2, places):
        first.reduce(number)
    for number in range(places):
        second.pass_on(number)
    first.share()
    for number in range(places):
        second.reduce(number)
    second.share()
    first.finish()
    second.finish()


def run_combine(columns, back, gates, ahead, number):
    places, rows, _ = columns.shape
    experts, groups, slots, width = back.shape
    heads = lax.axis_size(HEADS)
    quarter = rows // heads
    extra = gates.shape[3]
    f32, bf16 = jnp.float32, jnp.bfloat16
    shape = jax.ShapeDtypeStruct
    vmem, anywhere = pl.BlockSpec(memory_space=pltpu.VMEM), pl.BlockSpec(memory_space=pl.ANY)
    first, first_sems = combining_scratch(places, rows, quarter, (width, extra), True)
    second, second_sems = combining_scratch(places, rows, quarter, (width,), False)
    return pl.pallas_call(
        combine_kernel,
        in_specs=[vmem] * 4,
        out_specs=[anywhere] * 3,
        out_shape=[
            shape((heads, quarter, width), bf16),
            shape((heads, quarter, extra), f32),
            shape((heads, quarter, width), bf16),
        ],
        scratch_shapes=[pltpu.VMEM((places, groups, rows, experts * slots), bf16)]
        + first
        + second
        + first_sems
        + second_sems,
        compiler_params=pltpu.CompilerParams(
            collective_id=number, has_side_effects=True, vmem_limit_bytes=VMEM_LIMIT
        ),
        name="combine",
    )(columns, back, gates, ahead)


def halves(values):
    lanes = lax.broadcasted_iota(jnp.int32, values.shape, 1)
    zero = jnp.zeros_like(values)
    return jnp.where(lanes < HEAD_DIM, values, zero), jnp.where(lanes < HEAD_DIM, zero, values)


def join_heads(first, second):
    lanes = lax.broadcasted_iota(jnp.int32, first.shape, 1)
    return jnp.where(lanes < HEAD_DIM, first, second)


def probabilities(query, keys):
    scores = dot_low(query, keys, ((1,), (1,))) * HEAD_DIM ** (-0.5)
    lanes = lax.broadcasted_iota(jnp.int32, scores.shape, 1)
    scores = jnp.where(lanes < SEQ, scores, -1e30)
    raised = jnp.exp(scores - jnp.max(scores, axis=1, keepdims=True))
    return raised / jnp.sum(raised, axis=1, keepdims=True)


def wide_rows(low_ref, first_row, rows):
    cores, places, _, _, tile = low_ref.shape
    shards = [low_ref[c, t, 0, first_row : first_row + rows, :] for c in range(cores) for t in range(places)]
    shards = [shard.astype(jnp.float32) for shard in shards]
    lanes = lax.broadcasted_iota(jnp.int32, (rows, tile), 1)
    tiles = []
    for left, right in zip(shards[::2], shards[1::2]):
        tiles.append(jnp.where(lanes < tile // 2, left, pltpu.roll(right, tile // 2, 1)))
    return jnp.concatenate(tiles, axis=1)


def front_kernel(
    slots, flat_ref, images_ref, cot_ref, ids_ref,
    qkv_out, mixed_out, first_out, normed_out, router_out, gains_out, weights_out, slot_in_out,
    slot_cot_out, member_out, column_out,
    low_ref, all_normed, all_cot, all_ids, ranks, picks, members, normed, mixed, *sems,
):
    images, padded, width = images_ref.shape
    cores, places, heads, _, tile = low_ref.shape
    f32, bf16 = jnp.float32, jnp.bfloat16
    core, head_index = lax.axis_index(DP), lax.axis_index(HEADS)
    block = width // cores
    quarter = cot_ref.shape[1]
    per = heads // images
    own_normed = normed_out.at[
        lax.div(head_index, per),
        pl.ds(pl.multiple_of(lax.rem(head_index, per) * quarter, 16), quarter),
    ]
    sharing_low = Sharing(flat_ref, low_ref, sems[:7])
    sharing_cot = Sharing(cot_ref.at[head_index], all_cot, sems[7:14])
    sharing_normed = Sharing(own_normed, all_normed, sems[14:21])
    ids_sems = sems[21]
    enter(
        [{TENSOR: peer} for peer in sharing_low.along]
        + [{HEADS: sharing_low.beside}, {HEADS: sharing_low.above}, {DP: 1 - core}]
    )
    sharing_low.start()
    ids_home = pltpu.make_async_copy(ids_ref, all_ids.at[core], ids_sems.at[0])
    ids_home.start()
    ids_copy = send(
        ids_ref, all_ids.at[core], ids_sems.at[1], ids_sems.at[2], {DP: 1 - core}
    )
    sharing_low.pass_to_sides()
    sharing_cot.start()
    ids_home.wait()
    wait_for(all_ids.at[1 - core], ids_sems.at[2])
    slot_places(slots, all_ids, ranks, column_out)
    sharing_low.pass_round()
    experts = slot_in_out.shape[0]
    groups = cores
    for group in range(groups):
        for e in range(experts):
            rank = ranks[e * groups + group : e * groups + group + 1, :]
            place = lax.broadcasted_iota(jnp.int32, (slots, rank.shape[1]), 0)
            picks[group, e * slots : (e + 1) * slots, :] = jnp.where(
                rank == place, 1.0, 0.0
            ).astype(bf16)
        lanes = lax.broadcasted_iota(jnp.int32, members.shape[1:], 1)
        start = (groups + group) * TOP
        hit = lanes == column_out[:, start : start + 1]
        for k in range(1, TOP):
            hit = hit | (lanes == column_out[:, start + k : start + k + 1])
        members[group] = jnp.where(hit, 1.0, 0.0).astype(bf16)
    for group in range(groups):
        part = dot_low(picks[group], members[group])
        for e in range(experts):
            member_out[e, group] = part[e * slots : (e + 1) * slots]
    sharing_low.own_group()
    sharing_low.other_group()
    sharing_cot.pass_to_sides()

    for matrix in range(4):
        for c in range(cores):
            for head in range(heads):
                start = matrix * width + head * tile
                weights_out[c * block : (c + 1) * block, start : start + tile] = low_ref[
                    c, matrix, head, :block, :
                ]
    small = wide_rows(low_ref, block, ceil_to(EXPERTS + 4, 16))
    router_out[...] = small[:EXPERTS].astype(bf16)
    gains = small[EXPERTS : EXPERTS + 8]
    gains_out[...] = gains
    for image in range(images):
        tokens = images_ref[image].astype(f32)
        here, _, _ = norm_forward(tokens, gains[0:1], gains[1:2])
        normed[image] = here.astype(bf16)
    for image in range(images):
        for matrix in range(3):
            part = dot_low(normed[image], weights_out[:, matrix * width : (matrix + 1) * width])
            part = part.astype(bf16)
            for head in range(heads):
                qkv_out[matrix, head, image] = part[:, head * tile : (head + 1) * tile]
        for head in range(heads):
            keys = qkv_out[1, head, image]
            total = None
            for query, value in zip(
                halves(qkv_out[0, head, image]), halves(qkv_out[2, head, image])
            ):
                probs = probabilities(query, keys).astype(bf16)
                part = dot_low(probs, value)
                total = part if total is None else total + part
            mixed_out[head, image] = total.astype(bf16)
            mixed[:, head * tile : (head + 1) * tile] = total.astype(bf16)
        attended = dot_low(mixed[...], weights_out[:, 3 * width :], ((1,), (1,)))
        first = images_ref[image].astype(f32) + attended
        first_out[image] = first
        here, _, _ = norm_forward(first, gains[2:3], gains[3:4])
        normed_out[image] = here.astype(bf16)

    def dispatch(source, out, group):
        rows = places * heads * quarter
        part = dot_low(picks[group], source[group].reshape(rows, width)).astype(bf16)
        for e in range(experts):
            out[e, group] = part[e * slots : (e + 1) * slots]

    sharing_normed.start()
    sharing_cot.pass_round()
    sharing_normed.pass_to_sides()
    sharing_cot.own_group()
    sharing_normed.pass_round()
    dispatch(all_cot, slot_cot_out, core)
    sharing_cot.other_group()
    dispatch(all_cot, slot_cot_out, 1 - core)
    sharing_normed.own_group()
    dispatch(all_normed, slot_in_out, core)
    sharing_normed.other_group()
    dispatch(all_normed, slot_in_out, 1 - core)
    ids_copy.wait_send()
    for sharing in (sharing_low, sharing_cot, sharing_normed):
        sharing.finish()


def run_front(flat, images, cot, ids, experts, slots, number):
    count, padded, width = images.shape
    groups, heads = lax.axis_size(DP), lax.axis_size(HEADS)
    places, _, rows = ids.shape
    tokens = places * rows
    quarter = cot.shape[1]
    f32, bf16 = jnp.float32, jnp.bfloat16
    shape = jax.ShapeDtypeStruct
    dma = pltpu.SemaphoreType.DMA
    vmem, anywhere = pl.BlockSpec(memory_space=pltpu.VMEM), pl.BlockSpec(memory_space=pl.ANY)
    return pl.pallas_call(
        functools.partial(front_kernel, slots),
        in_specs=[anywhere, vmem, anywhere, anywhere],
        out_specs=[vmem] * 11,
        out_shape=[
            shape((3, heads, count, padded, TILE), bf16),
            shape((heads, count, padded, TILE), bf16),
            shape((count, padded, width), f32),
            shape((count, padded, width), bf16),
            shape((EXPERTS, width), bf16),
            shape((8, width), f32),
            shape((width, 4 * width), bf16),
            shape((experts, groups, slots, width), bf16),
            shape((experts, groups, slots, width), bf16),
            shape((experts, groups, slots, EXPERTS), f32),
            shape((tokens, 2 * groups * TOP), jnp.int32),
        ],
        scratch_shapes=[
            pltpu.VMEM((groups, places, heads) + flat.shape, bf16),
            pltpu.VMEM((groups, places, heads, quarter, width), bf16),
            pltpu.VMEM((groups, places, heads, quarter, width), bf16),
            pltpu.VMEM((groups,) + ids.shape, jnp.int32),
            pltpu.VMEM((experts * groups, tokens), jnp.int32),
            pltpu.VMEM((groups, experts * slots, tokens), bf16),
            pltpu.VMEM((groups, tokens, EXPERTS), bf16),
            pltpu.VMEM((count, padded, width), bf16),
            pltpu.VMEM((padded, width), bf16),
        ]
        + sharing_sems(places, heads) * 3
        + [dma((3,))],
        compiler_params=pltpu.CompilerParams(
            collective_id=number, has_side_effects=True, vmem_limit_bytes=VMEM_LIMIT
        ),
        name="front",
    )(flat, images, cot, ids)


def attend_back_kernel(
    back_ref, gate_ref, cot_ref, columns_ref, images_ref, first_ref, normed_b_ref, mixed_ref,
    qkv_ref, router_ref, gains_ref, weights_ref, input_out, grads_out,
    normed_a, branch, mixed_grad, qkv_grad, own_grad,
):
    images, padded, width = images_ref.shape
    heads, tile = mixed_ref.shape[0], mixed_ref.shape[3]
    cores = grads_out.shape[0]
    f32, bf16 = jnp.float32, jnp.bfloat16
    core = lax.axis_index(DP)
    head_index = lax.axis_index(HEADS)
    tensor = lax.axis_index(TENSOR)
    block = width // cores
    gains = gains_ref[...]
    router = router_ref[...]
    router_grad = jnp.zeros((EXPERTS, width), f32)
    sums = [jnp.zeros((1, width), f32) for _ in range(4)]
    for image in range(images):
        columns = columns_ref[tensor, image]
        ids = [
            jnp.where(core == 0, columns[:, 4 + k : 5 + k], columns[:, 6 + k : 7 + k])
            for k in range(TOP)
        ]
        lanes = lax.broadcasted_iota(jnp.int32, (padded, EXPERTS), 1)
        chosen = jnp.where((lanes == ids[0]) | (lanes == ids[1]), 1.0, 0.0)
        normed_b = normed_b_ref[image]
        logits = dot_low(normed_b, router, ((1,), (1,)))
        peak = jnp.max(jnp.where(chosen > 0, logits, -1e30), axis=1, keepdims=True)
        raised = jnp.exp(jnp.where(chosen > 0, logits - peak, -1e30))
        any_chosen = jnp.max(chosen, axis=1, keepdims=True)
        gates = raised / (jnp.sum(raised, axis=1, keepdims=True) + (1.0 - any_chosen))
        parts = gate_ref[image]
        gate_grad = (parts + pltpu.roll(parts, tile - EXPERTS, 1))[:, :EXPERTS]
        blend = jnp.sum(gates * gate_grad, axis=1, keepdims=True)
        logit_grad = (gates * (gate_grad - blend)).astype(bf16)
        normed_grad = back_ref[image].astype(f32) + dot_low(logit_grad, router)
        router_grad = router_grad + dot_low(logit_grad, normed_b, ((0,), (0,)))
        _, scaled, inverse = norm_forward(first_ref[image], gains[2:3], gains[3:4])
        sums[2] = sums[2] + jnp.sum(normed_grad * scaled, axis=0, keepdims=True)
        sums[3] = sums[3] + jnp.sum(normed_grad, axis=0, keepdims=True)
        first_grad = cot_ref[image].astype(f32) + norm_backward(
            normed_grad, scaled, inverse, gains[2:3]
        )
        input_out[image] = first_grad
        branch[image] = first_grad.astype(bf16)
        mixed_grad[...] = dot_low(branch[image], weights_ref[:, 3 * width :]).astype(bf16)
        for head in range(heads):
            query, keys = qkv_ref[0, head, image], qkv_ref[1, head, image]
            values = qkv_ref[2, head, image]
            out_grad = mixed_grad[:, head * tile : (head + 1) * tile]
            query_grads, key_grads, value_grad = [], [], None
            for query_half, grad_half in zip(halves(query), halves(out_grad)):
                probs = probabilities(query_half, keys)
                prob_grad = dot_low(grad_half, values, ((1,), (1,)))
                part = dot_low(probs.astype(bf16), grad_half, ((0,), (0,)))
                value_grad = part if value_grad is None else value_grad + part
                score_grad = (
                    probs * (prob_grad - jnp.sum(probs * prob_grad, axis=1, keepdims=True))
                ).astype(bf16)
                query_grads.append(dot_low(score_grad, keys))
                key_grads.append(dot_low(score_grad, query, ((0,), (0,))))
            scale = HEAD_DIM ** (-0.5)
            for matrix, grad in enumerate(
                (join_heads(*query_grads) * scale, join_heads(*key_grads) * scale, value_grad)
            ):
                grad = grad.astype(bf16)
                start = matrix * width + head * tile
                qkv_grad[:, start : start + tile] = grad
                own_grad[matrix, head, image * padded : (image + 1) * padded, :] = grad
        normed_grad = dot_low(qkv_grad[...], weights_ref[:, : 3 * width], ((1,), (1,)))
        here, scaled, inverse = norm_forward(
            images_ref[image].astype(f32), gains[0:1], gains[1:2]
        )
        normed_a[image] = here.astype(bf16)
        sums[0] = sums[0] + jnp.sum(normed_grad * scaled, axis=0, keepdims=True)
        sums[1] = sums[1] + jnp.sum(normed_grad, axis=0, keepdims=True)
        input_out[image] = input_out[image] + norm_backward(
            normed_grad, scaled, inverse, gains[0:1]
        )
    rows = images * padded
    left = normed_a[...].reshape(rows, width)
    for matrix in range(4):
        if matrix < 3:
            grad = dot_low(left, own_grad[matrix, head_index], ((0,), (0,)))
        else:
            own_mixed = mixed_ref[head_index].reshape(rows, tile)
            grad = dot_low(branch[...].reshape(rows, width), own_mixed, ((0,), (0,)))
        for c in range(cores):
            grads_out[c, matrix, :block, :] = grad[c * block : (c + 1) * block]
    pad = grads_out.shape[2] - block - EXPERTS - 4
    small = jnp.concatenate([router_grad] + sums + [jnp.zeros((pad, width), f32)], axis=0)
    places = grads_out.shape[1]
    for c in range(cores):
        for t in range(places):
            shard = c * places + t
            piece = small[:, shard // 2 * tile : (shard // 2 + 1) * tile]
            if shard % 2:
                piece = pltpu.roll(piece, tile // 2, 1)
            grads_out[c, t, block:, :] = piece


def run_attend_back(
    back, gates, cot, columns, images, first, normed_b, mixed, qkv, router, gains, weights, shards
):
    count, padded, width = images.shape
    heads, tile = mixed.shape[0], mixed.shape[3]
    f32, bf16 = jnp.float32, jnp.bfloat16
    shape = jax.ShapeDtypeStruct
    return pl.pallas_call(
        attend_back_kernel,
        in_specs=[pl.BlockSpec(memory_space=pltpu.VMEM)] * 12,
        out_specs=[pl.BlockSpec(memory_space=pltpu.VMEM)] * 2,
        out_shape=[shape((count, padded, width), f32), shape(shards, f32)],
        scratch_shapes=[
            pltpu.VMEM((count, padded, width), bf16),
            pltpu.VMEM((count, padded, width), bf16),
            pltpu.VMEM((padded, width), bf16),
            pltpu.VMEM((padded, 3 * width), bf16),
            pltpu.VMEM((3, heads, count * padded, tile), bf16),
        ],
        compiler_params=pltpu.CompilerParams(vmem_limit_bytes=VMEM_LIMIT),
        name="attend_back",
    )(back, gates, cot, columns, images, first, normed_b, mixed, qkv, router, gains, weights)


def attn_polish_kernel(whole_ref, weights_ref, out_ref, values, gram, poly):
    cores, heads, block, tile = whole_ref.shape
    width = values.shape[0]
    half = width // 2
    core, head_index = lax.axis_index(DP), lax.axis_index(HEADS)
    squares = jnp.zeros((1, 1), jnp.float32)
    for c in range(cores):
        for h in range(heads):
            part = whole_ref[c, h]
            squares = squares + jnp.sum(part * part, keepdims=True)
    factor = 1.0 / (jnp.sqrt(squares) + 1e-07)
    for c in range(cores):
        for h in range(heads):
            values[c * block : (c + 1) * block, h * tile : (h + 1) * tile] = whole_ref[c, h] * factor

    def store(ref, upper, corner):
        ref[:half, :] = upper
        ref[half:, half:] = corner
        ref[half:, :half] = upper[:, half:].T

    def product(left, right, contract):
        return lax.dot_general(
            left, right, (contract, ((), ())),
            precision=lax.Precision.HIGH, preferred_element_type=jnp.float32,
        )

    for step in range(ITERS):
        across = ((1,), (1,))
        store(
            gram,
            product(values[:half, :], values[...], across),
            product(values[half:, :], values[half:, :], across),
        )
        along = ((1,), (0,))
        upper = product(gram[:half, :], gram[...], along)
        corner = product(gram[half:, :], gram[:, half:], along)
        store(
            poly,
            coef_second * gram[:half, :] + coef_third * upper,
            coef_second * gram[half:, half:] + coef_third * corner,
        )
        values[...] = coef_first * values[...] + product(poly[...], values[...], along)
    scale = muon_scale(width, heads * tile)
    for c in range(cores):
        for h in range(heads):

            @pl.when((core == c) & (head_index == h))
            def _():
                own = values[c * block : (c + 1) * block, h * tile : (h + 1) * tile]
                out_ref[...] = weights_ref[...] * (1.0 - muon_rate * muon_decay) - scale * own


def run_attn_polish(whole, weights):
    width = whole.shape[0] * whole.shape[2]
    return pl.pallas_call(
        attn_polish_kernel,
        in_specs=[pl.BlockSpec(memory_space=pltpu.VMEM)] * 2,
        out_specs=pl.BlockSpec(memory_space=pltpu.VMEM),
        out_shape=jax.ShapeDtypeStruct(weights.shape, jnp.float32),
        scratch_shapes=[pltpu.VMEM((width, width), jnp.float32)] * 3,
        compiler_params=pltpu.CompilerParams(vmem_limit_bytes=VMEM_LIMIT),
        name="attn_polish",
    )(whole, weights)


def slot_places(slots, ids_ref, rank_out, column_out):
    groups, places, _, rows = ids_ref.shape
    experts = rank_out.shape[0] // groups
    labels = [own_label(experts, e).astype(jnp.float32) for e in range(experts)]
    wide = ceil_to(rows, TILE)
    earlier = lax.broadcasted_iota(jnp.int32, (rows, rows), 0)
    later = lax.broadcasted_iota(jnp.int32, (rows, rows), 1)
    before = jnp.where(earlier < later, 1.0, 0.0).astype(jnp.bfloat16)
    running = jnp.zeros((groups * experts, 1), jnp.float32)
    ranks = []
    for place in range(places):
        ids = [
            ids_ref[g, place, k : k + 1, :].astype(jnp.float32)
            for g in range(groups)
            for k in range(TOP)
        ]
        marks = []
        for e in range(experts):
            for g in range(groups):
                hit = ids[TOP * g] == labels[e]
                for k in range(1, TOP):
                    hit = hit | (ids[TOP * g + k] == labels[e])
                marks.append(jnp.where(hit, 1.0, 0.0))
        marks = jnp.concatenate(marks, axis=0)
        rank = running + dot_low(marks.astype(jnp.bfloat16), before)
        running = running + jnp.sum(marks, axis=1, keepdims=True)
        rank = jnp.where(marks > 0, rank, -1.0)
        ranks.append(rank)
        codes = []
        for g in range(groups):
            for k in range(TOP):
                code = jnp.full((1, rows), -1.0, jnp.float32)
                for e in range(experts):
                    own = ids[TOP * g + k] == labels[e]
                    number = e * groups + g
                    code = jnp.where(own, rank[number : number + 1] + float(slots * e), code)
                codes.append(code)
        both = jnp.concatenate(codes + ids, axis=0)
        columns = both.shape[0]
        both = jnp.concatenate(
            [both, jnp.zeros((columns, wide - rows), jnp.float32)], axis=1
        )
        both = jnp.concatenate([both, jnp.zeros((TILE - columns, wide), jnp.float32)], axis=0)
        for start in range(0, rows, TILE):
            turned = both[:, start : start + TILE].T
            count = min(TILE, rows - start)
            column_out[place * rows + start : place * rows + start + count, :] = turned[
                :count, :columns
            ].astype(jnp.int32)
    rank_out[...] = jnp.concatenate(ranks, axis=1).astype(jnp.int32)


def shards_fast(
    images_in,
    attn_weights,
    attn_momentum,
    router_weight,
    router_first,
    router_second,
    expert_weights,
    expert_momentum,
    norm_params,
    norm_first,
    norm_second,
    expert_ids,
    cotangent,
):
    rows, width = images_in.shape
    dp_count = lax.axis_size(DP)
    head_count = lax.axis_size(HEADS)
    tensor_count = lax.axis_size(TENSOR)
    mats = expert_weights.shape[0]
    hidden_cols = expert_weights.shape[2]
    group_rows = expert_ids.shape[0]
    slots = ceil_to(3 * TOP * group_rows // (2 * EXPERTS), 16)
    images = rows // SEQ
    image_rows = ceil_to(SEQ, 16 * head_count // math.gcd(images, head_count))
    padded_rows = images * image_rows
    quarter = padded_rows // head_count
    bf16, f32 = jnp.bfloat16, jnp.float32

    def pad_images(values):
        values = values.reshape(-1, SEQ, values.shape[-1])
        return jnp.pad(values, ((0, 0), (0, image_rows - SEQ), (0, 0)))

    def drop_padding(values):
        return values.reshape(images, image_rows, -1)[:, :SEQ].reshape(rows, -1)

    attn_rows = attn_weights.size // TILE
    small = jnp.concatenate((router_weight.T, norm_params), axis=0).astype(bf16)
    small_rows, small_lanes = small.shape
    small = jnp.pad(
        small, ((0, ceil_to(small_rows, 16) - small_rows), (0, TILE - small_lanes))
    )
    flat = jnp.concatenate((attn_weights.astype(bf16).reshape(attn_rows, TILE), small), axis=0)
    padded_cot = pad_images(cotangent)
    padded_images = pad_images(images_in)
    own_ids = jnp.pad(
        expert_ids.reshape(-1, SEQ, TOP), ((0, 0), (0, image_rows - SEQ), (0, 0)), constant_values=-1
    )
    own_ids = jnp.transpose(own_ids.reshape(tensor_count, padded_rows, TOP), (0, 2, 1))
    experts_own = mats // 2

    (
        qkv, mixed, first, normed_b, router_low, gains, weights_low, slot_in, slot_cot, member, columns,
    ) = run_front(
        flat, padded_images, padded_cot.reshape(head_count, quarter, width), own_ids,
        experts_own, slots, 1,
    )

    step = tensor_count // 2
    earlier = ()
    directions, packed = [], []
    for start in range(0, experts_own, step):
        *earlier, direction, gram = run_experts(
            start, step, slot_in, slot_cot, member, router_low, expert_weights, expert_momentum,
            tuple(earlier),
        )
        directions.append(direction)
        packed.append(lax.psum_scatter(gram, TENSOR, scatter_dimension=0, tiled=True))
    expert_mom, back, gate_back, ahead = earlier
    places = columns.reshape(tensor_count, padded_rows, -1)

    def by_group(values):
        return values.reshape(experts_own, dp_count, slots, values.shape[-1])

    back_total, gate_total, ahead_total = run_combine(
        places, by_group(back), by_group(gate_back), by_group(ahead), 3
    )
    packed[0], back_total = lax.optimization_barrier((packed[0], back_total))
    polished = run_polish(packed[0], width)
    back_total, polished = lax.optimization_barrier((back_total, polished))
    products = [lax.all_gather(polished, TENSOR, axis=0, tiled=True)]
    block_out = drop_padding(
        first + ahead_total.reshape(images, image_rows, width).astype(f32)
    )

    input_grad, grads = run_attend_back(
        back_total.reshape(images, image_rows, width),
        gate_total.reshape(images, image_rows, TILE),
        padded_cot, columns.reshape(tensor_count, images, image_rows, -1),
        padded_images, first, normed_b, mixed, qkv, router_low, gains, weights_low,
        (dp_count, tensor_count) + flat.shape,
    )
    packed[1:], grads = lax.optimization_barrier((packed[1:], grads))
    for gram in packed[1:]:
        polished = run_polish(gram, width)
        grads, polished = lax.optimization_barrier((grads, polished))
        products.append(lax.all_gather(polished, TENSOR, axis=0, tiled=True))
    input_grad = drop_padding(input_grad)
    sums, whole = attn_exchange(grads, attn_momentum.reshape(attn_rows, TILE), 5)
    attn_sum = sums[:attn_rows].reshape(attn_weights.shape)
    router_sum = sums[attn_rows : attn_rows + EXPERTS, :small_lanes].T
    norm_sum = sums[attn_rows + EXPERTS : attn_rows + small_rows, :small_lanes]
    attn_mom = momentum_decay * attn_momentum + attn_sum
    attn_new = run_attn_polish(whole, attn_weights.reshape(attn_rows, TILE))
    attn_new = attn_new.reshape(attn_weights.shape)

    expert_new = ()
    scale = muon_scale(width, hidden_cols * tensor_count)
    for place, (direction, product) in enumerate(zip(directions, products)):
        expert_new = (
            run_apply(place * tensor_count, scale, product, direction, expert_weights, expert_new),
        )
    expert_new = expert_new[0]

    router_first_new, router_second_new, router_new = adamw_update(
        router_weight, router_first, router_second, router_sum, router_rate, router_decay
    )
    norm_first_new, norm_second_new, norm_new = adamw_update(
        norm_params, norm_first, norm_second, norm_sum, gains_rate, 0.0
    )
    return (
        block_out,
        input_grad,
        attn_mom,
        attn_new,
        router_first_new,
        router_second_new,
        router_new,
        expert_mom,
        expert_new,
        norm_first_new,
        norm_second_new,
        norm_new,
    )


def solution(mesh):
    in_specs = (
        P((DP, TENSOR), None),
        P(TENSOR, DP, HEADS),
        P(TENSOR, DP, HEADS),
        P((DP, TENSOR), None),
        P((DP, TENSOR), None),
        P((DP, TENSOR), None),
        P((HEADS, DP), None, TENSOR),
        P((HEADS, DP), None, TENSOR),
        P(None, (DP, TENSOR)),
        P(None, (DP, TENSOR)),
        P(None, (DP, TENSOR)),
        P(DP, None),
        P((DP, TENSOR), None),
    )
    out_specs = (
        P((DP, TENSOR), None),
        P((DP, TENSOR), None),
        P(TENSOR, DP, HEADS),
        P(TENSOR, DP, HEADS),
        P((DP, TENSOR), None),
        P((DP, TENSOR), None),
        P((DP, TENSOR), None),
        P((HEADS, DP), None, TENSOR),
        P((HEADS, DP), None, TENSOR),
        P(None, (DP, TENSOR)),
        P(None, (DP, TENSOR)),
        P(None, (DP, TENSOR)),
    )
    shape = dict(mesh.shape)
    step = EXPERTS * 2 // (shape[HEADS] * shape[DP])
    fits = shape[DP] == 2 and shape[HEADS] == 4 and step % (2 * shape[TENSOR]) == 0
    fits = fits and shape[TENSOR] % 2 == 0
    shards = shards_fast if fits else shards_general
    return jax.shard_map(shards, mesh=mesh, in_specs=in_specs, out_specs=out_specs, check_vma=False)
```

```python
import functools
import math

import jax
import jax.numpy as jnp
from jax import lax
from jax.experimental import pallas as pl
from jax.experimental.pallas import tpu as pltpu
from jax.sharding import PartitionSpec as P

EXPERTS = 32
SEQ = 197
TOP = 2
ITERS = 5
STEP = 5
HEAD_DIM = 64


norm_epsilon = 1e-06
coef_first = 3.4445
coef_second = -4.775
coef_third = 2.0315
momentum_decay = 0.95
muon_rate = 0.2
muon_decay = 0.1
adam_first = 0.9
adam_second = 0.999
adam_epsilon = 1e-08
router_rate = 0.03
router_decay = 0.01
gains_rate = 0.1
TILE = 128
DP, HEADS, TENSOR = "dp", "heads", "tensor"
TO_ALL, OWN_HEAD, TO_CORE = range(3)
VMEM_LIMIT = 56 * 1024 * 1024
VMEM_LARGE = 62 * 1024 * 1024


def norm_forward(values, gain, shift):
    center = jnp.mean(values, axis=-1, keepdims=True)
    centred = values - center
    inverse = lax.rsqrt(jnp.mean(centred * centred, axis=-1, keepdims=True) + norm_epsilon)
    scaled = centred * inverse
    return (scaled * gain + shift, scaled, inverse)


def norm_backward(grad_normed, scaled, inverse, gain):
    grad_scaled = grad_normed * gain
    inner = grad_scaled - jnp.mean(grad_scaled, axis=-1, keepdims=True)
    inner = inner - scaled * jnp.mean(grad_scaled * scaled, axis=-1, keepdims=True)
    return inner * inverse


def exact_gelu(values):
    return jax.nn.gelu(values, approximate=False)


def batch_gram(values):
    return jnp.einsum("mij,mkj->mik", values, values, precision=lax.Precision.HIGHEST)


def batch_product(left, right):
    return jnp.einsum("mij,mjk->mik", left, right, precision=lax.Precision.HIGHEST)


def polish_step(values, gram):
    poly = coef_second * gram + coef_third * batch_product(gram, gram)
    return coef_first * values + batch_product(poly, values)


def muon_scale(rows, cols):
    return muon_rate * 0.2 * math.sqrt(max(rows, cols))


def adamw_update(values, first, second, grad, rate, decay):
    first_new = adam_first * first + (1.0 - adam_first) * grad
    second_new = adam_second * second + (1.0 - adam_second) * grad * grad
    first_hat = first_new / (1.0 - adam_first**STEP)
    second_hat = second_new / (1.0 - adam_second**STEP)
    values_new = values * (1.0 - rate * decay) - rate * first_hat / (
        jnp.sqrt(second_hat) + adam_epsilon
    )
    return (first_new, second_new, values_new)


def shards_general(
    images_in,
    attn_weights,
    attn_momentum,
    router_weight,
    router_first,
    router_second,
    expert_weights,
    expert_momentum,
    norm_params,
    norm_first,
    norm_second,
    expert_ids,
    cotangent,
):
    local_rows, width = images_in.shape
    dp_count = lax.axis_size(DP)
    head_count = lax.axis_size(HEADS)
    tensor_count = lax.axis_size(TENSOR)
    mats_here = attn_weights.shape[0]
    row_shard = attn_weights.shape[1]
    head_cols = attn_weights.shape[2]
    hidden_cols = expert_weights.shape[2]
    group_rows = expert_ids.shape[0]
    capacity = 3 * TOP * group_rows // (2 * EXPERTS)
    experts_here = EXPERTS // head_count
    heads_here = head_cols // HEAD_DIM
    images = local_rows // SEQ
    score_scale = HEAD_DIM ** (-0.5)
    head_index = lax.axis_index(HEADS)
    tensor_index = lax.axis_index(TENSOR)
    dp_index = lax.axis_index(DP)
    attn_low, router_low, norms_low = (
        lax.all_gather(attn_weights.astype(jnp.bfloat16), (DP, TENSOR), axis=0, tiled=True),
        lax.all_gather(router_weight.astype(jnp.bfloat16), (DP, TENSOR), axis=0, tiled=True),
        lax.all_gather(norm_params.astype(jnp.bfloat16), (DP, TENSOR), axis=1, tiled=True),
    )
    attn_low = attn_low.reshape(dp_count, tensor_count * mats_here, row_shard, head_cols)
    attn_low = jnp.transpose(attn_low, (1, 0, 2, 3)).reshape(
        tensor_count * mats_here, width, head_cols
    )
    gains = norms_low.astype(jnp.float32)
    qkv_weight = jnp.transpose(attn_low[:3], (1, 0, 2)).reshape(width, 3 * head_cols)
    out_weight = attn_low[3]
    tokens = images_in.astype(jnp.float32)
    normed_a, scaled_a, inverse_a = norm_forward(tokens, gains[0], gains[1])
    normed_a = normed_a.astype(jnp.bfloat16)
    qkv = jnp.dot(normed_a, qkv_weight, preferred_element_type=jnp.float32).astype(jnp.bfloat16)
    split = qkv.reshape(images, SEQ, 3, heads_here, HEAD_DIM)
    query = split[:, :, 0]
    keys = split[:, :, 1]
    values = split[:, :, 2]
    scores = (
        jnp.einsum("ishd,ithd->ihst", query, keys, preferred_element_type=jnp.float32) * score_scale
    )
    peak = jnp.max(scores, axis=-1, keepdims=True)
    logsum = peak + jnp.log(jnp.sum(jnp.exp(scores - peak), axis=-1, keepdims=True))
    probs_low = jnp.exp(scores - logsum).astype(jnp.bfloat16)
    mixed = jnp.einsum("ihst,ithd->ishd", probs_low, values, preferred_element_type=jnp.float32)
    mixed = mixed.reshape(local_rows, head_cols).astype(jnp.bfloat16)
    partial_out = jnp.einsum("tc,dc->td", mixed, out_weight, preferred_element_type=jnp.float32)
    attended = lax.psum(partial_out, HEADS)
    first = tokens + attended
    normed_b, scaled_b, inverse_b = norm_forward(first, gains[2], gains[3])
    normed_b = normed_b.astype(jnp.bfloat16)
    group_in, group_cot = (
        lax.all_gather(normed_b, TENSOR, axis=0, tiled=True),
        lax.all_gather(cotangent, TENSOR, axis=0, tiled=True),
    )
    logits = jnp.dot(group_in, router_low, preferred_element_type=jnp.float32)
    chosen = jnp.take_along_axis(logits, expert_ids, axis=1)
    raised = jnp.exp(chosen - jnp.max(chosen, axis=1, keepdims=True))
    gates = raised / jnp.sum(raised, axis=1, keepdims=True)
    routes = expert_ids.reshape(-1)
    route_count = routes.shape[0]
    order = jnp.argsort(routes * route_count + jnp.arange(route_count, dtype=jnp.int32))
    labels = head_index * experts_here + jnp.arange(experts_here, dtype=jnp.int32)
    counts = jnp.sum((routes[None, :] == labels[:, None]).astype(jnp.int32), axis=1)
    starts = jnp.sum((routes[None, :] < labels[:, None]).astype(jnp.int32), axis=1)
    slot_index = jnp.arange(capacity, dtype=jnp.int32)
    picked = order[jnp.minimum(starts[:, None] + slot_index[None, :], route_count - 1)]
    filled = (slot_index[None, :] < counts[:, None]).astype(jnp.float32)
    token_rows = (picked // TOP).reshape(-1)
    pick_cols = (picked % TOP).reshape(-1)
    slot_gate = gates[token_rows, pick_cols].reshape(experts_here, capacity) * filled
    slot_in = group_in[token_rows].reshape(experts_here, capacity, width)
    pair = lax.all_gather(expert_weights.astype(jnp.bfloat16), DP, axis=0, tiled=True).reshape(
        experts_here, 2, width, hidden_cols
    )
    hidden = jnp.einsum("ecd,edf->ecf", slot_in, pair[:, 0], preferred_element_type=jnp.float32)
    active, gelu_pull = jax.vjp(exact_gelu, hidden)
    active = active.astype(jnp.bfloat16)
    expert_out = jnp.einsum("ecf,edf->ecd", active, pair[:, 1], preferred_element_type=jnp.float32)
    weighted = (expert_out * slot_gate[:, :, None]).reshape(-1, width)
    spread = jnp.zeros((group_rows, width), jnp.float32).at[token_rows].add(weighted)
    own_sum = lax.psum_scatter(spread, TENSOR, scatter_dimension=0, tiled=True)
    moe_out = lax.psum(own_sum, HEADS)
    block_out = first + moe_out
    grad_out = cotangent.astype(jnp.float32)
    slot_cot = group_cot[token_rows].reshape(experts_here, capacity, width).astype(jnp.float32)
    gate_grad = jnp.sum(slot_cot * expert_out, axis=-1) * filled
    out_grad = (slot_cot * slot_gate[:, :, None]).astype(jnp.bfloat16)
    pair_back = lax.all_gather(
        expert_weights.astype(jnp.bfloat16), DP, axis=0, tiled=True
    ).reshape(experts_here, 2, width, hidden_cols)
    active_grad = jnp.einsum(
        "ecd,edf->ecf", out_grad, pair_back[:, 1], preferred_element_type=jnp.float32
    )
    hidden_grad = gelu_pull(active_grad)[0].astype(jnp.bfloat16)
    down_grad = jnp.einsum("ecd,ecf->edf", out_grad, active, preferred_element_type=jnp.float32)
    up_grad = jnp.einsum("ecd,ecf->edf", slot_in, hidden_grad, preferred_element_type=jnp.float32)
    slot_in_grad = jnp.einsum(
        "ecf,edf->ecd", hidden_grad, pair_back[:, 0], preferred_element_type=jnp.float32
    ).reshape(-1, width)
    back_spread = jnp.zeros((group_rows, width), jnp.float32).at[token_rows].add(slot_in_grad)
    gate_spread = (
        jnp.zeros((group_rows, TOP), jnp.float32)
        .at[token_rows, pick_cols]
        .add(gate_grad.reshape(-1))
    )
    own_back, own_gate = (
        lax.psum_scatter(back_spread, TENSOR, scatter_dimension=0, tiled=True),
        lax.psum_scatter(gate_spread, TENSOR, scatter_dimension=0, tiled=True),
    )
    normed_b_grad, gate_total = lax.psum((own_back, own_gate), HEADS)
    matrix_grads = jnp.stack((up_grad, down_grad), axis=1).reshape(
        2 * experts_here, width, hidden_cols
    )
    expert_grad = lax.psum_scatter(matrix_grads, DP, scatter_dimension=0, tiled=True)
    own_ids = lax.dynamic_slice_in_dim(expert_ids, tensor_index * local_rows, local_rows, 0)
    own_gates = lax.dynamic_slice_in_dim(gates, tensor_index * local_rows, local_rows, 0)
    blend = jnp.sum(own_gates * gate_total, axis=1, keepdims=True)
    chosen_grad = own_gates * (gate_total - blend)
    expert_labels = jnp.arange(EXPERTS, dtype=jnp.int32)
    matches = (own_ids[:, :, None] == expert_labels[None, None, :]).astype(jnp.float32)
    logit_grad = jnp.sum(matches * chosen_grad[:, :, None], axis=1).astype(jnp.bfloat16)
    normed_b_grad = normed_b_grad + jnp.einsum(
        "te,de->td", logit_grad, router_low, preferred_element_type=jnp.float32
    )
    router_grad = jnp.einsum("td,te->de", normed_b, logit_grad, preferred_element_type=jnp.float32)
    gain_b_grad = jnp.sum(normed_b_grad * scaled_b, axis=0)
    shift_b_grad = jnp.sum(normed_b_grad, axis=0)
    first_grad = grad_out + norm_backward(normed_b_grad, scaled_b, inverse_b, gains[2])
    branch_grad = first_grad.astype(jnp.bfloat16)
    out_weight_grad = jnp.einsum(
        "td,tc->dc", branch_grad, mixed, preferred_element_type=jnp.float32
    )
    mixed_grad = jnp.einsum(
        "td,dc->tc", branch_grad, out_weight, preferred_element_type=jnp.float32
    ).astype(jnp.bfloat16)
    mixed_grad = mixed_grad.reshape(images, SEQ, heads_here, HEAD_DIM)
    scores_again = (
        jnp.einsum("ishd,ithd->ihst", query, keys, preferred_element_type=jnp.float32) * score_scale
    )
    probs_again = jnp.exp(scores_again - logsum)
    prob_grad = jnp.einsum(
        "ishd,ithd->ihst", mixed_grad, values, preferred_element_type=jnp.float32
    )
    value_grad = jnp.einsum(
        "ihst,ishd->ithd",
        probs_again.astype(jnp.bfloat16),
        mixed_grad,
        preferred_element_type=jnp.float32,
    )
    score_grad = (
        probs_again * (prob_grad - jnp.sum(probs_again * prob_grad, axis=-1, keepdims=True))
    ).astype(jnp.bfloat16)
    query_grad = (
        jnp.einsum("ihst,ithd->ishd", score_grad, keys, preferred_element_type=jnp.float32)
        * score_scale
    )
    key_grad = (
        jnp.einsum("ihst,ishd->ithd", score_grad, query, preferred_element_type=jnp.float32)
        * score_scale
    )
    qkv_grad = (
        jnp.stack((query_grad, key_grad, value_grad), axis=2)
        .reshape(local_rows, 3 * head_cols)
        .astype(jnp.bfloat16)
    )
    normed_a_part = jnp.einsum(
        "tc,dc->td", qkv_grad, qkv_weight, preferred_element_type=jnp.float32
    )
    qkv_weight_grad = jnp.einsum(
        "td,tc->dc", normed_a, qkv_grad, preferred_element_type=jnp.float32
    )
    normed_a_grad = lax.psum(normed_a_part, HEADS)
    gain_a_grad = jnp.sum(normed_a_grad * scaled_a, axis=0)
    shift_a_grad = jnp.sum(normed_a_grad, axis=0)
    input_grad = first_grad + norm_backward(normed_a_grad, scaled_a, inverse_a, gains[0])
    attn_grad = jnp.concatenate(
        (
            jnp.transpose(qkv_weight_grad.reshape(width, 3, head_cols), (1, 0, 2)),
            out_weight_grad[None],
        ),
        axis=0,
    )
    arranged = attn_grad.reshape(tensor_count, mats_here, dp_count, row_shard, head_cols)
    arranged = jnp.transpose(arranged, (2, 0, 1, 3, 4)).reshape(
        dp_count * tensor_count * mats_here, row_shard, head_cols
    )
    norm_grad = jnp.stack((gain_a_grad, shift_a_grad, gain_b_grad, shift_b_grad))
    attn_sum, router_sum, norm_sum = (
        lax.psum_scatter(arranged, (DP, TENSOR), scatter_dimension=0, tiled=True),
        lax.psum_scatter(router_grad, (DP, TENSOR), scatter_dimension=0, tiled=True),
        lax.psum_scatter(norm_grad, (DP, TENSOR), scatter_dimension=1, tiled=True),
    )
    attn_mom = momentum_decay * attn_momentum + attn_sum
    attn_dir = attn_sum + momentum_decay * attn_mom
    whole = lax.all_gather(attn_dir, (DP, HEADS), axis=1, tiled=True)
    whole = whole.reshape(mats_here, dp_count, head_count, row_shard, head_cols)
    whole = jnp.transpose(whole, (0, 1, 3, 2, 4)).reshape(mats_here, width, head_count * head_cols)
    whole = whole / (jnp.sqrt(jnp.sum(whole * whole, axis=(1, 2), keepdims=True)) + 1e-07)
    for iteration in range(ITERS):
        whole = polish_step(whole, batch_gram(whole))
    own_part = lax.dynamic_slice(
        whole, (0, dp_index * row_shard, head_index * head_cols), (mats_here, row_shard, head_cols)
    )
    attn_new = (
        attn_weights * (1.0 - muon_rate * muon_decay)
        - muon_scale(width, head_count * head_cols) * own_part
    )
    expert_mom = momentum_decay * expert_momentum + expert_grad
    current = expert_grad + momentum_decay * expert_mom
    for iteration in range(ITERS):
        gram = lax.psum(batch_gram(current), TENSOR)
        if iteration == 0:
            factor = 1.0 / (jnp.sqrt(jnp.trace(gram, axis1=1, axis2=2)) + 1e-07)
            factor = factor[:, None, None]
            current = current * factor
            gram = gram * (factor * factor)
        current = polish_step(current, gram)
    expert_new = (
        expert_weights * (1.0 - muon_rate * muon_decay)
        - muon_scale(width, hidden_cols * tensor_count) * current
    )
    router_first_new, router_second_new, router_new = adamw_update(
        router_weight, router_first, router_second, router_sum, router_rate, router_decay
    )
    norm_first_new, norm_second_new, norm_new = adamw_update(
        norm_params, norm_first, norm_second, norm_sum, gains_rate, 0.0
    )
    return (
        block_out,
        input_grad,
        attn_mom,
        attn_new,
        router_first_new,
        router_second_new,
        router_new,
        expert_mom,
        expert_new,
        norm_first_new,
        norm_second_new,
        norm_new,
    )


def ceil_to(value, step):
    return -(-value // step) * step


def dot_exact(left, right):
    return jnp.dot(
        left, right, precision=lax.Precision.HIGH, preferred_element_type=jnp.float32
    )


def dot_low(left, right, contract=((1,), (0,))):
    return lax.dot_general(
        left, right, (contract, ((), ())), preferred_element_type=jnp.float32
    )


def block_pairs(width):
    tiles = width // TILE
    return [(i, j) for i in range(tiles) for j in range(i + 1, tiles)]


def packed_rows(width):
    tiles = width // TILE
    return (len(block_pairs(width)) + tiles // 2) * TILE + ceil_to(tiles // 2, 8)


def tile_places():
    rows = lax.broadcasted_iota(jnp.int32, (TILE, TILE), 0)
    lanes = lax.broadcasted_iota(jnp.int32, (TILE, TILE), 1)
    return rows, lanes


def pack_upper(block, width, out_ref):
    rows, lanes = tile_places()
    start = 0
    for i, j in block_pairs(width):
        out_ref[start : start + TILE, :] = block(i, j)
        start += TILE
    diagonals = []
    for i in range(0, width // TILE, 2):
        second = block(i + 1, i + 1)
        out_ref[start : start + TILE, :] = jnp.where(rows <= lanes, block(i, i), second)
        diagonals.append(
            jnp.sum(jnp.where(rows == lanes, second, 0.0), axis=0, keepdims=True)
        )
        start += TILE
    rest = out_ref.shape[0] - start - len(diagonals)
    if rest:
        diagonals.append(jnp.zeros((rest, TILE), jnp.float32))
    out_ref[start:, :] = jnp.concatenate(diagonals, axis=0)


def packed_trace(packed_ref, width):
    rows, lanes = tile_places()
    start = len(block_pairs(width)) * TILE
    total = jnp.zeros((1, 1), jnp.float32)
    pairs = width // TILE // 2
    for pair in range(pairs):
        block = packed_ref[start + pair * TILE : start + (pair + 1) * TILE, :]
        total = total + jnp.sum(jnp.where(rows == lanes, block, 0.0), keepdims=True)
    return total + jnp.sum(packed_ref[start + pairs * TILE :, :], keepdims=True)


def unpack_upper(packed_ref, out_ref, factor=None):
    rows, lanes = tile_places()
    width = out_ref.shape[0]

    def load(start, count):
        values = packed_ref[start : start + count, :]
        return values if factor is None else values * factor

    start = 0
    for i, j in block_pairs(width):
        block = load(start, TILE)
        out_ref[i * TILE : (i + 1) * TILE, j * TILE : (j + 1) * TILE] = block
        out_ref[j * TILE : (j + 1) * TILE, i * TILE : (i + 1) * TILE] = block.T
        start += TILE
    diagonals = load(start + width // 2, 8)
    for i in range(0, width // TILE, 2):
        block = load(start, TILE)
        turned = block.T
        first = jnp.where(rows <= lanes, block, turned)
        second = jnp.where(rows > lanes, block, turned)
        second = jnp.where(rows == lanes, diagonals[i // 2 : i // 2 + 1], second)
        out_ref[i * TILE : (i + 1) * TILE, i * TILE : (i + 1) * TILE] = first
        i += 1
        out_ref[i * TILE : (i + 1) * TILE, i * TILE : (i + 1) * TILE] = second
        start += TILE


def gram_packed(values, out_ref):
    rows = values.shape[0]
    half = rows // 2
    contract = (((1,), (1,)), ((), ()))
    upper = lax.dot_general(
        values[:half], values, contract,
        precision=lax.Precision.HIGH, preferred_element_type=jnp.float32,
    )
    lower = lax.dot_general(
        values[half:], values[half:], contract,
        precision=lax.Precision.HIGH, preferred_element_type=jnp.float32,
    )

    def block(i, j):
        top, left = i * TILE, j * TILE
        if top < half:
            return upper[top : top + TILE, left : left + TILE]
        return lower[top - half : top - half + TILE, left - half : left - half + TILE]

    pack_upper(block, rows, out_ref)


def own_label(experts, number):
    shard = lax.axis_index(HEADS) * lax.axis_size(DP) + lax.axis_index(DP)
    return shard * experts + number


def expert_kernel(
    first, slot_in_ref, slot_cot_ref, member_ref, router_ref, weight_ref, momentum_ref,
    momentum_out, back_out, gate_out, ahead_out, dir_out, gram_out,
):
    experts = EXPERTS // (lax.axis_size(HEADS) * lax.axis_size(DP))
    label = own_label(experts, first + pl.program_id(0))
    rows = slot_in_ref.shape[1] * slot_in_ref.shape[2]
    slot_in = slot_in_ref[0].reshape(rows, -1)
    slot_cot = slot_cot_ref[0].reshape(rows, -1).astype(jnp.float32)
    member = member_ref[0].reshape(rows, EXPERTS)
    logits = dot_low(slot_in, router_ref[...], ((1,), (1,)))
    lanes = lax.broadcasted_iota(jnp.int32, logits.shape, 1)
    own = jnp.where(lanes == label, 1.0, 0.0)
    filled = jnp.sum(member * own, axis=1, keepdims=True)
    logit_own = jnp.sum(logits * own, axis=1, keepdims=True)
    logit_other = jnp.sum(logits * (member - own), axis=1, keepdims=True)
    peak = jnp.maximum(logit_own, logit_other)
    raised = jnp.exp(logit_own - peak)
    gate = filled * raised / (raised + jnp.exp(logit_other - peak))
    up = weight_ref[0].astype(jnp.bfloat16)
    down = weight_ref[1].astype(jnp.bfloat16)
    hidden = dot_low(slot_in, up)
    cdf = 0.5 * (1.0 + lax.erf(hidden * math.sqrt(0.5)))
    active = (hidden * cdf).astype(jnp.bfloat16)
    slope = cdf + hidden * jnp.exp(-0.5 * hidden * hidden) * (1.0 / math.sqrt(2.0 * math.pi))
    expert_out = dot_low(active, down, ((1,), (1,)))
    gate_grad = jnp.sum(slot_cot * expert_out, axis=1, keepdims=True) * filled
    ahead_out[0] = (expert_out * gate).astype(jnp.bfloat16)
    out_grad = (slot_cot * gate).astype(jnp.bfloat16)
    hidden_grad = (dot_low(out_grad, down) * slope).astype(jnp.bfloat16)
    back_out[0] = dot_low(hidden_grad, up, ((1,), (1,))).astype(jnp.bfloat16)
    wide = lax.broadcasted_iota(jnp.int32, (gate_grad.shape[0], TILE), 1)
    high = gate_grad.astype(jnp.bfloat16).astype(jnp.float32)
    spread = jnp.where(wide == label, high, 0.0)
    spread = jnp.where(wide == label + EXPERTS, gate_grad - high, spread)
    gate_out[0] = spread.astype(jnp.bfloat16)
    for which, grad in enumerate(
        (
            dot_low(slot_in, hidden_grad, ((0,), (0,))),
            dot_low(out_grad, active, ((0,), (0,))),
        )
    ):
        momentum = momentum_decay * momentum_ref[which] + grad
        momentum_out[which] = momentum
        direction = grad + momentum_decay * momentum
        dir_out[which] = direction
        gram_packed(direction, gram_out.at[which])


def run_experts(first, count, slot_in, slot_cot, member, router, weights, momentum, earlier):
    _, groups, slots, width = slot_in.shape
    mats, _, hidden = weights.shape
    packed = packed_rows(width)
    shape = jax.ShapeDtypeStruct
    whole = (
        shape((mats, width, hidden), jnp.float32),
        shape((mats // 2, groups * slots, width), jnp.bfloat16),
        shape((mats // 2, groups * slots, TILE), jnp.bfloat16),
        shape((mats // 2, groups * slots, width), jnp.bfloat16),
    )
    part = (
        shape((2 * count, width, hidden), jnp.float32),
        shape((2 * count, packed, TILE), jnp.float32),
    )

    def shifted(e):
        return (first + e, 0, 0)

    def here(e):
        return (e, 0, 0)

    def slotted(e):
        return (first + e, 0, 0, 0)

    def kernel(*refs):
        expert_kernel(first, *refs[:6], *refs[6 + len(earlier) :])

    return pl.pallas_call(
        kernel,
        grid=(count,),
        in_specs=[
            pl.BlockSpec((1, groups, slots, width), slotted),
            pl.BlockSpec((1, groups, slots, width), slotted),
            pl.BlockSpec((1, groups, slots, EXPERTS), slotted),
            pl.BlockSpec(router.shape, lambda e: (0, 0)),
            pl.BlockSpec((2, width, hidden), shifted),
            pl.BlockSpec((2, width, hidden), shifted),
        ]
        + [pl.BlockSpec(memory_space=pl.ANY)] * len(earlier),
        out_specs=[
            pl.BlockSpec((2, width, hidden), shifted),
            pl.BlockSpec((1, groups * slots, width), shifted),
            pl.BlockSpec((1, groups * slots, TILE), shifted),
            pl.BlockSpec((1, groups * slots, width), shifted),
            pl.BlockSpec((2, width, hidden), here),
            pl.BlockSpec((2, packed, TILE), here),
        ],
        out_shape=whole + part,
        input_output_aliases={6 + place: place for place in range(len(earlier))},
        compiler_params=pltpu.CompilerParams(vmem_limit_bytes=VMEM_LIMIT),
        name="experts",
    )(slot_in, slot_cot, member, router, weights, momentum, *earlier)


def polish(packed_ref, out_ref, gram, poly, product, between=()):
    width = gram.shape[0]
    half = width // 2
    factor = 1.0 / (jnp.sqrt(packed_trace(packed_ref, width)) + 1e-07)
    unpack_upper(packed_ref, gram, factor * factor)

    def symmetric(left, right):
        upper = dot_exact(left[:half, :], right[...])
        corner = dot_exact(left[half:, :], right[:, half:])
        return upper, corner

    def store(ref, upper, corner):
        ref[:half, :] = upper
        ref[half:, half:] = corner
        ref[half:, :half] = upper[:, half:].T

    def eye(count):
        here = lax.broadcasted_iota(jnp.int32, (half, count), 0)
        there = lax.broadcasted_iota(jnp.int32, (half, count), 1)
        return jnp.where(here == there, coef_first, 0.0)

    def polynomial():
        upper, corner = symmetric(gram, gram)
        upper = eye(width) + coef_second * gram[:half, :] + coef_third * upper
        corner = eye(half) + coef_second * gram[half:, half:] + coef_third * corner
        return upper, corner

    def next_gram():
        store(poly, *symmetric(poly, poly))
        store(gram, *symmetric(gram, poly))

    def step(_, carry):
        store(poly, *polynomial())
        store(product, *symmetric(poly, product))
        next_gram()
        return carry

    upper, corner = polynomial()
    store(poly, upper, corner)
    store(product, upper, corner)
    next_gram()
    middle = ITERS // 2
    lax.fori_loop(1, middle, step, 0)
    for work in between:
        work()
    lax.fori_loop(middle, ITERS - 1, step, 0)
    store(poly, *polynomial())
    store(product, *symmetric(poly, product))

    def block(i, j):
        return product[i * TILE : (i + 1) * TILE, j * TILE : (j + 1) * TILE] * factor

    pack_upper(block, width, out_ref)


def neighbours(index, count):
    return [lax.rem(index + step, count) for step in range(1, count)]


def square_peers(index):
    return [3 - index, index + 1 - 2 * lax.rem(index, 2), lax.rem(index + 2, 4)]


def enter(peers):
    barrier = pltpu.get_barrier_semaphore()
    for peer in peers:
        pl.semaphore_signal(barrier, inc=1, device_id=peer, device_id_type=pl.DeviceIdType.MESH)
    pl.semaphore_wait(barrier, len(peers))


def send(source, target, send_sem, recv_sem, peer):
    copy = pltpu.make_async_remote_copy(
        src_ref=source,
        dst_ref=target,
        send_sem=send_sem,
        recv_sem=recv_sem,
        device_id=peer,
        device_id_type=pl.DeviceIdType.MESH,
    )
    copy.start()
    return copy


class Sharing:
    def __init__(self, values, out, sems):
        self.values, self.out, self.sems = values, out, sems
        self.core, self.tensor = lax.axis_index(DP), lax.axis_index(TENSOR)
        self.head, self.places = lax.axis_index(HEADS), lax.axis_size(TENSOR)
        self.along = neighbours(self.tensor, self.places)
        self.diagonal, self.beside, self.above = square_peers(self.head)
        self.origins = [self.tensor] + [
            lax.rem(self.tensor + self.places - step, self.places)
            for step in range(1, self.places)
        ]
        self.here = out.at[self.core, self.tensor, self.head]
        self.started = []

    def start(self):
        self.home = pltpu.make_async_copy(self.values, self.here, self.sems[0])
        self.home.start()
        for step, peer in enumerate(self.along):
            self.started.append(
                send(
                    self.values, self.here, self.sems[1].at[step], self.sems[2].at[step],
                    {TENSOR: peer},
                )
            )

    def to_partner(self, block, source, number):
        self.started.append(
            send(
                source, block, self.sems[5].at[number], self.sems[6].at[number],
                {DP: 1 - self.core},
            )
        )

    def to_sides(self, block, source, place):
        for step, peer in enumerate((self.beside, self.above)):
            number = 4 * place + step
            self.started.append(
                send(
                    source, block, self.sems[3].at[number], self.sems[4].at[number],
                    {HEADS: peer},
                )
            )

    def cut(self, block):
        rows = block.shape[0]
        middle = ceil_to(rows // 2, 16)
        return block.at[pl.ds(0, middle)], block.at[pl.ds(middle, rows - middle)]

    def pass_to_sides(self):
        self.to_sides(self.here, self.values, 0)
        self.to_partner(self.here, self.values, 0)
        for place in range(1, self.places):
            block = self.out.at[self.core, self.origins[place], self.head]
            wait_for(block, self.sems[2].at[place - 1])
            self.to_sides(block, block, place)
            self.to_partner(block, block, 4 * place)

    def pass_round(self):
        ways = ((self.beside, self.above), (self.above, self.beside))
        for place in range(self.places):
            for step, (peer, other) in enumerate(ways):
                block = self.out.at[self.core, self.origins[place], peer]
                wait_for(block, self.sems[4].at[4 * place + step])
                half = self.cut(block)[step]
                number = 4 * place + 2 + step
                self.started.append(
                    send(
                        half, half, self.sems[3].at[number], self.sems[4].at[number],
                        {HEADS: other},
                    )
                )
                self.to_partner(block, block, 4 * place + 1 + step)

    def own_group(self):
        for place in range(self.places):
            block = self.out.at[self.core, self.origins[place], self.diagonal]
            for step, half in enumerate(self.cut(block)):
                wait_for(half, self.sems[4].at[4 * place + 2 + step])
            self.to_partner(block, block, 4 * place + 3)
        self.home.wait()

    def other_group(self):
        corners = (self.head, self.beside, self.above, self.diagonal)
        for place in range(self.places):
            for step, peer in enumerate(corners):
                block = self.out.at[1 - self.core, self.origins[place], peer]
                wait_for(block, self.sems[6].at[4 * place + step])

    def finish(self):
        for copy in self.started:
            copy.wait_send()


def sharing_sems(places, corners):
    dma = pltpu.SemaphoreType.DMA
    blocks = places * corners
    return [dma(()), dma((places - 1,)), dma((places - 1,))] + [dma((blocks,))] * 4


def wait_for(block, sem):
    pltpu.make_async_copy(block, block, sem).wait()


class LineReduce:
    def __init__(self, parts, received, total, sems, ahead=None):
        self.parts, self.received, self.total = parts, received, total
        self.ahead = ahead
        self.send_sem, self.recv_sem = sems
        self.place = lax.axis_index(TENSOR)
        self.far = lax.axis_size(TENSOR) - 1
        self.ways = ((self.place, self.place + 1), (self.far - self.place, self.place - 1))

    def copy(self, way, slot, source):
        return pltpu.make_async_remote_copy(
            src_ref=source,
            dst_ref=self.received.at[way, slot],
            send_sem=self.send_sem.at[way, slot],
            recv_sem=self.recv_sem.at[way, slot],
            device_id={TENSOR: self.ways[way][1]},
            device_id_type=pl.DeviceIdType.MESH,
        )

    def slot(self, slot):
        for way, (behind, _) in enumerate(self.ways):
            owner = self.far - slot + behind if way == 0 else slot - behind

            @pl.when(behind == 0)
            def _():
                self.copy(way, slot, self.parts.at[owner]).start()

            if slot:

                @pl.when((behind > 0) & (behind <= slot))
                def _():
                    block = self.received.at[way, slot - 1]
                    if slot == 1 and self.ahead is not None:
                        block[...] = self.ahead[way][...] + self.parts[owner]
                    else:
                        wait_for(block, self.recv_sem.at[way, slot - 1])
                        block[...] = block[...] + self.parts[owner]
                    self.copy(way, slot, block).start()

    def final(self):
        self.total[...] = self.parts[self.place]
        for way, (behind, _) in enumerate(self.ways):

            @pl.when(behind > 0)
            def _():
                block = self.received.at[way, self.far - 1]
                wait_for(block, self.recv_sem.at[way, self.far - 1])
                self.total[...] = self.total[...] + block[...]

    def finish(self):
        for way, (behind, _) in enumerate(self.ways):
            for slot in range(0 if self.ahead is None else 1, self.far):

                @pl.when(behind <= slot)
                def _():
                    self.copy(way, slot, self.parts.at[0]).wait_send()


class LineShare:
    def __init__(self, own, out, sems):
        self.own, self.out = own, out
        self.send_sem, self.recv_sem, home_sem = sems
        self.place = lax.axis_index(TENSOR)
        self.home = pltpu.make_async_copy(own, out.at[self.place], home_sem)
        self.far = lax.axis_size(TENSOR) - 1
        self.ways = (
            (self.place, self.place + 1, -1),
            (self.far - self.place, self.place - 1, 1),
        )

    def copy(self, way, slot):
        block = self.out.at[self.place + self.ways[way][2] * slot]
        return pltpu.make_async_remote_copy(
            src_ref=block if slot else self.own,
            dst_ref=block,
            send_sem=self.send_sem.at[way, slot],
            recv_sem=self.recv_sem.at[way, slot],
            device_id={TENSOR: self.ways[way][1]},
            device_id_type=pl.DeviceIdType.MESH,
        )

    def slot(self, slot):
        if slot == 0:
            self.home.start()
        for way, (behind, _, step) in enumerate(self.ways):
            if slot:

                @pl.when(behind >= slot)
                def _():
                    block = self.out.at[self.place + step * slot]
                    wait_for(block, self.recv_sem.at[way, slot - 1])

            if slot < self.far:

                @pl.when((behind >= slot) & (behind < self.far))
                def _():
                    self.copy(way, slot).start()

    def finish(self):
        self.slot(self.far)
        self.home.wait()
        for way, (behind, _, _) in enumerate(self.ways):
            for slot in range(self.far):

                @pl.when((behind >= slot) & (behind < self.far))
                def _():
                    self.copy(way, slot).wait_send()


def line_sems(places):
    dma = pltpu.SemaphoreType.DMA
    return [dma((2, places - 1)), dma((2, places - 1))]


class Exchange:
    def __init__(self, grads, momentum, sums, whole, scratch, sems):
        self.grads, self.momentum, self.sums, self.whole = grads, momentum, sums, whole
        (
            self.from_core, self.merged, self.low, self.from_z, self.from_z_small, self.direction,
        ) = scratch
        (
            self.own_sem, self.core_send, self.core_recv, self.z_send, self.z_recv,
            self.xy_send, self.xy_recv, self.pass_send, self.pass_recv,
        ) = sems
        self.core, self.tensor = lax.axis_index(DP), lax.axis_index(TENSOR)
        self.head, self.places = lax.axis_index(HEADS), lax.axis_size(TENSOR)
        self.along = neighbours(self.tensor, self.places)
        self.across = square_peers(self.head)
        self.rows = momentum.shape[0]
        self.started = []

    def send(self, *args):
        self.started.append(send(*args))

    def start(self):
        self.send(
            self.grads.at[1 - self.core], self.from_core, self.core_send, self.core_recv,
            {DP: 1 - self.core},
        )

    def along_tensor(self):
        rows = self.rows
        wait_for(self.from_core, self.core_recv)
        for place in range(self.places):
            both = self.grads[self.core, place] + self.from_core[place]
            self.merged[place] = both
            self.low[place] = both[:rows].astype(self.low.dtype)
        others = len(self.along)
        for step, peer in enumerate(self.along):
            self.send(
                self.low.at[peer], self.from_z.at[step], self.z_send.at[step],
                self.z_recv.at[step], {TENSOR: peer},
            )
            self.send(
                self.merged.at[peer, pl.ds(rows, self.from_z_small.shape[1])],
                self.from_z_small.at[step], self.z_send.at[others + step],
                self.z_recv.at[others + step], {TENSOR: peer},
            )

    def share(self):
        rows, others = self.rows, len(self.along)
        grad = self.merged[self.tensor, :rows, :]
        small = self.merged[self.tensor, rows:, :]
        for step in range(others):
            wait_for(self.from_z.at[step], self.z_recv.at[step])
            grad = grad + self.from_z[step].astype(jnp.float32)
            wait_for(self.from_z_small.at[step], self.z_recv.at[others + step])
            small = small + self.from_z_small[step]
        self.sums[:rows, :] = grad
        self.sums[rows:, :] = small
        momentum = momentum_decay * self.momentum[...] + grad
        self.direction[...] = grad + momentum_decay * momentum
        here = self.whole.at[self.core, self.head]
        self.home = pltpu.make_async_copy(self.direction, here, self.own_sem)
        self.home.start()
        for step, peer in enumerate(self.across):
            self.send(
                self.direction, here, self.xy_send.at[step], self.xy_recv.at[step],
                {HEADS: peer},
            )
        self.send(
            self.direction, here, self.pass_send.at[0], self.pass_recv.at[0],
            {DP: 1 - self.core},
        )

    def finish(self):
        for step, peer in enumerate(self.across):
            block = self.whole.at[self.core, peer]
            wait_for(block, self.xy_recv.at[step])
            self.send(
                block, block, self.pass_send.at[step + 1], self.pass_recv.at[step + 1],
                {DP: 1 - self.core},
            )
        for step, peer in enumerate([self.head] + self.across):
            wait_for(self.whole.at[1 - self.core, peer], self.pass_recv.at[step])
        self.home.wait()
        for copy in self.started:
            copy.wait_send()


def exchange_scratch(places, heads, rows, momentum):
    f32, bf16 = jnp.float32, jnp.bfloat16
    dma = pltpu.SemaphoreType.DMA
    scratch = [
        pltpu.VMEM((places, rows, TILE), f32),
        pltpu.VMEM((places, rows, TILE), f32),
        pltpu.VMEM((places,) + momentum, bf16),
        pltpu.VMEM((places - 1,) + momentum, bf16),
        pltpu.VMEM((places - 1, rows - momentum[0], TILE), f32),
        pltpu.VMEM(momentum, f32),
    ]
    sems = [
        dma(()),
        dma(()),
        dma(()),
        dma((2 * (places - 1),)),
        dma((2 * (places - 1),)),
        dma((heads - 1,)),
        dma((heads - 1,)),
        dma((heads,)),
        dma((heads,)),
    ]
    return scratch, sems


class Combining:
    def __init__(self, payloads, out, exact_out, scratch, sems):
        self.payloads, self.out, self.exact_out = payloads, out, exact_out
        self.widths = [payload.shape[3] for payload in payloads]
        (
            self.stage, self.own, self.from_core, self.from_side, self.relay,
            self.from_next, self.low, self.from_z, self.done, *self.exact,
        ) = scratch
        (
            self.home_sem, self.core_send, self.core_recv, self.xy_send, self.xy_recv,
            self.z_send, self.z_recv, self.back_send, self.back_recv,
        ) = sems
        self.core, self.tensor = lax.axis_index(DP), lax.axis_index(TENSOR)
        self.head, self.places = lax.axis_index(HEADS), lax.axis_size(TENSOR)
        self.across = square_peers(self.head)
        self.order = neighbours(self.tensor, self.places) + [self.tensor]
        self.quarter = self.done.shape[0]
        self.started, self.homes, self.to_core = [], [], []
        self.result = None

    def send(self, *args):
        self.started.append(send(*args))

    def write(self, ref, number, pick, group):
        start = 0
        for payload, width in zip(self.payloads, self.widths):
            slots = payload[:, group].reshape(-1, width)
            ref[number, :, start : start + width] = dot_low(pick, slots).astype(ref.dtype)
            start += width

    def spread(self, number, picks):
        self.write(self.stage, number, picks[1], 1 - self.core)
        self.to_core.append(
            send(
                self.stage.at[number], self.from_core.at[number], self.core_send.at[number],
                self.core_recv.at[number], {DP: 1 - self.core},
            )
        )
        self.write(self.own, number, picks[0], self.core)

    def sides(self, number):
        _, beside, above = self.across
        return (beside, above) if number % 2 == 0 else (above, beside)

    def rows(self, corner):
        return pl.ds(pl.multiple_of(corner * self.quarter, 16), self.quarter)

    def exchange(self, number):
        wait_for(self.from_core.at[number], self.core_recv.at[number])
        both = self.own[number] + self.from_core[number].astype(jnp.float32)
        self.own[number] = both
        self.to_core[number].wait_send()
        self.stage[number] = both.astype(jnp.bfloat16)
        side = self.sides(number)[0]
        for step, corner in enumerate((self.across[0], side)):
            place = 3 * number + step
            self.send(
                self.stage.at[number, self.rows(corner)], self.from_side.at[number, step],
                self.xy_send.at[place], self.xy_recv.at[place], {HEADS: side},
            )

    def pass_on(self, number):
        following = self.sides(number)[1]
        place = 3 * number
        wait_for(self.from_side.at[number, 0], self.xy_recv.at[place])
        both = self.own[number, self.rows(following), :]
        both = both + self.from_side[number, 0].astype(jnp.float32)
        self.relay[number] = both.astype(jnp.bfloat16)
        self.send(
            self.relay.at[number], self.from_next.at[number], self.xy_send.at[place + 2],
            self.xy_recv.at[place + 2], {HEADS: following},
        )

    def reduce(self, number):
        wait_for(self.from_side.at[number, 1], self.xy_recv.at[3 * number + 1])
        wait_for(self.from_next.at[number], self.xy_recv.at[3 * number + 2])
        both = self.own[number, self.rows(self.head), :]
        both = both + self.from_side[number, 1].astype(jnp.float32)
        both = both + self.from_next[number].astype(jnp.float32)
        if number == self.places - 1:
            self.result = both
            return
        self.low[number] = both.astype(jnp.bfloat16)
        self.send(
            self.low.at[number], self.from_z.at[number], self.z_send.at[number],
            self.z_recv.at[number], {TENSOR: self.order[number]},
        )

    def share(self):
        result = self.result
        for number in range(self.places - 1):
            wait_for(self.from_z.at[number], self.z_recv.at[number])
            result = result + self.from_z[number].astype(jnp.float32)
        main = self.done.shape[1]
        self.done[...] = result[:, :main].astype(jnp.bfloat16)
        parts = [(self.done, self.out)]
        if self.exact:
            self.exact[0][...] = result[:, main:]
            parts.append((self.exact[0], self.exact_out))
        for which, (source, out) in enumerate(parts):
            here = out.at[self.head]
            home = pltpu.make_async_copy(source, here, self.home_sem.at[which])
            home.start()
            self.homes.append(home)
            for step, peer in enumerate(self.across):
                number = which * len(self.across) + step
                self.send(
                    source, here, self.back_send.at[number], self.back_recv.at[number],
                    {HEADS: peer},
                )

    def finish(self):
        outs = [self.out] + ([self.exact_out] if self.exact else [])
        for which, out in enumerate(outs):
            for step, peer in enumerate(self.across):
                number = which * len(self.across) + step
                wait_for(out.at[peer], self.back_recv.at[number])
        for home in self.homes:
            home.wait()
        for copy in self.started:
            copy.wait_send()


def combining_scratch(places, rows, quarter, widths, exact):
    wide = sum(widths)
    main = wide - (widths[-1] if exact else 0)
    f32, bf16 = jnp.float32, jnp.bfloat16
    dma = pltpu.SemaphoreType.DMA
    scratch = [
        pltpu.VMEM((places, rows, wide), bf16),
        pltpu.VMEM((places, rows, wide), f32),
        pltpu.VMEM((places, rows, wide), bf16),
        pltpu.VMEM((places, 2, quarter, wide), bf16),
        pltpu.VMEM((places, quarter, wide), bf16),
        pltpu.VMEM((places, quarter, wide), bf16),
        pltpu.VMEM((places - 1, quarter, wide), bf16),
        pltpu.VMEM((places - 1, quarter, wide), bf16),
        pltpu.VMEM((quarter, main), bf16),
    ]
    if exact:
        scratch.append(pltpu.VMEM((quarter, wide - main), f32))
    sems = [
        dma((2,)),
        dma((places,)),
        dma((places,)),
        dma((places * 3,)),
        dma((places * 3,)),
        dma((places - 1,)),
        dma((places - 1,)),
        dma((6,)),
        dma((6,)),
    ]
    return scratch, sems


def halves(values):
    lanes = lax.broadcasted_iota(jnp.int32, values.shape, 1)
    zero = jnp.zeros_like(values)
    return jnp.where(lanes < HEAD_DIM, values, zero), jnp.where(lanes < HEAD_DIM, zero, values)


def join_heads(first, second):
    lanes = lax.broadcasted_iota(jnp.int32, first.shape, 1)
    return jnp.where(lanes < HEAD_DIM, first, second)


def probabilities(query, keys):
    scores = dot_low(query, keys, ((1,), (1,))) * HEAD_DIM ** (-0.5)
    lanes = lax.broadcasted_iota(jnp.int32, scores.shape, 1)
    scores = jnp.where(lanes < SEQ, scores, -1e30)
    raised = jnp.exp(scores - jnp.max(scores, axis=1, keepdims=True))
    return raised / jnp.sum(raised, axis=1, keepdims=True)


def wide_rows(low_ref, first_row, rows):
    cores, places, _, _, tile = low_ref.shape
    shards = [low_ref[c, t, 0, first_row : first_row + rows, :] for c in range(cores) for t in range(places)]
    shards = [shard.astype(jnp.float32) for shard in shards]
    lanes = lax.broadcasted_iota(jnp.int32, (rows, tile), 1)
    tiles = []
    for left, right in zip(shards[::2], shards[1::2]):
        tiles.append(jnp.where(lanes < tile // 2, left, pltpu.roll(right, tile // 2, 1)))
    return jnp.concatenate(tiles, axis=1)


def front_kernel(slots, flat_ref, images_ref, cot_ref, ids_ref, *refs):
    outs, refs = refs[:11], refs[11:]
    results, refs = refs[:11], refs[11:]
    (
        qkv_out, mixed_out, first_out, normed_out, router_out, gains_out, weights_out,
        slot_in_out, slot_cot_out, member_out, column_out,
    ) = results
    low_ref, all_normed, all_cot, all_ids, ranks, picks, members, normed, mixed, *sems = refs
    leaving = []

    def leave(*numbers):
        for number in numbers:
            copy = pltpu.make_async_copy(results[number], outs[number], sems[22].at[number])
            copy.start()
            leaving.append(copy)

    images, padded, width = images_ref.shape
    cores, places, heads, _, tile = low_ref.shape
    f32, bf16 = jnp.float32, jnp.bfloat16
    core, head_index = lax.axis_index(DP), lax.axis_index(HEADS)
    block = width // cores
    quarter = cot_ref.shape[1]
    per = heads // images
    own_normed = normed_out.at[
        lax.div(head_index, per),
        pl.ds(pl.multiple_of(lax.rem(head_index, per) * quarter, 16), quarter),
    ]
    sharing_low = Sharing(flat_ref, low_ref, sems[:7])
    sharing_cot = Sharing(cot_ref.at[head_index], all_cot, sems[7:14])
    sharing_normed = Sharing(own_normed, all_normed, sems[14:21])
    ids_sems = sems[21]
    enter(
        [{TENSOR: peer} for peer in sharing_low.along]
        + [{HEADS: sharing_low.beside}, {HEADS: sharing_low.above}, {DP: 1 - core}]
    )
    sharing_low.start()
    ids_home = pltpu.make_async_copy(ids_ref, all_ids.at[core], ids_sems.at[0])
    ids_home.start()
    ids_copy = send(
        ids_ref, all_ids.at[core], ids_sems.at[1], ids_sems.at[2], {DP: 1 - core}
    )
    sharing_low.pass_to_sides()
    sharing_cot.start()
    ids_home.wait()
    wait_for(all_ids.at[1 - core], ids_sems.at[2])
    slot_places(slots, all_ids, ranks, column_out)
    sharing_low.pass_round()
    experts = slot_in_out.shape[0]
    groups = cores
    for group in range(groups):
        for e in range(experts):
            rank = ranks[e * groups + group : e * groups + group + 1, :]
            place = lax.broadcasted_iota(jnp.int32, (slots, rank.shape[1]), 0)
            picks[group, e * slots : (e + 1) * slots, :] = jnp.where(
                rank == place, 1.0, 0.0
            ).astype(bf16)
        lanes = lax.broadcasted_iota(jnp.int32, members.shape[1:], 1)
        start = (groups + group) * TOP
        hit = lanes == column_out[:, start : start + 1]
        for k in range(1, TOP):
            hit = hit | (lanes == column_out[:, start + k : start + k + 1])
        members[group] = jnp.where(hit, 1.0, 0.0).astype(bf16)
    for group in range(groups):
        part = dot_low(picks[group], members[group])
        for e in range(experts):
            member_out[e, group] = part[e * slots : (e + 1) * slots]
    leave(9, 10)
    sharing_cot.pass_to_sides()
    sharing_low.own_group()
    sharing_low.other_group()

    for matrix in range(4):
        for c in range(cores):
            for head in range(heads):
                start = matrix * width + head * tile
                weights_out[c * block : (c + 1) * block, start : start + tile] = low_ref[
                    c, matrix, head, :block, :
                ]
    small = wide_rows(low_ref, block, ceil_to(EXPERTS + 4, 16))
    router_out[...] = small[:EXPERTS].astype(bf16)
    gains = small[EXPERTS : EXPERTS + 8]
    gains_out[...] = gains
    leave(4, 5, 6)
    def attend(image):
        tokens = images_ref[image].astype(f32)
        here, _, _ = norm_forward(tokens, gains[0:1], gains[1:2])
        normed[...] = here.astype(bf16)
        for matrix in range(3):
            part = dot_low(normed[...], weights_out[:, matrix * width : (matrix + 1) * width])
            part = part.astype(bf16)
            for head in range(heads):
                qkv_out[matrix, head, image] = part[:, head * tile : (head + 1) * tile]
        for head in range(heads):
            keys = qkv_out[1, head, image]
            total = None
            for query, value in zip(
                halves(qkv_out[0, head, image]), halves(qkv_out[2, head, image])
            ):
                probs = probabilities(query, keys).astype(bf16)
                part = dot_low(probs, value)
                total = part if total is None else total + part
            mixed_out[head, image] = total.astype(bf16)
            mixed[:, head * tile : (head + 1) * tile] = total.astype(bf16)
        attended = dot_low(mixed[...], weights_out[:, 3 * width :], ((1,), (1,)))
        first = tokens + attended
        first_out[image] = first
        here, _, _ = norm_forward(first, gains[2:3], gains[3:4])
        normed_out[image] = here.astype(bf16)

    own_image = lax.div(head_index, per)
    attend(own_image)
    sharing_normed.start()
    sharing_cot.pass_round()
    for step in range(1, images):
        attend(lax.rem(own_image + step, images))

    def dispatch(source, out, group):
        rows = places * heads * quarter
        part = dot_low(picks[group], source[group].reshape(rows, width)).astype(bf16)
        for e in range(experts):
            out[e, group] = part[e * slots : (e + 1) * slots]

    sharing_normed.pass_to_sides()
    leave(0, 1, 2, 3)
    sharing_cot.own_group()
    sharing_normed.pass_round()
    dispatch(all_cot, slot_cot_out, core)
    sharing_cot.other_group()
    dispatch(all_cot, slot_cot_out, 1 - core)
    leave(8)
    sharing_normed.own_group()
    dispatch(all_normed, slot_in_out, core)
    sharing_normed.other_group()
    dispatch(all_normed, slot_in_out, 1 - core)
    leave(7)
    for copy in leaving:
        copy.wait()
    ids_copy.wait_send()
    for sharing in (sharing_low, sharing_cot, sharing_normed):
        sharing.finish()


def run_front(flat, images, cot, ids, experts, slots, number):
    count, padded, width = images.shape
    groups, heads = lax.axis_size(DP), lax.axis_size(HEADS)
    places, _, rows = ids.shape
    tokens = places * rows
    quarter = cot.shape[1]
    f32, bf16 = jnp.float32, jnp.bfloat16
    shape = jax.ShapeDtypeStruct
    dma = pltpu.SemaphoreType.DMA
    vmem, anywhere = pl.BlockSpec(memory_space=pltpu.VMEM), pl.BlockSpec(memory_space=pl.ANY)
    results = [
        shape((3, heads, count, padded, TILE), bf16),
        shape((heads, count, padded, TILE), bf16),
        shape((count, padded, width), f32),
        shape((count, padded, width), bf16),
        shape((EXPERTS, width), bf16),
        shape((8, width), f32),
        shape((width, 4 * width), bf16),
        shape((experts, groups, slots, width), bf16),
        shape((experts, groups, slots, width), bf16),
        shape((experts, groups, slots, EXPERTS), f32),
        shape((tokens, 2 * groups * TOP), jnp.int32),
    ]
    return pl.pallas_call(
        functools.partial(front_kernel, slots),
        in_specs=[anywhere, vmem, anywhere, anywhere],
        out_specs=[anywhere] * 11,
        out_shape=results,
        scratch_shapes=[pltpu.VMEM(result.shape, result.dtype) for result in results]
        + [
            pltpu.VMEM((groups, places, heads) + flat.shape, bf16),
            pltpu.VMEM((groups, places, heads, quarter, width), bf16),
            pltpu.VMEM((groups, places, heads, quarter, width), bf16),
            pltpu.VMEM((groups,) + ids.shape, jnp.int32),
            pltpu.VMEM((experts * groups, tokens), jnp.int32),
            pltpu.VMEM((groups, experts * slots, tokens), bf16),
            pltpu.VMEM((groups, tokens, EXPERTS), bf16),
            pltpu.VMEM((padded, width), bf16),
            pltpu.VMEM((padded, width), bf16),
        ]
        + sharing_sems(places, heads) * 3
        + [dma((3,)), dma((11,))],
        compiler_params=pltpu.CompilerParams(
            collective_id=number, has_side_effects=True, vmem_limit_bytes=VMEM_LIMIT
        ),
        name="front",
    )(flat, images, cot, ids)


def attend_back(
    back_ref, gate_ref, cot_ref, columns_ref, images_ref, first_ref, normed_b_ref, mixed_ref,
    qkv_ref, router_ref, gains_ref, weights_ref, input_out, grads_out,
    normed_a, branch, mixed_grad, qkv_grad, own_grad, between,
):
    images, padded, width = images_ref.shape
    heads, tile = mixed_ref.shape[0], mixed_ref.shape[3]
    cores = grads_out.shape[0]
    f32, bf16 = jnp.float32, jnp.bfloat16
    core = lax.axis_index(DP)
    head_index = lax.axis_index(HEADS)
    tensor = lax.axis_index(TENSOR)
    block = width // cores
    gains = gains_ref[...]
    router = router_ref[...]
    router_grad = jnp.zeros((EXPERTS, width), f32)
    sums = [jnp.zeros((1, width), f32) for _ in range(4)]
    for image in range(images):
        per = back_ref.shape[0] // images
        quarters = range(image * per, (image + 1) * per)
        back = jnp.concatenate([back_ref[q] for q in quarters], axis=0).astype(f32)
        parts = jnp.concatenate([gate_ref[q] for q in quarters], axis=0)
        columns = columns_ref[tensor, image * padded : (image + 1) * padded, :]
        ids = [
            jnp.where(core == 0, columns[:, 4 + k : 5 + k], columns[:, 6 + k : 7 + k])
            for k in range(TOP)
        ]
        lanes = lax.broadcasted_iota(jnp.int32, (padded, EXPERTS), 1)
        chosen = jnp.where((lanes == ids[0]) | (lanes == ids[1]), 1.0, 0.0)
        normed_b = normed_b_ref[image]
        logits = dot_low(normed_b, router, ((1,), (1,)))
        peak = jnp.max(jnp.where(chosen > 0, logits, -1e30), axis=1, keepdims=True)
        raised = jnp.exp(jnp.where(chosen > 0, logits - peak, -1e30))
        any_chosen = jnp.max(chosen, axis=1, keepdims=True)
        gates = raised / (jnp.sum(raised, axis=1, keepdims=True) + (1.0 - any_chosen))
        gate_grad = (parts + pltpu.roll(parts, tile - EXPERTS, 1))[:, :EXPERTS]
        blend = jnp.sum(gates * gate_grad, axis=1, keepdims=True)
        logit_grad = (gates * (gate_grad - blend)).astype(bf16)
        normed_grad = back + dot_low(logit_grad, router)
        router_grad = router_grad + dot_low(logit_grad, normed_b, ((0,), (0,)))
        _, scaled, inverse = norm_forward(first_ref[image], gains[2:3], gains[3:4])
        sums[2] = sums[2] + jnp.sum(normed_grad * scaled, axis=0, keepdims=True)
        sums[3] = sums[3] + jnp.sum(normed_grad, axis=0, keepdims=True)
        first_grad = cot_ref[image].astype(f32) + norm_backward(
            normed_grad, scaled, inverse, gains[2:3]
        )
        input_out[image] = first_grad
        branch[image] = first_grad.astype(bf16)
        mixed_grad[...] = dot_low(branch[image], weights_ref[:, 3 * width :]).astype(bf16)
        for head in range(heads):
            query, keys = qkv_ref[0, head, image], qkv_ref[1, head, image]
            values = qkv_ref[2, head, image]
            out_grad = mixed_grad[:, head * tile : (head + 1) * tile]
            query_grads, key_grads, value_grad = [], [], None
            for query_half, grad_half in zip(halves(query), halves(out_grad)):
                probs = probabilities(query_half, keys)
                prob_grad = dot_low(grad_half, values, ((1,), (1,)))
                part = dot_low(probs.astype(bf16), grad_half, ((0,), (0,)))
                value_grad = part if value_grad is None else value_grad + part
                score_grad = (
                    probs * (prob_grad - jnp.sum(probs * prob_grad, axis=1, keepdims=True))
                ).astype(bf16)
                query_grads.append(dot_low(score_grad, keys))
                key_grads.append(dot_low(score_grad, query, ((0,), (0,))))
            scale = HEAD_DIM ** (-0.5)
            for matrix, grad in enumerate(
                (join_heads(*query_grads) * scale, join_heads(*key_grads) * scale, value_grad)
            ):
                grad = grad.astype(bf16)
                start = matrix * width + head * tile
                qkv_grad[:, start : start + tile] = grad
                own_grad[matrix, head, image * padded : (image + 1) * padded, :] = grad
            for work in between.get((image, head), ()):
                work()
        normed_grad = dot_low(qkv_grad[...], weights_ref[:, : 3 * width], ((1,), (1,)))
        here, scaled, inverse = norm_forward(
            images_ref[image].astype(f32), gains[0:1], gains[1:2]
        )
        normed_a[image] = here.astype(bf16)
        sums[0] = sums[0] + jnp.sum(normed_grad * scaled, axis=0, keepdims=True)
        sums[1] = sums[1] + jnp.sum(normed_grad, axis=0, keepdims=True)
        input_out[image] = input_out[image] + norm_backward(
            normed_grad, scaled, inverse, gains[0:1]
        )
    rows = images * padded
    left = normed_a[...].reshape(rows, width)
    for matrix in range(4):
        if matrix < 3:
            grad = dot_low(left, own_grad[matrix, head_index], ((0,), (0,)))
        else:
            own_mixed = mixed_ref[head_index].reshape(rows, tile)
            grad = dot_low(branch[...].reshape(rows, width), own_mixed, ((0,), (0,)))
        for c in range(cores):
            grads_out[c, matrix, :block, :] = grad[c * block : (c + 1) * block]
    pad = grads_out.shape[2] - block - EXPERTS - 4
    small = jnp.concatenate([router_grad] + sums + [jnp.zeros((pad, width), f32)], axis=0)
    places = grads_out.shape[1]
    for c in range(cores):
        for t in range(places):
            shard = c * places + t
            piece = small[:, shard // 2 * tile : (shard // 2 + 1) * tile]
            if shard % 2:
                piece = pltpu.roll(piece, tile // 2, 1)
            grads_out[c, t, block:, :] = piece


def attn_polish(whole_ref, weights_ref, out_ref, values, gram, poly, between=()):
    cores, heads, block, tile = whole_ref.shape
    width = values.shape[0]
    half = width // 2
    core, head_index = lax.axis_index(DP), lax.axis_index(HEADS)
    squares = jnp.zeros((1, 1), jnp.float32)
    for c in range(cores):
        for h in range(heads):
            part = whole_ref[c, h]
            squares = squares + jnp.sum(part * part, keepdims=True)
    factor = 1.0 / (jnp.sqrt(squares) + 1e-07)
    for c in range(cores):
        for h in range(heads):
            values[c * block : (c + 1) * block, h * tile : (h + 1) * tile] = whole_ref[c, h] * factor

    def store(ref, upper, corner):
        ref[:half, :] = upper
        ref[half:, half:] = corner
        ref[half:, :half] = upper[:, half:].T

    def product(left, right, contract):
        return lax.dot_general(
            left, right, (contract, ((), ())),
            precision=lax.Precision.HIGH, preferred_element_type=jnp.float32,
        )

    for step in range(ITERS):
        across = ((1,), (1,))
        store(
            gram,
            product(values[:half, :], values[...], across),
            product(values[half:, :], values[half:, :], across),
        )
        along = ((1,), (0,))
        upper = product(gram[:half, :], gram[...], along)
        corner = product(gram[half:, :], gram[:, half:], along)
        store(
            poly,
            coef_second * gram[:half, :] + coef_third * upper,
            coef_second * gram[half:, half:] + coef_third * corner,
        )
        values[...] = coef_first * values[...] + product(poly[...], values[...], along)
        if step == ITERS // 2:
            for work in between:
                work()
    scale = muon_scale(width, heads * tile)
    for c in range(cores):
        for h in range(heads):

            @pl.when((core == c) & (head_index == h))
            def _():
                own = values[c * block : (c + 1) * block, h * tile : (h + 1) * tile]
                out_ref[...] = weights_ref[...] * (1.0 - muon_rate * muon_decay) - scale * own


def back_kernel(
    gram_first, ahead_right, ahead_left, columns, back, gates, router, gains, momentum,
    attn_weights, *refs,
):
    late, refs = refs[:9], refs[9:]
    ahead_out, input_out, sums_out, attn_out, share_first, share_second, *refs = refs
    loaded, refs = refs[:9], refs[9:]
    ahead, gram_second, weights, qkv, first, cot, images, normed_b, mixed = loaded
    (
        back_total, gates_total, received_first, received_second, total_first, total_second,
        polish_gram, polish_poly, polish_product, grads, normed_a, branch, mixed_grad, qkv_grad,
        own_grad, whole, load_sem, *refs,
    ) = refs
    loading = [
        pltpu.make_async_copy(source, target, load_sem.at[number])
        for number, (source, target) in enumerate(zip(late, loaded))
    ]
    for copy in loading:
        copy.start()
    refs = list(refs)

    def take(count):
        taken = refs[:count]
        del refs[:count]
        return taken

    combine_back = Combining((back, gates), back_total, gates_total, take(10), take(9))
    combine_ahead = Combining((ahead,), ahead_out, None, take(9), take(9))
    reduce_first = LineReduce(
        gram_first, received_first, total_first, take(2), (ahead_right, ahead_left)
    )
    reduce_second = LineReduce(gram_second, received_second, total_second, take(2))
    line_first = LineShare(total_first, share_first, take(3))
    line_second = LineShare(total_second, share_second, take(3))
    exchange = Exchange(grads, momentum, sums_out, whole, take(6), take(9))
    core = lax.axis_index(DP)
    places, rows, _ = columns.shape
    experts, _, slots, _ = back.shape
    lanes_total = experts * slots
    enter(
        [{TENSOR: peer} for peer in combine_back.order[:-1]]
        + [{HEADS: peer} for peer in combine_back.across]
        + [{DP: 1 - core}]
    )

    def pick(group, place):
        table = columns[place]
        lanes = lax.broadcasted_iota(jnp.int32, (rows, lanes_total), 1)
        hit = None
        for k in range(TOP):
            code = jnp.where(group == 0, table[:, k : k + 1], table[:, TOP + k : TOP + k + 1])
            here = code == lanes
            hit = here if hit is None else hit | here
        return jnp.where(hit, 1.0, 0.0).astype(jnp.bfloat16)

    reduce_first.slot(1)
    last = places - 1
    for number, place in enumerate(combine_back.order):
        combine_back.spread(number, (pick(core, place), pick(1 - core, place)))
        if number > 0:
            combine_back.exchange(number - 1)
        if number > 1:
            combine_back.pass_on(number - 2)
    combine_back.exchange(last)
    reduce_first.slot(2)
    loading[0].wait()
    for number, place in enumerate(combine_back.order):
        combine_ahead.spread(number, (pick(core, place), pick(1 - core, place)))
        if number >= 2:
            combine_back.pass_on(last - 3 + number)
    for copy in loading[1:]:
        copy.wait()
    reduce_first.final()
    reduce_second.slot(0)
    for number in range(places):
        combine_back.reduce(number)
    polish_refs = (polish_gram, polish_poly, polish_product)
    polish(
        total_first, total_first, *polish_refs,
        between=(combine_back.share, lambda: reduce_second.slot(1)),
    )
    for number in range(places):
        combine_ahead.exchange(number)
    combine_back.finish()
    between = {
        (0, 0): (lambda: reduce_second.slot(2),),
        (0, 2): (lambda: [combine_ahead.pass_on(number) for number in range(places)],),
        (1, 1): (lambda: line_first.slot(0),),
    }
    attend_back(
        back_total, gates_total, cot, columns, images, first, normed_b, mixed, qkv, router, gains,
        weights, input_out, grads, normed_a, branch, mixed_grad, qkv_grad, own_grad, between,
    )
    exchange.start()
    reduce_second.final()
    exchange.along_tensor()
    for number in range(places):
        combine_ahead.reduce(number)
    polish(
        total_second, total_second, *polish_refs,
        between=(exchange.share, lambda: line_first.slot(1)),
    )
    line_second.slot(0)
    combine_ahead.share()
    exchange.finish()
    line_first.slot(2)
    line_second.slot(1)
    attn_polish(
        whole, attn_weights, attn_out, *polish_refs, between=(lambda: line_second.slot(2),)
    )
    line_first.finish()
    combine_ahead.finish()
    reduce_first.finish()
    reduce_second.finish()
    line_second.finish()


def run_back(
    grams, sent, columns, back, gates, ahead, cot, images, first, normed_b, mixed, qkv, router,
    gains, weights, momentum, attn_weights, rows, number,
):
    places, block_rows, _ = columns.shape
    groups, heads = lax.axis_size(DP), lax.axis_size(HEADS)
    count, padded, width = images.shape
    quarter = block_rows // heads
    extra = gates.shape[3]
    f32, bf16 = jnp.float32, jnp.bfloat16
    shape = jax.ShapeDtypeStruct
    vmem, anywhere = pl.BlockSpec(memory_space=pltpu.VMEM), pl.BlockSpec(memory_space=pl.ANY)
    back_scratch, back_sems = combining_scratch(places, block_rows, quarter, (width, extra), True)
    ahead_scratch, ahead_sems = combining_scratch(places, block_rows, quarter, (width,), False)
    gram = grams[0].shape[1:]
    exchange_refs, exchange_sems = exchange_scratch(places, heads, rows, momentum.shape)
    early = (
        grams[0], *sent, columns, back, gates, router, gains, momentum, attn_weights,
    )
    late = (ahead, grams[1], weights, qkv, first, cot, images, normed_b, mixed)
    return pl.pallas_call(
        back_kernel,
        in_specs=[vmem] * len(early) + [anywhere] * len(late),
        out_specs=[anywhere] + [vmem] * 3 + [anywhere] * 2,
        out_shape=[
            shape((heads, quarter, width), bf16),
            shape((count, padded, width), f32),
            shape((rows, TILE), f32),
            shape(attn_weights.shape, f32),
            shape((places,) + gram, f32),
            shape((places,) + gram, f32),
        ],
        scratch_shapes=[pltpu.VMEM(values.shape, values.dtype) for values in late]
        + [
            pltpu.VMEM((heads, quarter, width), bf16),
            pltpu.VMEM((heads, quarter, extra), f32),
            pltpu.VMEM((2, places - 1) + gram, f32),
            pltpu.VMEM((2, places - 1) + gram, f32),
            pltpu.VMEM(gram, f32),
            pltpu.VMEM(gram, f32),
            pltpu.VMEM((width, width), f32),
            pltpu.VMEM((width, width), f32),
            pltpu.VMEM((width, width), f32),
            pltpu.VMEM((groups, places, rows, TILE), f32),
            pltpu.VMEM((count, padded, width), bf16),
            pltpu.VMEM((count, padded, width), bf16),
            pltpu.VMEM((padded, width), bf16),
            pltpu.VMEM((padded, 3 * width), bf16),
            pltpu.VMEM((3, heads, count * padded, TILE), bf16),
            pltpu.VMEM((groups, heads) + momentum.shape, f32),
            pltpu.SemaphoreType.DMA((len(late),)),
        ]
        + back_scratch
        + back_sems
        + ahead_scratch
        + ahead_sems
        + line_sems(places) * 2
        + (line_sems(places) + [pltpu.SemaphoreType.DMA(())]) * 2
        + exchange_refs
        + exchange_sems,
        compiler_params=pltpu.CompilerParams(
            collective_id=number, has_side_effects=True, vmem_limit_bytes=VMEM_LARGE
        ),
        name="back",
    )(*early, *late)


def slot_places(slots, ids_ref, rank_out, column_out):
    groups, places, _, rows = ids_ref.shape
    experts = rank_out.shape[0] // groups
    labels = [own_label(experts, e).astype(jnp.float32) for e in range(experts)]
    wide = ceil_to(rows, TILE)
    earlier = lax.broadcasted_iota(jnp.int32, (rows, rows), 0)
    later = lax.broadcasted_iota(jnp.int32, (rows, rows), 1)
    before = jnp.where(earlier < later, 1.0, 0.0).astype(jnp.bfloat16)
    running = jnp.zeros((groups * experts, 1), jnp.float32)
    ranks = []
    for place in range(places):
        ids = [
            ids_ref[g, place, k : k + 1, :].astype(jnp.float32)
            for g in range(groups)
            for k in range(TOP)
        ]
        marks = []
        for e in range(experts):
            for g in range(groups):
                hit = ids[TOP * g] == labels[e]
                for k in range(1, TOP):
                    hit = hit | (ids[TOP * g + k] == labels[e])
                marks.append(jnp.where(hit, 1.0, 0.0))
        marks = jnp.concatenate(marks, axis=0)
        rank = running + dot_low(marks.astype(jnp.bfloat16), before)
        running = running + jnp.sum(marks, axis=1, keepdims=True)
        rank = jnp.where(marks > 0, rank, -1.0)
        ranks.append(rank)
        codes = []
        for g in range(groups):
            for k in range(TOP):
                code = jnp.full((1, rows), -1.0, jnp.float32)
                for e in range(experts):
                    own = ids[TOP * g + k] == labels[e]
                    number = e * groups + g
                    code = jnp.where(own, rank[number : number + 1] + float(slots * e), code)
                codes.append(code)
        both = jnp.concatenate(codes + ids, axis=0)
        columns = both.shape[0]
        both = jnp.concatenate(
            [both, jnp.zeros((columns, wide - rows), jnp.float32)], axis=1
        )
        both = jnp.concatenate([both, jnp.zeros((TILE - columns, wide), jnp.float32)], axis=0)
        for start in range(0, rows, TILE):
            turned = both[:, start : start + TILE].T
            count = min(TILE, rows - start)
            column_out[place * rows + start : place * rows + start + count, :] = turned[
                :count, :columns
            ].astype(jnp.int32)
    rank_out[...] = jnp.concatenate(ranks, axis=1).astype(jnp.int32)


def apply_kernel(scale, packed_ref, dir_ref, weight_ref, out_ref, whole):
    unpack_upper(packed_ref.at[0], whole)
    ortho = dot_exact(whole[...], dir_ref[0])
    out_ref[0] = weight_ref[0] * (1.0 - muon_rate * muon_decay) - scale * ortho


def run_apply(first, scale, packed, direction, weights, earlier):
    count, width, hidden = direction.shape

    def kernel(packed_ref, dir_ref, weight_ref, *refs):
        apply_kernel(scale, packed_ref, dir_ref, weight_ref, *refs[len(earlier) :])

    return pl.pallas_call(
        kernel,
        grid=(count,),
        in_specs=[
            pl.BlockSpec((1,) + packed.shape[1:], lambda m: (m, 0, 0)),
            pl.BlockSpec((1, width, hidden), lambda m: (m, 0, 0)),
            pl.BlockSpec((1, width, hidden), lambda m: (first + m, 0, 0)),
        ]
        + [pl.BlockSpec(memory_space=pl.ANY)] * len(earlier),
        out_specs=pl.BlockSpec((1, width, hidden), lambda m: (first + m, 0, 0)),
        out_shape=jax.ShapeDtypeStruct(weights.shape, jnp.float32),
        input_output_aliases={3 + place: place for place in range(len(earlier))},
        scratch_shapes=[pltpu.VMEM((width, width), jnp.float32)],
        compiler_params=pltpu.CompilerParams(vmem_limit_bytes=VMEM_LIMIT),
        name="apply",
    )(packed, direction, weights, *earlier)


def shards_fast(
    images_in,
    attn_weights,
    attn_momentum,
    router_weight,
    router_first,
    router_second,
    expert_weights,
    expert_momentum,
    norm_params,
    norm_first,
    norm_second,
    expert_ids,
    cotangent,
):
    rows, width = images_in.shape
    dp_count = lax.axis_size(DP)
    head_count = lax.axis_size(HEADS)
    tensor_count = lax.axis_size(TENSOR)
    mats = expert_weights.shape[0]
    hidden_cols = expert_weights.shape[2]
    group_rows = expert_ids.shape[0]
    slots = ceil_to(3 * TOP * group_rows // (2 * EXPERTS), 16)
    images = rows // SEQ
    image_rows = ceil_to(SEQ, 16 * head_count // math.gcd(images, head_count))
    padded_rows = images * image_rows
    quarter = padded_rows // head_count
    bf16, f32 = jnp.bfloat16, jnp.float32

    def pad_images(values):
        values = values.reshape(-1, SEQ, values.shape[-1])
        return jnp.pad(values, ((0, 0), (0, image_rows - SEQ), (0, 0)))

    def drop_padding(values):
        return values.reshape(images, image_rows, -1)[:, :SEQ].reshape(rows, -1)

    attn_rows = attn_weights.size // TILE
    small = jnp.concatenate((router_weight.T, norm_params), axis=0).astype(bf16)
    small_rows, small_lanes = small.shape
    small = jnp.pad(
        small, ((0, ceil_to(small_rows, 16) - small_rows), (0, TILE - small_lanes))
    )
    flat = jnp.concatenate((attn_weights.astype(bf16).reshape(attn_rows, TILE), small), axis=0)
    padded_cot = pad_images(cotangent)
    padded_images = pad_images(images_in)
    own_ids = jnp.pad(
        expert_ids.reshape(-1, SEQ, TOP), ((0, 0), (0, image_rows - SEQ), (0, 0)), constant_values=-1
    )
    own_ids = jnp.transpose(own_ids.reshape(tensor_count, padded_rows, TOP), (0, 2, 1))
    experts_own = mats // 2

    (
        qkv, mixed, first, normed_b, router_low, gains, weights_low, slot_in, slot_cot, member, columns,
    ) = run_front(
        flat, padded_images, padded_cot.reshape(head_count, quarter, width), own_ids,
        experts_own, slots, 1,
    )

    step = tensor_count // 2
    earlier = ()
    directions, packed = [], []
    for start in range(0, experts_own, step):
        *earlier, direction, gram = run_experts(
            start, step, slot_in, slot_cot, member, router_low, expert_weights, expert_momentum,
            tuple(earlier),
        )
        directions.append(direction)
        packed.append(gram)
    expert_mom, back, gate_back, ahead = earlier
    places = columns.reshape(tensor_count, padded_rows, -1)

    def by_group(values):
        return values.reshape(experts_own, dp_count, slots, values.shape[-1])

    far = tensor_count - 1
    sent = (
        lax.ppermute(packed[0][far], TENSOR, [(0, 1)]),
        lax.ppermute(packed[0][0], TENSOR, [(far, far - 1)]),
    )
    ahead_total, input_grad, sums, attn_new, *products = run_back(
        packed, sent, places, by_group(back), by_group(gate_back), by_group(ahead), padded_cot,
        padded_images, first, normed_b, mixed, qkv, router_low, gains, weights_low,
        attn_momentum.reshape(attn_rows, TILE), attn_weights.reshape(attn_rows, TILE),
        flat.shape[0], 2,
    )
    scale = muon_scale(width, hidden_cols * tensor_count)
    expert_new = ()
    for number, (product, direction) in enumerate(zip(products, directions)):
        expert_new = (
            run_apply(number * tensor_count, scale, product, direction, expert_weights, expert_new),
        )
    expert_new = expert_new[0]
    block_out = drop_padding(
        first + ahead_total.reshape(images, image_rows, width).astype(f32)
    )
    input_grad = drop_padding(input_grad)
    attn_sum = sums[:attn_rows].reshape(attn_weights.shape)
    router_sum = sums[attn_rows : attn_rows + EXPERTS, :small_lanes].T
    norm_sum = sums[attn_rows + EXPERTS : attn_rows + small_rows, :small_lanes]
    attn_mom = momentum_decay * attn_momentum + attn_sum
    attn_new = attn_new.reshape(attn_weights.shape)

    router_first_new, router_second_new, router_new = adamw_update(
        router_weight, router_first, router_second, router_sum, router_rate, router_decay
    )
    norm_first_new, norm_second_new, norm_new = adamw_update(
        norm_params, norm_first, norm_second, norm_sum, gains_rate, 0.0
    )
    return (
        block_out,
        input_grad,
        attn_mom,
        attn_new,
        router_first_new,
        router_second_new,
        router_new,
        expert_mom,
        expert_new,
        norm_first_new,
        norm_second_new,
        norm_new,
    )


def solution(mesh):
    in_specs = (
        P((DP, TENSOR), None),
        P(TENSOR, DP, HEADS),
        P(TENSOR, DP, HEADS),
        P((DP, TENSOR), None),
        P((DP, TENSOR), None),
        P((DP, TENSOR), None),
        P((HEADS, DP), None, TENSOR),
        P((HEADS, DP), None, TENSOR),
        P(None, (DP, TENSOR)),
        P(None, (DP, TENSOR)),
        P(None, (DP, TENSOR)),
        P(DP, None),
        P((DP, TENSOR), None),
    )
    out_specs = (
        P((DP, TENSOR), None),
        P((DP, TENSOR), None),
        P(TENSOR, DP, HEADS),
        P(TENSOR, DP, HEADS),
        P((DP, TENSOR), None),
        P((DP, TENSOR), None),
        P((DP, TENSOR), None),
        P((HEADS, DP), None, TENSOR),
        P((HEADS, DP), None, TENSOR),
        P(None, (DP, TENSOR)),
        P(None, (DP, TENSOR)),
        P(None, (DP, TENSOR)),
    )
    shape = dict(mesh.shape)
    step = EXPERTS * 2 // (shape[HEADS] * shape[DP])
    fits = shape[DP] == 2 and shape[HEADS] == 4 and step % (2 * shape[TENSOR]) == 0
    fits = fits and step == 2 * shape[TENSOR] and shape[TENSOR] % 2 == 0
    shards = shards_fast if fits else shards_general
    return jax.shard_map(shards, mesh=mesh, in_specs=in_specs, out_specs=out_specs, check_vma=False)
```

```python
import functools
import math

import jax
import jax.numpy as jnp
from jax import lax
from jax.experimental import pallas as pl
from jax.experimental.pallas import tpu as pltpu
from jax.sharding import PartitionSpec as P

EXPERTS = 32
SEQ = 197
TOP = 2
ITERS = 5
STEP = 5
HEAD_DIM = 64


norm_epsilon = 1e-06
coef_first = 3.4445
coef_second = -4.775
coef_third = 2.0315
momentum_decay = 0.95
muon_rate = 0.2
muon_decay = 0.1
adam_first = 0.9
adam_second = 0.999
adam_epsilon = 1e-08
router_rate = 0.03
router_decay = 0.01
gains_rate = 0.1
TILE = 128
DP, HEADS, TENSOR = "dp", "heads", "tensor"
TO_ALL, OWN_HEAD, TO_CORE = range(3)
VMEM_LIMIT = 56 * 1024 * 1024
VMEM_LARGE = 62 * 1024 * 1024


def norm_forward(values, gain, shift):
    center = jnp.mean(values, axis=-1, keepdims=True)
    centred = values - center
    inverse = lax.rsqrt(jnp.mean(centred * centred, axis=-1, keepdims=True) + norm_epsilon)
    scaled = centred * inverse
    return (scaled * gain + shift, scaled, inverse)


def norm_backward(grad_normed, scaled, inverse, gain):
    grad_scaled = grad_normed * gain
    inner = grad_scaled - jnp.mean(grad_scaled, axis=-1, keepdims=True)
    inner = inner - scaled * jnp.mean(grad_scaled * scaled, axis=-1, keepdims=True)
    return inner * inverse


def exact_gelu(values):
    return jax.nn.gelu(values, approximate=False)


def batch_gram(values):
    return jnp.einsum("mij,mkj->mik", values, values, precision=lax.Precision.HIGHEST)


def batch_product(left, right):
    return jnp.einsum("mij,mjk->mik", left, right, precision=lax.Precision.HIGHEST)


def polish_step(values, gram):
    poly = coef_second * gram + coef_third * batch_product(gram, gram)
    return coef_first * values + batch_product(poly, values)


def muon_scale(rows, cols):
    return muon_rate * 0.2 * math.sqrt(max(rows, cols))


def adamw_update(values, first, second, grad, rate, decay):
    first_new = adam_first * first + (1.0 - adam_first) * grad
    second_new = adam_second * second + (1.0 - adam_second) * grad * grad
    first_hat = first_new / (1.0 - adam_first**STEP)
    second_hat = second_new / (1.0 - adam_second**STEP)
    values_new = values * (1.0 - rate * decay) - rate * first_hat / (
        jnp.sqrt(second_hat) + adam_epsilon
    )
    return (first_new, second_new, values_new)


def shards_general(
    images_in,
    attn_weights,
    attn_momentum,
    router_weight,
    router_first,
    router_second,
    expert_weights,
    expert_momentum,
    norm_params,
    norm_first,
    norm_second,
    expert_ids,
    cotangent,
):
    local_rows, width = images_in.shape
    dp_count = lax.axis_size(DP)
    head_count = lax.axis_size(HEADS)
    tensor_count = lax.axis_size(TENSOR)
    mats_here = attn_weights.shape[0]
    row_shard = attn_weights.shape[1]
    head_cols = attn_weights.shape[2]
    hidden_cols = expert_weights.shape[2]
    group_rows = expert_ids.shape[0]
    capacity = 3 * TOP * group_rows // (2 * EXPERTS)
    experts_here = EXPERTS // head_count
    heads_here = head_cols // HEAD_DIM
    images = local_rows // SEQ
    score_scale = HEAD_DIM ** (-0.5)
    head_index = lax.axis_index(HEADS)
    tensor_index = lax.axis_index(TENSOR)
    dp_index = lax.axis_index(DP)
    attn_low, router_low, norms_low = (
        lax.all_gather(attn_weights.astype(jnp.bfloat16), (DP, TENSOR), axis=0, tiled=True),
        lax.all_gather(router_weight.astype(jnp.bfloat16), (DP, TENSOR), axis=0, tiled=True),
        lax.all_gather(norm_params.astype(jnp.bfloat16), (DP, TENSOR), axis=1, tiled=True),
    )
    attn_low = attn_low.reshape(dp_count, tensor_count * mats_here, row_shard, head_cols)
    attn_low = jnp.transpose(attn_low, (1, 0, 2, 3)).reshape(
        tensor_count * mats_here, width, head_cols
    )
    gains = norms_low.astype(jnp.float32)
    qkv_weight = jnp.transpose(attn_low[:3], (1, 0, 2)).reshape(width, 3 * head_cols)
    out_weight = attn_low[3]
    tokens = images_in.astype(jnp.float32)
    normed_a, scaled_a, inverse_a = norm_forward(tokens, gains[0], gains[1])
    normed_a = normed_a.astype(jnp.bfloat16)
    qkv = jnp.dot(normed_a, qkv_weight, preferred_element_type=jnp.float32).astype(jnp.bfloat16)
    split = qkv.reshape(images, SEQ, 3, heads_here, HEAD_DIM)
    query = split[:, :, 0]
    keys = split[:, :, 1]
    values = split[:, :, 2]
    scores = (
        jnp.einsum("ishd,ithd->ihst", query, keys, preferred_element_type=jnp.float32) * score_scale
    )
    peak = jnp.max(scores, axis=-1, keepdims=True)
    logsum = peak + jnp.log(jnp.sum(jnp.exp(scores - peak), axis=-1, keepdims=True))
    probs_low = jnp.exp(scores - logsum).astype(jnp.bfloat16)
    mixed = jnp.einsum("ihst,ithd->ishd", probs_low, values, preferred_element_type=jnp.float32)
    mixed = mixed.reshape(local_rows, head_cols).astype(jnp.bfloat16)
    partial_out = jnp.einsum("tc,dc->td", mixed, out_weight, preferred_element_type=jnp.float32)
    attended = lax.psum(partial_out, HEADS)
    first = tokens + attended
    normed_b, scaled_b, inverse_b = norm_forward(first, gains[2], gains[3])
    normed_b = normed_b.astype(jnp.bfloat16)
    group_in, group_cot = (
        lax.all_gather(normed_b, TENSOR, axis=0, tiled=True),
        lax.all_gather(cotangent, TENSOR, axis=0, tiled=True),
    )
    logits = jnp.dot(group_in, router_low, preferred_element_type=jnp.float32)
    chosen = jnp.take_along_axis(logits, expert_ids, axis=1)
    raised = jnp.exp(chosen - jnp.max(chosen, axis=1, keepdims=True))
    gates = raised / jnp.sum(raised, axis=1, keepdims=True)
    routes = expert_ids.reshape(-1)
    route_count = routes.shape[0]
    order = jnp.argsort(routes * route_count + jnp.arange(route_count, dtype=jnp.int32))
    labels = head_index * experts_here + jnp.arange(experts_here, dtype=jnp.int32)
    counts = jnp.sum((routes[None, :] == labels[:, None]).astype(jnp.int32), axis=1)
    starts = jnp.sum((routes[None, :] < labels[:, None]).astype(jnp.int32), axis=1)
    slot_index = jnp.arange(capacity, dtype=jnp.int32)
    picked = order[jnp.minimum(starts[:, None] + slot_index[None, :], route_count - 1)]
    filled = (slot_index[None, :] < counts[:, None]).astype(jnp.float32)
    token_rows = (picked // TOP).reshape(-1)
    pick_cols = (picked % TOP).reshape(-1)
    slot_gate = gates[token_rows, pick_cols].reshape(experts_here, capacity) * filled
    slot_in = group_in[token_rows].reshape(experts_here, capacity, width)
    pair = lax.all_gather(expert_weights.astype(jnp.bfloat16), DP, axis=0, tiled=True).reshape(
        experts_here, 2, width, hidden_cols
    )
    hidden = jnp.einsum("ecd,edf->ecf", slot_in, pair[:, 0], preferred_element_type=jnp.float32)
    active, gelu_pull = jax.vjp(exact_gelu, hidden)
    active = active.astype(jnp.bfloat16)
    expert_out = jnp.einsum("ecf,edf->ecd", active, pair[:, 1], preferred_element_type=jnp.float32)
    weighted = (expert_out * slot_gate[:, :, None]).reshape(-1, width)
    spread = jnp.zeros((group_rows, width), jnp.float32).at[token_rows].add(weighted)
    own_sum = lax.psum_scatter(spread, TENSOR, scatter_dimension=0, tiled=True)
    moe_out = lax.psum(own_sum, HEADS)
    block_out = first + moe_out
    grad_out = cotangent.astype(jnp.float32)
    slot_cot = group_cot[token_rows].reshape(experts_here, capacity, width).astype(jnp.float32)
    gate_grad = jnp.sum(slot_cot * expert_out, axis=-1) * filled
    out_grad = (slot_cot * slot_gate[:, :, None]).astype(jnp.bfloat16)
    pair_back = lax.all_gather(
        expert_weights.astype(jnp.bfloat16), DP, axis=0, tiled=True
    ).reshape(experts_here, 2, width, hidden_cols)
    active_grad = jnp.einsum(
        "ecd,edf->ecf", out_grad, pair_back[:, 1], preferred_element_type=jnp.float32
    )
    hidden_grad = gelu_pull(active_grad)[0].astype(jnp.bfloat16)
    down_grad = jnp.einsum("ecd,ecf->edf", out_grad, active, preferred_element_type=jnp.float32)
    up_grad = jnp.einsum("ecd,ecf->edf", slot_in, hidden_grad, preferred_element_type=jnp.float32)
    slot_in_grad = jnp.einsum(
        "ecf,edf->ecd", hidden_grad, pair_back[:, 0], preferred_element_type=jnp.float32
    ).reshape(-1, width)
    back_spread = jnp.zeros((group_rows, width), jnp.float32).at[token_rows].add(slot_in_grad)
    gate_spread = (
        jnp.zeros((group_rows, TOP), jnp.float32)
        .at[token_rows, pick_cols]
        .add(gate_grad.reshape(-1))
    )
    own_back, own_gate = (
        lax.psum_scatter(back_spread, TENSOR, scatter_dimension=0, tiled=True),
        lax.psum_scatter(gate_spread, TENSOR, scatter_dimension=0, tiled=True),
    )
    normed_b_grad, gate_total = lax.psum((own_back, own_gate), HEADS)
    matrix_grads = jnp.stack((up_grad, down_grad), axis=1).reshape(
        2 * experts_here, width, hidden_cols
    )
    expert_grad = lax.psum_scatter(matrix_grads, DP, scatter_dimension=0, tiled=True)
    own_ids = lax.dynamic_slice_in_dim(expert_ids, tensor_index * local_rows, local_rows, 0)
    own_gates = lax.dynamic_slice_in_dim(gates, tensor_index * local_rows, local_rows, 0)
    blend = jnp.sum(own_gates * gate_total, axis=1, keepdims=True)
    chosen_grad = own_gates * (gate_total - blend)
    expert_labels = jnp.arange(EXPERTS, dtype=jnp.int32)
    matches = (own_ids[:, :, None] == expert_labels[None, None, :]).astype(jnp.float32)
    logit_grad = jnp.sum(matches * chosen_grad[:, :, None], axis=1).astype(jnp.bfloat16)
    normed_b_grad = normed_b_grad + jnp.einsum(
        "te,de->td", logit_grad, router_low, preferred_element_type=jnp.float32
    )
    router_grad = jnp.einsum("td,te->de", normed_b, logit_grad, preferred_element_type=jnp.float32)
    gain_b_grad = jnp.sum(normed_b_grad * scaled_b, axis=0)
    shift_b_grad = jnp.sum(normed_b_grad, axis=0)
    first_grad = grad_out + norm_backward(normed_b_grad, scaled_b, inverse_b, gains[2])
    branch_grad = first_grad.astype(jnp.bfloat16)
    out_weight_grad = jnp.einsum(
        "td,tc->dc", branch_grad, mixed, preferred_element_type=jnp.float32
    )
    mixed_grad = jnp.einsum(
        "td,dc->tc", branch_grad, out_weight, preferred_element_type=jnp.float32
    ).astype(jnp.bfloat16)
    mixed_grad = mixed_grad.reshape(images, SEQ, heads_here, HEAD_DIM)
    scores_again = (
        jnp.einsum("ishd,ithd->ihst", query, keys, preferred_element_type=jnp.float32) * score_scale
    )
    probs_again = jnp.exp(scores_again - logsum)
    prob_grad = jnp.einsum(
        "ishd,ithd->ihst", mixed_grad, values, preferred_element_type=jnp.float32
    )
    value_grad = jnp.einsum(
        "ihst,ishd->ithd",
        probs_again.astype(jnp.bfloat16),
        mixed_grad,
        preferred_element_type=jnp.float32,
    )
    score_grad = (
        probs_again * (prob_grad - jnp.sum(probs_again * prob_grad, axis=-1, keepdims=True))
    ).astype(jnp.bfloat16)
    query_grad = (
        jnp.einsum("ihst,ithd->ishd", score_grad, keys, preferred_element_type=jnp.float32)
        * score_scale
    )
    key_grad = (
        jnp.einsum("ihst,ishd->ithd", score_grad, query, preferred_element_type=jnp.float32)
        * score_scale
    )
    qkv_grad = (
        jnp.stack((query_grad, key_grad, value_grad), axis=2)
        .reshape(local_rows, 3 * head_cols)
        .astype(jnp.bfloat16)
    )
    normed_a_part = jnp.einsum(
        "tc,dc->td", qkv_grad, qkv_weight, preferred_element_type=jnp.float32
    )
    qkv_weight_grad = jnp.einsum(
        "td,tc->dc", normed_a, qkv_grad, preferred_element_type=jnp.float32
    )
    normed_a_grad = lax.psum(normed_a_part, HEADS)
    gain_a_grad = jnp.sum(normed_a_grad * scaled_a, axis=0)
    shift_a_grad = jnp.sum(normed_a_grad, axis=0)
    input_grad = first_grad + norm_backward(normed_a_grad, scaled_a, inverse_a, gains[0])
    attn_grad = jnp.concatenate(
        (
            jnp.transpose(qkv_weight_grad.reshape(width, 3, head_cols), (1, 0, 2)),
            out_weight_grad[None],
        ),
        axis=0,
    )
    arranged = attn_grad.reshape(tensor_count, mats_here, dp_count, row_shard, head_cols)
    arranged = jnp.transpose(arranged, (2, 0, 1, 3, 4)).reshape(
        dp_count * tensor_count * mats_here, row_shard, head_cols
    )
    norm_grad = jnp.stack((gain_a_grad, shift_a_grad, gain_b_grad, shift_b_grad))
    attn_sum, router_sum, norm_sum = (
        lax.psum_scatter(arranged, (DP, TENSOR), scatter_dimension=0, tiled=True),
        lax.psum_scatter(router_grad, (DP, TENSOR), scatter_dimension=0, tiled=True),
        lax.psum_scatter(norm_grad, (DP, TENSOR), scatter_dimension=1, tiled=True),
    )
    attn_mom = momentum_decay * attn_momentum + attn_sum
    attn_dir = attn_sum + momentum_decay * attn_mom
    whole = lax.all_gather(attn_dir, (DP, HEADS), axis=1, tiled=True)
    whole = whole.reshape(mats_here, dp_count, head_count, row_shard, head_cols)
    whole = jnp.transpose(whole, (0, 1, 3, 2, 4)).reshape(mats_here, width, head_count * head_cols)
    whole = whole / (jnp.sqrt(jnp.sum(whole * whole, axis=(1, 2), keepdims=True)) + 1e-07)
    for iteration in range(ITERS):
        whole = polish_step(whole, batch_gram(whole))
    own_part = lax.dynamic_slice(
        whole, (0, dp_index * row_shard, head_index * head_cols), (mats_here, row_shard, head_cols)
    )
    attn_new = (
        attn_weights * (1.0 - muon_rate * muon_decay)
        - muon_scale(width, head_count * head_cols) * own_part
    )
    expert_mom = momentum_decay * expert_momentum + expert_grad
    current = expert_grad + momentum_decay * expert_mom
    for iteration in range(ITERS):
        gram = lax.psum(batch_gram(current), TENSOR)
        if iteration == 0:
            factor = 1.0 / (jnp.sqrt(jnp.trace(gram, axis1=1, axis2=2)) + 1e-07)
            factor = factor[:, None, None]
            current = current * factor
            gram = gram * (factor * factor)
        current = polish_step(current, gram)
    expert_new = (
        expert_weights * (1.0 - muon_rate * muon_decay)
        - muon_scale(width, hidden_cols * tensor_count) * current
    )
    router_first_new, router_second_new, router_new = adamw_update(
        router_weight, router_first, router_second, router_sum, router_rate, router_decay
    )
    norm_first_new, norm_second_new, norm_new = adamw_update(
        norm_params, norm_first, norm_second, norm_sum, gains_rate, 0.0
    )
    return (
        block_out,
        input_grad,
        attn_mom,
        attn_new,
        router_first_new,
        router_second_new,
        router_new,
        expert_mom,
        expert_new,
        norm_first_new,
        norm_second_new,
        norm_new,
    )


def ceil_to(value, step):
    return -(-value // step) * step


def dot_exact(left, right):
    return jnp.dot(
        left, right, precision=lax.Precision.HIGH, preferred_element_type=jnp.float32
    )


def dot_low(left, right, contract=((1,), (0,))):
    return lax.dot_general(
        left, right, (contract, ((), ())), preferred_element_type=jnp.float32
    )


def block_pairs(width):
    tiles = width // TILE
    return [(i, j) for i in range(tiles) for j in range(i + 1, tiles)]


def packed_rows(width):
    tiles = width // TILE
    return (len(block_pairs(width)) + tiles // 2) * TILE + ceil_to(tiles // 2, 8)


def tile_places():
    rows = lax.broadcasted_iota(jnp.int32, (TILE, TILE), 0)
    lanes = lax.broadcasted_iota(jnp.int32, (TILE, TILE), 1)
    return rows, lanes


def pack_upper(block, width, out_ref):
    rows, lanes = tile_places()
    start = 0
    for i, j in block_pairs(width):
        out_ref[start : start + TILE, :] = block(i, j)
        start += TILE
    diagonals = []
    for i in range(0, width // TILE, 2):
        second = block(i + 1, i + 1)
        out_ref[start : start + TILE, :] = jnp.where(rows <= lanes, block(i, i), second)
        diagonals.append(
            jnp.sum(jnp.where(rows == lanes, second, 0.0), axis=0, keepdims=True)
        )
        start += TILE
    rest = out_ref.shape[0] - start - len(diagonals)
    if rest:
        diagonals.append(jnp.zeros((rest, TILE), jnp.float32))
    out_ref[start:, :] = jnp.concatenate(diagonals, axis=0)


def packed_trace(packed_ref, width):
    rows, lanes = tile_places()
    start = len(block_pairs(width)) * TILE
    total = jnp.zeros((1, 1), jnp.float32)
    pairs = width // TILE // 2
    for pair in range(pairs):
        block = packed_ref[start + pair * TILE : start + (pair + 1) * TILE, :]
        total = total + jnp.sum(jnp.where(rows == lanes, block, 0.0), keepdims=True)
    return total + jnp.sum(packed_ref[start + pairs * TILE :, :], keepdims=True)


def unpack_upper(packed_ref, out_ref, factor=None):
    rows, lanes = tile_places()
    width = out_ref.shape[0]

    def load(start, count):
        values = packed_ref[start : start + count, :]
        return values if factor is None else values * factor

    start = 0
    for i, j in block_pairs(width):
        block = load(start, TILE)
        out_ref[i * TILE : (i + 1) * TILE, j * TILE : (j + 1) * TILE] = block
        out_ref[j * TILE : (j + 1) * TILE, i * TILE : (i + 1) * TILE] = block.T
        start += TILE
    diagonals = load(start + width // 2, 8)
    for i in range(0, width // TILE, 2):
        block = load(start, TILE)
        turned = block.T
        first = jnp.where(rows <= lanes, block, turned)
        second = jnp.where(rows > lanes, block, turned)
        second = jnp.where(rows == lanes, diagonals[i // 2 : i // 2 + 1], second)
        out_ref[i * TILE : (i + 1) * TILE, i * TILE : (i + 1) * TILE] = first
        i += 1
        out_ref[i * TILE : (i + 1) * TILE, i * TILE : (i + 1) * TILE] = second
        start += TILE


def gram_packed(values, out_ref):
    rows = values.shape[0]
    half = rows // 2
    contract = (((1,), (1,)), ((), ()))
    upper = lax.dot_general(
        values[:half], values, contract,
        precision=lax.Precision.HIGH, preferred_element_type=jnp.float32,
    )
    lower = lax.dot_general(
        values[half:], values[half:], contract,
        precision=lax.Precision.HIGH, preferred_element_type=jnp.float32,
    )

    def block(i, j):
        top, left = i * TILE, j * TILE
        if top < half:
            return upper[top : top + TILE, left : left + TILE]
        return lower[top - half : top - half + TILE, left - half : left - half + TILE]

    pack_upper(block, rows, out_ref)


def own_label(experts, number):
    shard = lax.axis_index(HEADS) * lax.axis_size(DP) + lax.axis_index(DP)
    return shard * experts + number


def expert_kernel(
    first, slot_in_ref, slot_cot_ref, member_ref, router_ref, weight_ref, momentum_ref,
    momentum_out, back_out, gate_out, ahead_out, dir_out, gram_out,
):
    experts = EXPERTS // (lax.axis_size(HEADS) * lax.axis_size(DP))
    label = own_label(experts, first + pl.program_id(0))
    rows = slot_in_ref.shape[1] * slot_in_ref.shape[2]
    slot_in = slot_in_ref[0].reshape(rows, -1)
    slot_cot = slot_cot_ref[0].reshape(rows, -1).astype(jnp.float32)
    member = member_ref[0].reshape(rows, EXPERTS)
    logits = dot_low(slot_in, router_ref[...], ((1,), (1,)))
    lanes = lax.broadcasted_iota(jnp.int32, logits.shape, 1)
    own = jnp.where(lanes == label, 1.0, 0.0)
    filled = jnp.sum(member * own, axis=1, keepdims=True)
    logit_own = jnp.sum(logits * own, axis=1, keepdims=True)
    logit_other = jnp.sum(logits * (member - own), axis=1, keepdims=True)
    peak = jnp.maximum(logit_own, logit_other)
    raised = jnp.exp(logit_own - peak)
    gate = filled * raised / (raised + jnp.exp(logit_other - peak))
    up = weight_ref[0].astype(jnp.bfloat16)
    down = weight_ref[1].astype(jnp.bfloat16)
    hidden = dot_low(slot_in, up)
    cdf = 0.5 * (1.0 + lax.erf(hidden * math.sqrt(0.5)))
    active = (hidden * cdf).astype(jnp.bfloat16)
    slope = cdf + hidden * jnp.exp(-0.5 * hidden * hidden) * (1.0 / math.sqrt(2.0 * math.pi))
    expert_out = dot_low(active, down, ((1,), (1,)))
    gate_grad = jnp.sum(slot_cot * expert_out, axis=1, keepdims=True) * filled
    ahead_out[0] = (expert_out * gate).astype(jnp.bfloat16)
    out_grad = (slot_cot * gate).astype(jnp.bfloat16)
    hidden_grad = (dot_low(out_grad, down) * slope).astype(jnp.bfloat16)
    back_out[0] = dot_low(hidden_grad, up, ((1,), (1,))).astype(jnp.bfloat16)
    wide = lax.broadcasted_iota(jnp.int32, (gate_grad.shape[0], TILE), 1)
    high = gate_grad.astype(jnp.bfloat16).astype(jnp.float32)
    spread = jnp.where(wide == label, high, 0.0)
    spread = jnp.where(wide == label + EXPERTS, gate_grad - high, spread)
    gate_out[0] = spread.astype(jnp.bfloat16)
    for which, grad in enumerate(
        (
            dot_low(slot_in, hidden_grad, ((0,), (0,))),
            dot_low(out_grad, active, ((0,), (0,))),
        )
    ):
        momentum = momentum_decay * momentum_ref[which] + grad
        momentum_out[which] = momentum
        direction = grad + momentum_decay * momentum
        dir_out[which] = direction
        gram_packed(direction, gram_out.at[which])


def run_experts(first, count, slot_in, slot_cot, member, router, weights, momentum, earlier):
    _, groups, slots, width = slot_in.shape
    mats, _, hidden = weights.shape
    packed = packed_rows(width)
    shape = jax.ShapeDtypeStruct
    whole = (
        shape((mats, width, hidden), jnp.float32),
        shape((mats // 2, groups * slots, width), jnp.bfloat16),
        shape((mats // 2, groups * slots, TILE), jnp.bfloat16),
        shape((mats // 2, groups * slots, width), jnp.bfloat16),
    )
    part = (
        shape((2 * count, width, hidden), jnp.float32),
        shape((2 * count, packed, TILE), jnp.float32),
    )

    def shifted(e):
        return (first + e, 0, 0)

    def here(e):
        return (e, 0, 0)

    def slotted(e):
        return (first + e, 0, 0, 0)

    def kernel(*refs):
        expert_kernel(first, *refs[:6], *refs[6 + len(earlier) :])

    return pl.pallas_call(
        kernel,
        grid=(count,),
        in_specs=[
            pl.BlockSpec((1, groups, slots, width), slotted),
            pl.BlockSpec((1, groups, slots, width), slotted),
            pl.BlockSpec((1, groups, slots, EXPERTS), slotted),
            pl.BlockSpec(router.shape, lambda e: (0, 0)),
            pl.BlockSpec((2, width, hidden), shifted),
            pl.BlockSpec((2, width, hidden), shifted),
        ]
        + [pl.BlockSpec(memory_space=pl.ANY)] * len(earlier),
        out_specs=[
            pl.BlockSpec((2, width, hidden), shifted),
            pl.BlockSpec((1, groups * slots, width), shifted),
            pl.BlockSpec((1, groups * slots, TILE), shifted),
            pl.BlockSpec((1, groups * slots, width), shifted),
            pl.BlockSpec((2, width, hidden), here),
            pl.BlockSpec((2, packed, TILE), here),
        ],
        out_shape=whole + part,
        input_output_aliases={6 + place: place for place in range(len(earlier))},
        compiler_params=pltpu.CompilerParams(vmem_limit_bytes=VMEM_LIMIT),
        name="experts",
    )(slot_in, slot_cot, member, router, weights, momentum, *earlier)


def polish(packed_ref, out_ref, gram, poly, product, between=()):
    width = gram.shape[0]
    half = width // 2
    factor = 1.0 / (jnp.sqrt(packed_trace(packed_ref, width)) + 1e-07)
    unpack_upper(packed_ref, gram, factor * factor)

    def symmetric(left, right):
        upper = dot_exact(left[:half, :], right[...])
        corner = dot_exact(left[half:, :], right[:, half:])
        return upper, corner

    def store(ref, upper, corner):
        ref[:half, :] = upper
        ref[half:, half:] = corner
        ref[half:, :half] = upper[:, half:].T

    def eye(count):
        here = lax.broadcasted_iota(jnp.int32, (half, count), 0)
        there = lax.broadcasted_iota(jnp.int32, (half, count), 1)
        return jnp.where(here == there, coef_first, 0.0)

    def polynomial():
        upper, corner = symmetric(gram, gram)
        upper = eye(width) + coef_second * gram[:half, :] + coef_third * upper
        corner = eye(half) + coef_second * gram[half:, half:] + coef_third * corner
        return upper, corner

    def next_gram():
        store(poly, *symmetric(poly, poly))
        store(gram, *symmetric(gram, poly))

    def step(_, carry):
        store(poly, *polynomial())
        store(product, *symmetric(poly, product))
        next_gram()
        return carry

    upper, corner = polynomial()
    store(poly, upper, corner)
    store(product, upper, corner)
    next_gram()
    middle = ITERS // 2
    lax.fori_loop(1, middle, step, 0)
    for work in between:
        work()
    lax.fori_loop(middle, ITERS - 1, step, 0)
    store(poly, *polynomial())
    store(product, *symmetric(poly, product))

    def block(i, j):
        return product[i * TILE : (i + 1) * TILE, j * TILE : (j + 1) * TILE] * factor

    pack_upper(block, width, out_ref)


def neighbours(index, count):
    return [lax.rem(index + step, count) for step in range(1, count)]


def square_peers(index):
    return [3 - index, index + 1 - 2 * lax.rem(index, 2), lax.rem(index + 2, 4)]


def enter(peers):
    barrier = pltpu.get_barrier_semaphore()
    for peer in peers:
        pl.semaphore_signal(barrier, inc=1, device_id=peer, device_id_type=pl.DeviceIdType.MESH)
    pl.semaphore_wait(barrier, len(peers))


def send(source, target, send_sem, recv_sem, peer):
    copy = pltpu.make_async_remote_copy(
        src_ref=source,
        dst_ref=target,
        send_sem=send_sem,
        recv_sem=recv_sem,
        device_id=peer,
        device_id_type=pl.DeviceIdType.MESH,
    )
    copy.start()
    return copy


class Sharing:
    def __init__(self, values, out, sems):
        self.values, self.out, self.sems = values, out, sems
        self.core, self.tensor = lax.axis_index(DP), lax.axis_index(TENSOR)
        self.head, self.places = lax.axis_index(HEADS), lax.axis_size(TENSOR)
        self.along = neighbours(self.tensor, self.places)
        self.diagonal, self.beside, self.above = square_peers(self.head)
        self.origins = [self.tensor] + [
            lax.rem(self.tensor + self.places - step, self.places)
            for step in range(1, self.places)
        ]
        self.here = out.at[self.core, self.tensor, self.head]
        self.started = []

    def start(self):
        self.home = pltpu.make_async_copy(self.values, self.here, self.sems[0])
        self.home.start()
        for step, peer in enumerate(self.along):
            self.started.append(
                send(
                    self.values, self.here, self.sems[1].at[step], self.sems[2].at[step],
                    {TENSOR: peer},
                )
            )

    def to_partner(self, block, source, number):
        self.started.append(
            send(
                source, block, self.sems[5].at[number], self.sems[6].at[number],
                {DP: 1 - self.core},
            )
        )

    def to_sides(self, block, source, place):
        for step, peer in enumerate((self.beside, self.above)):
            number = 4 * place + step
            self.started.append(
                send(
                    source, block, self.sems[3].at[number], self.sems[4].at[number],
                    {HEADS: peer},
                )
            )

    def cut(self, block):
        rows = block.shape[0]
        middle = ceil_to(rows // 2, 16)
        return block.at[pl.ds(0, middle)], block.at[pl.ds(middle, rows - middle)]

    def pass_to_sides(self):
        self.to_sides(self.here, self.values, 0)
        self.to_partner(self.here, self.values, 0)
        for place in range(1, self.places):
            block = self.out.at[self.core, self.origins[place], self.head]
            wait_for(block, self.sems[2].at[place - 1])
            self.to_sides(block, block, place)
            self.to_partner(block, block, 4 * place)

    def pass_round(self):
        ways = ((self.beside, self.above), (self.above, self.beside))
        for place in range(self.places):
            for step, (peer, other) in enumerate(ways):
                block = self.out.at[self.core, self.origins[place], peer]
                wait_for(block, self.sems[4].at[4 * place + step])
                half = self.cut(block)[step]
                number = 4 * place + 2 + step
                self.started.append(
                    send(
                        half, half, self.sems[3].at[number], self.sems[4].at[number],
                        {HEADS: other},
                    )
                )
                self.to_partner(block, block, 4 * place + 1 + step)

    def own_group(self):
        for place in range(self.places):
            block = self.out.at[self.core, self.origins[place], self.diagonal]
            for step, half in enumerate(self.cut(block)):
                wait_for(half, self.sems[4].at[4 * place + 2 + step])
            self.to_partner(block, block, 4 * place + 3)
        self.home.wait()

    def other_group(self):
        corners = (self.head, self.beside, self.above, self.diagonal)
        for place in range(self.places):
            for step, peer in enumerate(corners):
                block = self.out.at[1 - self.core, self.origins[place], peer]
                wait_for(block, self.sems[6].at[4 * place + step])

    def finish(self):
        for copy in self.started:
            copy.wait_send()


def sharing_sems(places, corners):
    dma = pltpu.SemaphoreType.DMA
    blocks = places * corners
    return [dma(()), dma((places - 1,)), dma((places - 1,))] + [dma((blocks,))] * 4


def wait_for(block, sem):
    pltpu.make_async_copy(block, block, sem).wait()


class LineReduce:
    def __init__(self, parts, received, total, sems, ahead=None):
        self.parts, self.received, self.total = parts, received, total
        self.ahead = ahead
        self.send_sem, self.recv_sem = sems
        self.place = lax.axis_index(TENSOR)
        self.far = lax.axis_size(TENSOR) - 1
        self.ways = ((self.place, self.place + 1), (self.far - self.place, self.place - 1))

    def copy(self, way, slot, source):
        return pltpu.make_async_remote_copy(
            src_ref=source,
            dst_ref=self.received.at[way, slot],
            send_sem=self.send_sem.at[way, slot],
            recv_sem=self.recv_sem.at[way, slot],
            device_id={TENSOR: self.ways[way][1]},
            device_id_type=pl.DeviceIdType.MESH,
        )

    def slot(self, slot):
        for way, (behind, _) in enumerate(self.ways):
            owner = self.far - slot + behind if way == 0 else slot - behind

            @pl.when(behind == 0)
            def _():
                self.copy(way, slot, self.parts.at[owner]).start()

            if slot:

                @pl.when((behind > 0) & (behind <= slot))
                def _():
                    block = self.received.at[way, slot - 1]
                    if slot == 1 and self.ahead is not None:
                        block[...] = self.ahead[way][...] + self.parts[owner]
                    else:
                        wait_for(block, self.recv_sem.at[way, slot - 1])
                        block[...] = block[...] + self.parts[owner]
                    self.copy(way, slot, block).start()

    def final(self):
        self.total[...] = self.parts[self.place]
        for way, (behind, _) in enumerate(self.ways):

            @pl.when(behind > 0)
            def _():
                block = self.received.at[way, self.far - 1]
                wait_for(block, self.recv_sem.at[way, self.far - 1])
                self.total[...] = self.total[...] + block[...]

    def finish(self):
        for way, (behind, _) in enumerate(self.ways):
            for slot in range(0 if self.ahead is None else 1, self.far):

                @pl.when(behind <= slot)
                def _():
                    self.copy(way, slot, self.parts.at[0]).wait_send()


class LineShare:
    def __init__(self, own, out, sems):
        self.own, self.out = own, out
        self.send_sem, self.recv_sem, home_sem = sems
        self.place = lax.axis_index(TENSOR)
        self.home = pltpu.make_async_copy(own, out.at[self.place], home_sem)
        self.far = lax.axis_size(TENSOR) - 1
        self.ways = (
            (self.place, self.place + 1, -1),
            (self.far - self.place, self.place - 1, 1),
        )

    def copy(self, way, slot):
        block = self.out.at[self.place + self.ways[way][2] * slot]
        return pltpu.make_async_remote_copy(
            src_ref=block if slot else self.own,
            dst_ref=block,
            send_sem=self.send_sem.at[way, slot],
            recv_sem=self.recv_sem.at[way, slot],
            device_id={TENSOR: self.ways[way][1]},
            device_id_type=pl.DeviceIdType.MESH,
        )

    def slot(self, slot):
        if slot == 0:
            self.home.start()
        for way, (behind, _, step) in enumerate(self.ways):
            if slot:

                @pl.when(behind >= slot)
                def _():
                    block = self.out.at[self.place + step * slot]
                    wait_for(block, self.recv_sem.at[way, slot - 1])

            if slot < self.far:

                @pl.when((behind >= slot) & (behind < self.far))
                def _():
                    self.copy(way, slot).start()

    def finish(self):
        self.slot(self.far)
        self.home.wait()
        for way, (behind, _, _) in enumerate(self.ways):
            for slot in range(self.far):

                @pl.when((behind >= slot) & (behind < self.far))
                def _():
                    self.copy(way, slot).wait_send()


def line_sems(places):
    dma = pltpu.SemaphoreType.DMA
    return [dma((2, places - 1)), dma((2, places - 1))]


class Exchange:
    def __init__(self, grads, momentum, sums, whole, scratch, sems):
        self.grads, self.momentum, self.sums, self.whole = grads, momentum, sums, whole
        (
            self.from_core, self.merged, self.low, self.from_z, self.from_z_small, self.direction,
        ) = scratch
        (
            self.own_sem, self.core_send, self.core_recv, self.z_send, self.z_recv,
            self.xy_send, self.xy_recv, self.pass_send, self.pass_recv,
        ) = sems
        self.core, self.tensor = lax.axis_index(DP), lax.axis_index(TENSOR)
        self.head, self.places = lax.axis_index(HEADS), lax.axis_size(TENSOR)
        self.along = neighbours(self.tensor, self.places)
        self.across = square_peers(self.head)
        self.rows = momentum.shape[0]
        self.started = []

    def send(self, *args):
        self.started.append(send(*args))

    def start(self):
        self.send(
            self.grads.at[1 - self.core], self.from_core, self.core_send, self.core_recv,
            {DP: 1 - self.core},
        )

    def along_tensor(self):
        rows = self.rows
        wait_for(self.from_core, self.core_recv)
        for place in range(self.places):
            both = self.grads[self.core, place] + self.from_core[place]
            self.merged[place] = both
            self.low[place] = both[:rows].astype(self.low.dtype)
        others = len(self.along)
        for step, peer in enumerate(self.along):
            self.send(
                self.low.at[peer], self.from_z.at[step], self.z_send.at[step],
                self.z_recv.at[step], {TENSOR: peer},
            )
            self.send(
                self.merged.at[peer, pl.ds(rows, self.from_z_small.shape[1])],
                self.from_z_small.at[step], self.z_send.at[others + step],
                self.z_recv.at[others + step], {TENSOR: peer},
            )

    def share(self):
        rows, others = self.rows, len(self.along)
        grad = self.merged[self.tensor, :rows, :]
        small = self.merged[self.tensor, rows:, :]
        for step in range(others):
            wait_for(self.from_z.at[step], self.z_recv.at[step])
            grad = grad + self.from_z[step].astype(jnp.float32)
            wait_for(self.from_z_small.at[step], self.z_recv.at[others + step])
            small = small + self.from_z_small[step]
        self.sums[:rows, :] = grad
        self.sums[rows:, :] = small
        momentum = momentum_decay * self.momentum[...] + grad
        self.direction[...] = grad + momentum_decay * momentum
        here = self.whole.at[self.core, self.head]
        self.home = pltpu.make_async_copy(self.direction, here, self.own_sem)
        self.home.start()
        for step, peer in enumerate(self.across):
            self.send(
                self.direction, here, self.xy_send.at[step], self.xy_recv.at[step],
                {HEADS: peer},
            )
        self.send(
            self.direction, here, self.pass_send.at[0], self.pass_recv.at[0],
            {DP: 1 - self.core},
        )

    def finish(self):
        for step, peer in enumerate(self.across):
            block = self.whole.at[self.core, peer]
            wait_for(block, self.xy_recv.at[step])
            self.send(
                block, block, self.pass_send.at[step + 1], self.pass_recv.at[step + 1],
                {DP: 1 - self.core},
            )
        for step, peer in enumerate([self.head] + self.across):
            wait_for(self.whole.at[1 - self.core, peer], self.pass_recv.at[step])
        self.home.wait()
        for copy in self.started:
            copy.wait_send()


def exchange_scratch(places, heads, rows, momentum):
    f32, bf16 = jnp.float32, jnp.bfloat16
    dma = pltpu.SemaphoreType.DMA
    scratch = [
        pltpu.VMEM((places, rows, TILE), f32),
        pltpu.VMEM((places, rows, TILE), f32),
        pltpu.VMEM((places,) + momentum, bf16),
        pltpu.VMEM((places - 1,) + momentum, bf16),
        pltpu.VMEM((places - 1, rows - momentum[0], TILE), f32),
        pltpu.VMEM(momentum, f32),
    ]
    sems = [
        dma(()),
        dma(()),
        dma(()),
        dma((2 * (places - 1),)),
        dma((2 * (places - 1),)),
        dma((heads - 1,)),
        dma((heads - 1,)),
        dma((heads,)),
        dma((heads,)),
    ]
    return scratch, sems


class Combining:
    def __init__(self, payloads, out, exact_out, scratch, sems):
        self.payloads, self.out, self.exact_out = payloads, out, exact_out
        self.widths = [payload.shape[3] for payload in payloads]
        (
            self.stage, self.own, self.from_core, self.from_side, self.relay,
            self.from_next, self.low, self.from_z, self.done, *self.exact,
        ) = scratch
        (
            self.home_sem, self.core_send, self.core_recv, self.xy_send, self.xy_recv,
            self.z_send, self.z_recv, self.back_send, self.back_recv,
        ) = sems
        self.core, self.tensor = lax.axis_index(DP), lax.axis_index(TENSOR)
        self.head, self.places = lax.axis_index(HEADS), lax.axis_size(TENSOR)
        self.across = square_peers(self.head)
        self.order = neighbours(self.tensor, self.places) + [self.tensor]
        self.quarter = self.done.shape[0]
        self.started, self.homes, self.to_core = [], [], []
        self.result = None

    def send(self, *args):
        self.started.append(send(*args))

    def write(self, ref, number, pick, group):
        start = 0
        rows = pick.shape[0]
        for payload, width in zip(self.payloads, self.widths):
            slots = payload[:, group].reshape(-1, width)
            ref[number, :rows, start : start + width] = dot_low(pick, slots).astype(ref.dtype)
            start += width

    def spread(self, number, picks):
        self.write(self.stage, number, picks[1], 1 - self.core)
        self.to_core.append(
            send(
                self.stage.at[number], self.from_core.at[number], self.core_send.at[number],
                self.core_recv.at[number], {DP: 1 - self.core},
            )
        )
        self.write(self.own, number, picks[0], self.core)

    def sides(self, number):
        _, beside, above = self.across
        return (beside, above) if number % 2 == 0 else (above, beside)

    def rows(self, corner):
        return pl.ds(pl.multiple_of(corner * self.quarter, 16), self.quarter)

    def exchange(self, number):
        wait_for(self.from_core.at[number], self.core_recv.at[number])
        rows = self.from_core.shape[1]
        both = self.own[number, :rows] + self.from_core[number].astype(jnp.float32)
        self.own[number, :rows] = both
        self.to_core[number].wait_send()
        self.stage[number] = both.astype(jnp.bfloat16)
        side = self.sides(number)[0]
        for step, corner in enumerate((self.across[0], side)):
            place = 3 * number + step
            self.send(
                self.stage.at[number, self.rows(corner)], self.from_side.at[number, step],
                self.xy_send.at[place], self.xy_recv.at[place], {HEADS: side},
            )

    def pass_on(self, number):
        following = self.sides(number)[1]
        place = 3 * number
        wait_for(self.from_side.at[number, 0], self.xy_recv.at[place])
        both = self.own[number, self.rows(following), :]
        both = both + self.from_side[number, 0].astype(jnp.float32)
        self.relay[number] = both.astype(jnp.bfloat16)
        self.send(
            self.relay.at[number], self.from_next.at[number], self.xy_send.at[place + 2],
            self.xy_recv.at[place + 2], {HEADS: following},
        )

    def reduce(self, number):
        wait_for(self.from_side.at[number, 1], self.xy_recv.at[3 * number + 1])
        wait_for(self.from_next.at[number], self.xy_recv.at[3 * number + 2])
        both = self.own[number, self.rows(self.head), :]
        both = both + self.from_side[number, 1].astype(jnp.float32)
        both = both + self.from_next[number].astype(jnp.float32)
        if number == self.places - 1:
            self.result = both
            return
        self.low[number] = both.astype(jnp.bfloat16)
        self.send(
            self.low.at[number], self.from_z.at[number], self.z_send.at[number],
            self.z_recv.at[number], {TENSOR: self.order[number]},
        )

    def share(self):
        result = self.result
        for number in range(self.places - 1):
            wait_for(self.from_z.at[number], self.z_recv.at[number])
            result = result + self.from_z[number].astype(jnp.float32)
        main = self.done.shape[1]
        self.done[...] = result[:, :main].astype(jnp.bfloat16)
        parts = [(self.done, self.out)]
        if self.exact:
            self.exact[0][...] = result[:, main:]
            parts.append((self.exact[0], self.exact_out))
        for which, (source, out) in enumerate(parts):
            here = out.at[self.head]
            home = pltpu.make_async_copy(source, here, self.home_sem.at[which])
            home.start()
            self.homes.append(home)
            for step, peer in enumerate(self.across):
                number = which * len(self.across) + step
                self.send(
                    source, here, self.back_send.at[number], self.back_recv.at[number],
                    {HEADS: peer},
                )

    def finish(self):
        outs = [self.out] + ([self.exact_out] if self.exact else [])
        for which, out in enumerate(outs):
            for step, peer in enumerate(self.across):
                number = which * len(self.across) + step
                wait_for(out.at[peer], self.back_recv.at[number])
        for home in self.homes:
            home.wait()
        for copy in self.started:
            copy.wait_send()


def combining_scratch(places, rows, quarter, widths, exact, room=0):
    wide = sum(widths)
    main = wide - (widths[-1] if exact else 0)
    f32, bf16 = jnp.float32, jnp.bfloat16
    dma = pltpu.SemaphoreType.DMA
    scratch = [
        pltpu.VMEM((places, rows, wide), bf16),
        pltpu.VMEM((places, max(rows, room), wide), f32),
        pltpu.VMEM((places, rows, wide), bf16),
        pltpu.VMEM((places, 2, quarter, wide), bf16),
        pltpu.VMEM((places, quarter, wide), bf16),
        pltpu.VMEM((places, quarter, wide), bf16),
        pltpu.VMEM((places - 1, quarter, wide), bf16),
        pltpu.VMEM((places - 1, quarter, wide), bf16),
        pltpu.VMEM((quarter, main), bf16),
    ]
    if exact:
        scratch.append(pltpu.VMEM((quarter, wide - main), f32))
    sems = [
        dma((2,)),
        dma((places,)),
        dma((places,)),
        dma((places * 3,)),
        dma((places * 3,)),
        dma((places - 1,)),
        dma((places - 1,)),
        dma((6,)),
        dma((6,)),
    ]
    return scratch, sems


def halves(values):
    lanes = lax.broadcasted_iota(jnp.int32, values.shape, 1)
    zero = jnp.zeros_like(values)
    return jnp.where(lanes < HEAD_DIM, values, zero), jnp.where(lanes < HEAD_DIM, zero, values)


def join_heads(first, second):
    lanes = lax.broadcasted_iota(jnp.int32, first.shape, 1)
    return jnp.where(lanes < HEAD_DIM, first, second)


def probabilities(query, keys):
    scores = dot_low(query, keys, ((1,), (1,))) * HEAD_DIM ** (-0.5)
    lanes = lax.broadcasted_iota(jnp.int32, scores.shape, 1)
    scores = jnp.where(lanes < SEQ, scores, -1e30)
    raised = jnp.exp(scores - jnp.max(scores, axis=1, keepdims=True))
    return raised / jnp.sum(raised, axis=1, keepdims=True)


def wide_rows(low_ref, first_row, rows):
    cores, places, _, _, tile = low_ref.shape
    shards = [low_ref[c, t, 0, first_row : first_row + rows, :] for c in range(cores) for t in range(places)]
    shards = [shard.astype(jnp.float32) for shard in shards]
    lanes = lax.broadcasted_iota(jnp.int32, (rows, tile), 1)
    tiles = []
    for left, right in zip(shards[::2], shards[1::2]):
        tiles.append(jnp.where(lanes < tile // 2, left, pltpu.roll(right, tile // 2, 1)))
    return jnp.concatenate(tiles, axis=1)


def front_kernel(slots, flat_ref, images_ref, cot_ref, ids_ref, *refs):
    outs, refs = refs[:11], refs[11:]
    results, refs = refs[:11], refs[11:]
    (
        qkv_out, mixed_out, first_out, normed_out, router_out, gains_out, weights_out,
        slot_in_out, slot_cot_out, member_out, column_out,
    ) = results
    low_ref, all_normed, all_cot, all_ids, ranks, picks, members, normed, mixed, *sems = refs
    leaving = []

    def leave(*numbers):
        for number in numbers:
            copy = pltpu.make_async_copy(results[number], outs[number], sems[22].at[number])
            copy.start()
            leaving.append(copy)

    images, padded, width = images_ref.shape
    cores, places, heads, _, tile = low_ref.shape
    f32, bf16 = jnp.float32, jnp.bfloat16
    core, head_index = lax.axis_index(DP), lax.axis_index(HEADS)
    block = width // cores
    quarter = cot_ref.shape[1]
    per = heads // images
    own_normed = normed_out.at[
        lax.div(head_index, per),
        pl.ds(pl.multiple_of(lax.rem(head_index, per) * quarter, 16), quarter),
    ]
    sharing_low = Sharing(flat_ref, low_ref, sems[:7])
    sharing_cot = Sharing(cot_ref.at[head_index], all_cot, sems[7:14])
    sharing_normed = Sharing(own_normed, all_normed, sems[14:21])
    ids_sems = sems[21]
    enter(
        [{TENSOR: peer} for peer in sharing_low.along]
        + [{HEADS: sharing_low.beside}, {HEADS: sharing_low.above}, {DP: 1 - core}]
    )
    sharing_low.start()
    ids_home = pltpu.make_async_copy(ids_ref, all_ids.at[core], ids_sems.at[0])
    ids_home.start()
    ids_copy = send(
        ids_ref, all_ids.at[core], ids_sems.at[1], ids_sems.at[2], {DP: 1 - core}
    )
    sharing_low.pass_to_sides()
    sharing_cot.start()
    ids_home.wait()
    wait_for(all_ids.at[1 - core], ids_sems.at[2])
    slot_places(slots, all_ids, ranks, column_out)
    sharing_low.pass_round()
    experts = slot_in_out.shape[0]
    groups = cores
    for group in range(groups):
        for e in range(experts):
            rank = ranks[e * groups + group : e * groups + group + 1, :]
            place = lax.broadcasted_iota(jnp.int32, (slots, rank.shape[1]), 0)
            picks[group, e * slots : (e + 1) * slots, :] = jnp.where(
                rank == place, 1.0, 0.0
            ).astype(bf16)
        lanes = lax.broadcasted_iota(jnp.int32, members.shape[1:], 1)
        start = (groups + group) * TOP
        hit = lanes == column_out[:, start : start + 1]
        for k in range(1, TOP):
            hit = hit | (lanes == column_out[:, start + k : start + k + 1])
        members[group] = jnp.where(hit, 1.0, 0.0).astype(bf16)
    for group in range(groups):
        part = dot_low(picks[group], members[group])
        for e in range(experts):
            member_out[e, group] = part[e * slots : (e + 1) * slots]
    leave(9, 10)
    sharing_cot.pass_to_sides()
    sharing_low.own_group()
    sharing_low.other_group()

    for matrix in range(4):
        for c in range(cores):
            for head in range(heads):
                start = matrix * width + head * tile
                weights_out[c * block : (c + 1) * block, start : start + tile] = low_ref[
                    c, matrix, head, :block, :
                ]
    small = wide_rows(low_ref, block, ceil_to(EXPERTS + 4, 16))
    router_out[...] = small[:EXPERTS].astype(bf16)
    gains = small[EXPERTS : EXPERTS + 8]
    gains_out[...] = gains
    leave(4, 5, 6)
    def attend(image):
        tokens = images_ref[image].astype(f32)
        here, _, _ = norm_forward(tokens, gains[0:1], gains[1:2])
        normed[...] = here.astype(bf16)
        for matrix in range(3):
            part = dot_low(normed[...], weights_out[:, matrix * width : (matrix + 1) * width])
            part = part.astype(bf16)
            for head in range(heads):
                qkv_out[matrix, head, image] = part[:, head * tile : (head + 1) * tile]
        for head in range(heads):
            keys = qkv_out[1, head, image]
            total = None
            for query, value in zip(
                halves(qkv_out[0, head, image]), halves(qkv_out[2, head, image])
            ):
                probs = probabilities(query, keys).astype(bf16)
                part = dot_low(probs, value)
                total = part if total is None else total + part
            mixed_out[head, image] = total.astype(bf16)
            mixed[:, head * tile : (head + 1) * tile] = total.astype(bf16)
        attended = dot_low(mixed[...], weights_out[:, 3 * width :], ((1,), (1,)))
        first = tokens + attended
        first_out[image] = first
        here, _, _ = norm_forward(first, gains[2:3], gains[3:4])
        normed_out[image] = here.astype(bf16)

    own_image = lax.div(head_index, per)
    attend(own_image)
    sharing_normed.start()
    sharing_cot.pass_round()
    for step in range(1, images):
        attend(lax.rem(own_image + step, images))

    def dispatch(source, out, group):
        rows = places * heads * quarter
        part = dot_low(picks[group], source[group].reshape(rows, width)).astype(bf16)
        for e in range(experts):
            out[e, group] = part[e * slots : (e + 1) * slots]

    sharing_normed.pass_to_sides()
    leave(0, 1, 2, 3)
    sharing_cot.own_group()
    sharing_normed.pass_round()
    dispatch(all_cot, slot_cot_out, core)
    sharing_cot.other_group()
    dispatch(all_cot, slot_cot_out, 1 - core)
    leave(8)
    sharing_normed.own_group()
    dispatch(all_normed, slot_in_out, core)
    sharing_normed.other_group()
    dispatch(all_normed, slot_in_out, 1 - core)
    leave(7)
    for copy in leaving:
        copy.wait()
    ids_copy.wait_send()
    for sharing in (sharing_low, sharing_cot, sharing_normed):
        sharing.finish()


def run_front(flat, images, cot, ids, experts, slots, number):
    count, padded, width = images.shape
    groups, heads = lax.axis_size(DP), lax.axis_size(HEADS)
    places, _, rows = ids.shape
    tokens = places * rows
    quarter = cot.shape[1]
    f32, bf16 = jnp.float32, jnp.bfloat16
    shape = jax.ShapeDtypeStruct
    dma = pltpu.SemaphoreType.DMA
    vmem, anywhere = pl.BlockSpec(memory_space=pltpu.VMEM), pl.BlockSpec(memory_space=pl.ANY)
    results = [
        shape((3, heads, count, padded, TILE), bf16),
        shape((heads, count, padded, TILE), bf16),
        shape((count, padded, width), f32),
        shape((count, padded, width), bf16),
        shape((EXPERTS, width), bf16),
        shape((8, width), f32),
        shape((width, 4 * width), bf16),
        shape((experts, groups, slots, width), bf16),
        shape((experts, groups, slots, width), bf16),
        shape((experts, groups, slots, EXPERTS), f32),
        shape((tokens, 2 * groups * TOP), jnp.int32),
    ]
    return pl.pallas_call(
        functools.partial(front_kernel, slots),
        in_specs=[anywhere, vmem, anywhere, anywhere],
        out_specs=[anywhere] * 11,
        out_shape=results,
        scratch_shapes=[pltpu.VMEM(result.shape, result.dtype) for result in results]
        + [
            pltpu.VMEM((groups, places, heads) + flat.shape, bf16),
            pltpu.VMEM((groups, places, heads, quarter, width), bf16),
            pltpu.VMEM((groups, places, heads, quarter, width), bf16),
            pltpu.VMEM((groups,) + ids.shape, jnp.int32),
            pltpu.VMEM((experts * groups, tokens), jnp.int32),
            pltpu.VMEM((groups, experts * slots, tokens), bf16),
            pltpu.VMEM((groups, tokens, EXPERTS), bf16),
            pltpu.VMEM((padded, width), bf16),
            pltpu.VMEM((padded, width), bf16),
        ]
        + sharing_sems(places, heads) * 3
        + [dma((3,)), dma((11,))],
        compiler_params=pltpu.CompilerParams(
            collective_id=number, has_side_effects=True, vmem_limit_bytes=VMEM_LIMIT
        ),
        name="front",
    )(flat, images, cot, ids)


def attend_back(
    back_ref, gate_ref, cot_ref, columns_ref, images_ref, first_ref, normed_b_ref, mixed_ref,
    qkv_ref, router_ref, gains_ref, weights_ref, input_out, grads_out,
    normed_a, branch, mixed_grad, qkv_grad, own_grad, between,
):
    images, padded, width = images_ref.shape
    heads, tile = mixed_ref.shape[0], mixed_ref.shape[3]
    cores = grads_out.shape[0]
    f32, bf16 = jnp.float32, jnp.bfloat16
    core = lax.axis_index(DP)
    head_index = lax.axis_index(HEADS)
    tensor = lax.axis_index(TENSOR)
    block = width // cores
    gains = gains_ref[...]
    router = router_ref[...]
    router_grad = jnp.zeros((EXPERTS, width), f32)
    sums = [jnp.zeros((1, width), f32) for _ in range(4)]
    for image in range(images):
        per = back_ref.shape[0] // images
        quarters = range(image * per, (image + 1) * per)
        back = jnp.concatenate([back_ref[q] for q in quarters], axis=0).astype(f32)
        parts = jnp.concatenate([gate_ref[q] for q in quarters], axis=0)
        columns = columns_ref[tensor, image * padded : (image + 1) * padded, :]
        ids = [
            jnp.where(core == 0, columns[:, 4 + k : 5 + k], columns[:, 6 + k : 7 + k])
            for k in range(TOP)
        ]
        lanes = lax.broadcasted_iota(jnp.int32, (padded, EXPERTS), 1)
        chosen = jnp.where((lanes == ids[0]) | (lanes == ids[1]), 1.0, 0.0)
        normed_b = normed_b_ref[image]
        logits = dot_low(normed_b, router, ((1,), (1,)))
        peak = jnp.max(jnp.where(chosen > 0, logits, -1e30), axis=1, keepdims=True)
        raised = jnp.exp(jnp.where(chosen > 0, logits - peak, -1e30))
        any_chosen = jnp.max(chosen, axis=1, keepdims=True)
        gates = raised / (jnp.sum(raised, axis=1, keepdims=True) + (1.0 - any_chosen))
        gate_grad = (parts + pltpu.roll(parts, tile - EXPERTS, 1))[:, :EXPERTS]
        blend = jnp.sum(gates * gate_grad, axis=1, keepdims=True)
        logit_grad = (gates * (gate_grad - blend)).astype(bf16)
        normed_grad = back + dot_low(logit_grad, router)
        router_grad = router_grad + dot_low(logit_grad, normed_b, ((0,), (0,)))
        _, scaled, inverse = norm_forward(first_ref[image], gains[2:3], gains[3:4])
        sums[2] = sums[2] + jnp.sum(normed_grad * scaled, axis=0, keepdims=True)
        sums[3] = sums[3] + jnp.sum(normed_grad, axis=0, keepdims=True)
        first_grad = cot_ref[image].astype(f32) + norm_backward(
            normed_grad, scaled, inverse, gains[2:3]
        )
        input_out[image] = first_grad
        branch[image] = first_grad.astype(bf16)
        mixed_grad[...] = dot_low(branch[image], weights_ref[:, 3 * width :]).astype(bf16)
        for head in range(heads):
            query, keys = qkv_ref[0, head, image], qkv_ref[1, head, image]
            values = qkv_ref[2, head, image]
            out_grad = mixed_grad[:, head * tile : (head + 1) * tile]
            query_grads, key_grads, value_grad = [], [], None
            for query_half, grad_half in zip(halves(query), halves(out_grad)):
                probs = probabilities(query_half, keys)
                prob_grad = dot_low(grad_half, values, ((1,), (1,)))
                part = dot_low(probs.astype(bf16), grad_half, ((0,), (0,)))
                value_grad = part if value_grad is None else value_grad + part
                score_grad = (
                    probs * (prob_grad - jnp.sum(probs * prob_grad, axis=1, keepdims=True))
                ).astype(bf16)
                query_grads.append(dot_low(score_grad, keys))
                key_grads.append(dot_low(score_grad, query, ((0,), (0,))))
            scale = HEAD_DIM ** (-0.5)
            for matrix, grad in enumerate(
                (join_heads(*query_grads) * scale, join_heads(*key_grads) * scale, value_grad)
            ):
                grad = grad.astype(bf16)
                start = matrix * width + head * tile
                qkv_grad[:, start : start + tile] = grad
                own_grad[matrix, head, image * padded : (image + 1) * padded, :] = grad
            for work in between.get((image, head), ()):
                work()
        normed_grad = dot_low(qkv_grad[...], weights_ref[:, : 3 * width], ((1,), (1,)))
        here, scaled, inverse = norm_forward(
            images_ref[image].astype(f32), gains[0:1], gains[1:2]
        )
        normed_a[image] = here.astype(bf16)
        sums[0] = sums[0] + jnp.sum(normed_grad * scaled, axis=0, keepdims=True)
        sums[1] = sums[1] + jnp.sum(normed_grad, axis=0, keepdims=True)
        input_out[image] = input_out[image] + norm_backward(
            normed_grad, scaled, inverse, gains[0:1]
        )
    rows = images * padded
    left = normed_a[...].reshape(rows, width)
    for matrix in range(4):
        if matrix < 3:
            grad = dot_low(left, own_grad[matrix, head_index], ((0,), (0,)))
        else:
            own_mixed = mixed_ref[head_index].reshape(rows, tile)
            grad = dot_low(branch[...].reshape(rows, width), own_mixed, ((0,), (0,)))
        for c in range(cores):
            grads_out[c, matrix, :block, :] = grad[c * block : (c + 1) * block]
    pad = grads_out.shape[2] - block - EXPERTS - 4
    small = jnp.concatenate([router_grad] + sums + [jnp.zeros((pad, width), f32)], axis=0)
    places = grads_out.shape[1]
    for c in range(cores):
        for t in range(places):
            shard = c * places + t
            piece = small[:, shard // 2 * tile : (shard // 2 + 1) * tile]
            if shard % 2:
                piece = pltpu.roll(piece, tile // 2, 1)
            grads_out[c, t, block:, :] = piece


def attn_polish(whole_ref, weights_ref, out_ref, values, gram, poly, between=()):
    cores, heads, block, tile = whole_ref.shape
    width = values.shape[0]
    half = width // 2
    core, head_index = lax.axis_index(DP), lax.axis_index(HEADS)
    squares = jnp.zeros((1, 1), jnp.float32)
    for c in range(cores):
        for h in range(heads):
            part = whole_ref[c, h]
            squares = squares + jnp.sum(part * part, keepdims=True)
    factor = 1.0 / (jnp.sqrt(squares) + 1e-07)
    for c in range(cores):
        for h in range(heads):
            values[c * block : (c + 1) * block, h * tile : (h + 1) * tile] = whole_ref[c, h] * factor

    def store(ref, upper, corner):
        ref[:half, :] = upper
        ref[half:, half:] = corner
        ref[half:, :half] = upper[:, half:].T

    def product(left, right, contract):
        return lax.dot_general(
            left, right, (contract, ((), ())),
            precision=lax.Precision.HIGH, preferred_element_type=jnp.float32,
        )

    for step in range(ITERS):
        across = ((1,), (1,))
        store(
            gram,
            product(values[:half, :], values[...], across),
            product(values[half:, :], values[half:, :], across),
        )
        along = ((1,), (0,))
        upper = product(gram[:half, :], gram[...], along)
        corner = product(gram[half:, :], gram[:, half:], along)
        store(
            poly,
            coef_second * gram[:half, :] + coef_third * upper,
            coef_second * gram[half:, half:] + coef_third * corner,
        )
        values[...] = coef_first * values[...] + product(poly[...], values[...], along)
        if step == ITERS // 2:
            for work in between:
                work()
    scale = muon_scale(width, heads * tile)
    for c in range(cores):
        for h in range(heads):

            @pl.when((core == c) & (head_index == h))
            def _():
                own = values[c * block : (c + 1) * block, h * tile : (h + 1) * tile]
                out_ref[...] = weights_ref[...] * (1.0 - muon_rate * muon_decay) - scale * own


def back_kernel(
    scale, gram_first, ahead_right, ahead_left, columns, back, gates, router, gains, momentum,
    attn_weights, *refs,
):
    late, refs = refs[:9], refs[9:]
    (
        directions, expert_weights, ahead_out, input_out, sums_out, attn_out, share_first,
        share_second, expert_out, *refs,
    ) = refs
    loaded, refs = refs[:9], refs[9:]
    ahead, gram_second, weights, qkv, first, cot, images, normed_b, mixed = loaded
    (
        back_total, gates_total, received_first, received_second, total_first, total_second,
        polish_gram, polish_poly, polish_product, grads, normed_a, branch, mixed_grad, qkv_grad,
        own_grad, whole, load_sem, apply_sem, *refs,
    ) = refs
    loading = [
        pltpu.make_async_copy(source, target, load_sem.at[number])
        for number, (source, target) in enumerate(zip(late, loaded))
    ]
    for copy in loading:
        copy.start()
    refs = list(refs)

    def take(count):
        taken = refs[:count]
        del refs[:count]
        return taken

    combine_back = Combining((back, gates), back_total, gates_total, take(10), take(9))
    combine_ahead = Combining((ahead,), ahead_out, None, take(9), take(9))
    reduce_first = LineReduce(
        gram_first, received_first, total_first, take(2), (ahead_right, ahead_left)
    )
    reduce_second = LineReduce(gram_second, received_second, total_second, take(2))
    line_first = LineShare(total_first, share_first, take(3))
    line_second = LineShare(total_second, share_second, take(3))
    exchange = Exchange(grads, momentum, sums_out, whole, take(6), take(9))
    core = lax.axis_index(DP)
    places, rows, _ = columns.shape
    experts, _, slots, _ = back.shape
    lanes_total = experts * slots
    enter(
        [{TENSOR: peer} for peer in combine_back.order[:-1]]
        + [{HEADS: peer} for peer in combine_back.across]
        + [{DP: 1 - core}]
    )

    def pick(group, place):
        table = columns[place]
        lanes = lax.broadcasted_iota(jnp.int32, (rows, lanes_total), 1)
        hit = None
        for k in range(TOP):
            code = jnp.where(group == 0, table[:, k : k + 1], table[:, TOP + k : TOP + k + 1])
            here = code == lanes
            hit = here if hit is None else hit | here
        return jnp.where(hit, 1.0, 0.0).astype(jnp.bfloat16)

    reduce_first.slot(1)
    last = places - 1
    for number, place in enumerate(combine_back.order):
        combine_back.spread(number, (pick(core, place), pick(1 - core, place)))
        if number > 0:
            combine_back.exchange(number - 1)
        if number > 1:
            combine_back.pass_on(number - 2)
    combine_back.exchange(last)
    reduce_first.slot(2)
    loading[0].wait()
    for number, place in enumerate(combine_back.order):
        combine_ahead.spread(number, (pick(core, place), pick(1 - core, place)))
        if number >= 2:
            combine_back.pass_on(last - 3 + number)
    for copy in loading[1:]:
        copy.wait()
    reduce_first.final()
    reduce_second.slot(0)
    polish_refs = (polish_gram, polish_poly, polish_product)
    polish(
        total_first, total_first, *polish_refs,
        between=(lambda: [combine_back.reduce(number) for number in range(places)],),
    )
    line_first.slot(0)
    combine_back.share()
    reduce_second.slot(1)
    combine_back.finish()
    between = {
        (0, 0): (lambda: [combine_ahead.exchange(number) for number in range(places)],),
        (0, 3): (lambda: line_first.slot(1),),
        (1, 0): (lambda: [combine_ahead.pass_on(number) for number in range(places)],),
        (1, 2): (lambda: reduce_second.slot(2),),
    }
    attend_back(
        back_total, gates_total, cot, columns, images, first, normed_b, mixed, qkv, router, gains,
        weights, input_out, grads, normed_a, branch, mixed_grad, qkv_grad, own_grad, between,
    )
    exchange.start()
    line_first.slot(2)
    for number in range(places):
        combine_ahead.reduce(number)
    exchange.along_tensor()
    reduce_second.final()
    packed_bufs = [received_first.at[0, 0], received_first.at[0, 1]]
    own = combine_back.own
    width = polish_gram.shape[0]
    views = [own.at[k, pl.ds(0, width), pl.ds(0, width)] for k in range(4)]
    fetched, stored = {}, {}

    def fetch(m):
        k = m % 2
        fetched[m] = [
            pltpu.make_async_copy(source, target, apply_sem.at[3 * k + which])
            for which, (source, target) in enumerate(
                (
                    (share_first.at[m], packed_bufs[k]),
                    (directions.at[m], views[k]),
                    (expert_weights.at[m], views[2 + k]),
                )
            )
        ]
        for copy in fetched[m]:
            copy.start()

    def new_matrix(m):
        k = m % 2
        for copy in fetched[m]:
            copy.wait()
        unpack_upper(packed_bufs[k], polish_poly)
        ortho = dot_exact(polish_poly[...], views[k][...])
        views[2 + k][...] = views[2 + k][...] * (1.0 - muon_rate * muon_decay) - scale * ortho
        stored[m] = pltpu.make_async_copy(views[2 + k], expert_out.at[m], apply_sem.at[6 + k])
        stored[m].start()

    def prepare():
        line_first.finish()
        reduce_first.finish()
        fetch(0)
        fetch(1)

    polish(total_second, total_second, *polish_refs, between=(prepare,))
    line_second.slot(0)
    for m in range(places):
        new_matrix(m)
        if m + 2 < places:
            stored[m].wait()
            fetch(m + 2)
    exchange.share()
    line_second.slot(1)
    combine_ahead.share()
    exchange.finish()
    attn_polish(
        whole, attn_weights, attn_out, *polish_refs, between=(lambda: line_second.slot(2),)
    )
    for m in range(places - 2, places):
        stored[m].wait()
    combine_ahead.finish()
    reduce_second.finish()
    line_second.finish()


def run_back(
    grams, sent, columns, back, gates, ahead, cot, images, first, normed_b, mixed, qkv, router,
    gains, weights, momentum, attn_weights, direction, expert_weights, scale, rows, number,
):
    places, block_rows, _ = columns.shape
    groups, heads = lax.axis_size(DP), lax.axis_size(HEADS)
    count, padded, width = images.shape
    quarter = block_rows // heads
    extra = gates.shape[3]
    f32, bf16 = jnp.float32, jnp.bfloat16
    shape = jax.ShapeDtypeStruct
    vmem, anywhere = pl.BlockSpec(memory_space=pltpu.VMEM), pl.BlockSpec(memory_space=pl.ANY)
    back_scratch, back_sems = combining_scratch(
        places, block_rows, quarter, (width, extra), True, width
    )
    ahead_scratch, ahead_sems = combining_scratch(places, block_rows, quarter, (width,), False)
    gram = grams[0].shape[1:]
    exchange_refs, exchange_sems = exchange_scratch(places, heads, rows, momentum.shape)
    early = (
        grams[0], *sent, columns, back, gates, router, gains, momentum, attn_weights,
    )
    late = (ahead, grams[1], weights, qkv, first, cot, images, normed_b, mixed)
    return pl.pallas_call(
        functools.partial(back_kernel, scale),
        in_specs=[vmem] * len(early) + [anywhere] * (len(late) + 2),
        out_specs=[anywhere] + [vmem] * 3 + [anywhere] * 3,
        out_shape=[
            shape((heads, quarter, width), bf16),
            shape((count, padded, width), f32),
            shape((rows, TILE), f32),
            shape(attn_weights.shape, f32),
            shape((places,) + gram, f32),
            shape((places,) + gram, f32),
            shape((places,) + expert_weights.shape[1:], f32),
        ],
        scratch_shapes=[pltpu.VMEM(values.shape, values.dtype) for values in late]
        + [
            pltpu.VMEM((heads, quarter, width), bf16),
            pltpu.VMEM((heads, quarter, extra), f32),
            pltpu.VMEM((2, places - 1) + gram, f32),
            pltpu.VMEM((2, places - 1) + gram, f32),
            pltpu.VMEM(gram, f32),
            pltpu.VMEM(gram, f32),
            pltpu.VMEM((width, width), f32),
            pltpu.VMEM((width, width), f32),
            pltpu.VMEM((width, width), f32),
            pltpu.VMEM((groups, places, rows, TILE), f32),
            pltpu.VMEM((count, padded, width), bf16),
            pltpu.VMEM((count, padded, width), bf16),
            pltpu.VMEM((padded, width), bf16),
            pltpu.VMEM((padded, 3 * width), bf16),
            pltpu.VMEM((3, heads, count * padded, TILE), bf16),
            pltpu.VMEM((groups, heads) + momentum.shape, f32),
            pltpu.SemaphoreType.DMA((len(late),)),
            pltpu.SemaphoreType.DMA((8,)),
        ]
        + back_scratch
        + back_sems
        + ahead_scratch
        + ahead_sems
        + line_sems(places) * 2
        + (line_sems(places) + [pltpu.SemaphoreType.DMA(())]) * 2
        + exchange_refs
        + exchange_sems,
        compiler_params=pltpu.CompilerParams(
            collective_id=number, has_side_effects=True, vmem_limit_bytes=VMEM_LARGE
        ),
        name="back",
    )(*early, *late, direction, expert_weights)


def slot_places(slots, ids_ref, rank_out, column_out):
    groups, places, _, rows = ids_ref.shape
    experts = rank_out.shape[0] // groups
    labels = [own_label(experts, e).astype(jnp.float32) for e in range(experts)]
    wide = ceil_to(rows, TILE)
    earlier = lax.broadcasted_iota(jnp.int32, (rows, rows), 0)
    later = lax.broadcasted_iota(jnp.int32, (rows, rows), 1)
    before = jnp.where(earlier < later, 1.0, 0.0).astype(jnp.bfloat16)
    running = jnp.zeros((groups * experts, 1), jnp.float32)
    ranks = []
    for place in range(places):
        ids = [
            ids_ref[g, place, k : k + 1, :].astype(jnp.float32)
            for g in range(groups)
            for k in range(TOP)
        ]
        marks = []
        for e in range(experts):
            for g in range(groups):
                hit = ids[TOP * g] == labels[e]
                for k in range(1, TOP):
                    hit = hit | (ids[TOP * g + k] == labels[e])
                marks.append(jnp.where(hit, 1.0, 0.0))
        marks = jnp.concatenate(marks, axis=0)
        rank = running + dot_low(marks.astype(jnp.bfloat16), before)
        running = running + jnp.sum(marks, axis=1, keepdims=True)
        rank = jnp.where(marks > 0, rank, -1.0)
        ranks.append(rank)
        codes = []
        for g in range(groups):
            for k in range(TOP):
                code = jnp.full((1, rows), -1.0, jnp.float32)
                for e in range(experts):
                    own = ids[TOP * g + k] == labels[e]
                    number = e * groups + g
                    code = jnp.where(own, rank[number : number + 1] + float(slots * e), code)
                codes.append(code)
        both = jnp.concatenate(codes + ids, axis=0)
        columns = both.shape[0]
        both = jnp.concatenate(
            [both, jnp.zeros((columns, wide - rows), jnp.float32)], axis=1
        )
        both = jnp.concatenate([both, jnp.zeros((TILE - columns, wide), jnp.float32)], axis=0)
        for start in range(0, rows, TILE):
            turned = both[:, start : start + TILE].T
            count = min(TILE, rows - start)
            column_out[place * rows + start : place * rows + start + count, :] = turned[
                :count, :columns
            ].astype(jnp.int32)
    rank_out[...] = jnp.concatenate(ranks, axis=1).astype(jnp.int32)


def last_kernel(scale, made_ref, packed_ref, dir_ref, weight_ref, out_ref, whole):
    count = pl.num_programs(0) // 2

    @pl.when(pl.program_id(0) < count)
    def _():
        out_ref[...] = made_ref[...]

    @pl.when(pl.program_id(0) >= count)
    def _():
        unpack_upper(packed_ref.at[0], whole)
        ortho = dot_exact(whole[...], dir_ref[0])
        out_ref[0] = weight_ref[0] * (1.0 - muon_rate * muon_decay) - scale * ortho


def run_last(scale, made, packed, direction, weights):
    mats, width, hidden = weights.shape
    count = mats // 2
    block = (1, width, hidden)

    def early(m):
        return (jnp.minimum(m, count - 1), 0, 0)

    def late(m):
        return (jnp.maximum(m - count, 0), 0, 0)

    return pl.pallas_call(
        functools.partial(last_kernel, scale),
        grid=(mats,),
        in_specs=[
            pl.BlockSpec(block, early),
            pl.BlockSpec((1,) + packed.shape[1:], late),
            pl.BlockSpec(block, late),
            pl.BlockSpec(block, lambda m: (jnp.maximum(m, count), 0, 0)),
        ],
        out_specs=pl.BlockSpec(block, lambda m: (m, 0, 0)),
        out_shape=jax.ShapeDtypeStruct(weights.shape, jnp.float32),
        scratch_shapes=[pltpu.VMEM((width, width), jnp.float32)],
        compiler_params=pltpu.CompilerParams(vmem_limit_bytes=VMEM_LIMIT),
        name="last",
    )(made, packed, direction, weights)


def shards_fast(
    images_in,
    attn_weights,
    attn_momentum,
    router_weight,
    router_first,
    router_second,
    expert_weights,
    expert_momentum,
    norm_params,
    norm_first,
    norm_second,
    expert_ids,
    cotangent,
):
    rows, width = images_in.shape
    dp_count = lax.axis_size(DP)
    head_count = lax.axis_size(HEADS)
    tensor_count = lax.axis_size(TENSOR)
    mats = expert_weights.shape[0]
    hidden_cols = expert_weights.shape[2]
    group_rows = expert_ids.shape[0]
    slots = ceil_to(3 * TOP * group_rows // (2 * EXPERTS), 16)
    images = rows // SEQ
    image_rows = ceil_to(SEQ, 16 * head_count // math.gcd(images, head_count))
    padded_rows = images * image_rows
    quarter = padded_rows // head_count
    bf16, f32 = jnp.bfloat16, jnp.float32

    def pad_images(values):
        values = values.reshape(-1, SEQ, values.shape[-1])
        return jnp.pad(values, ((0, 0), (0, image_rows - SEQ), (0, 0)))

    def drop_padding(values):
        return values.reshape(images, image_rows, -1)[:, :SEQ].reshape(rows, -1)

    attn_rows = attn_weights.size // TILE
    small = jnp.concatenate((router_weight.T, norm_params), axis=0).astype(bf16)
    small_rows, small_lanes = small.shape
    small = jnp.pad(
        small, ((0, ceil_to(small_rows, 16) - small_rows), (0, TILE - small_lanes))
    )
    flat = jnp.concatenate((attn_weights.astype(bf16).reshape(attn_rows, TILE), small), axis=0)
    padded_cot = pad_images(cotangent)
    padded_images = pad_images(images_in)
    own_ids = jnp.pad(
        expert_ids.reshape(-1, SEQ, TOP), ((0, 0), (0, image_rows - SEQ), (0, 0)), constant_values=-1
    )
    own_ids = jnp.transpose(own_ids.reshape(tensor_count, padded_rows, TOP), (0, 2, 1))
    experts_own = mats // 2

    (
        qkv, mixed, first, normed_b, router_low, gains, weights_low, slot_in, slot_cot, member, columns,
    ) = run_front(
        flat, padded_images, padded_cot.reshape(head_count, quarter, width), own_ids,
        experts_own, slots, 1,
    )

    step = tensor_count // 2
    earlier = ()
    directions, packed = [], []
    for start in range(0, experts_own, step):
        *earlier, direction, gram = run_experts(
            start, step, slot_in, slot_cot, member, router_low, expert_weights, expert_momentum,
            tuple(earlier),
        )
        directions.append(direction)
        packed.append(gram)
    expert_mom, back, gate_back, ahead = earlier
    places = columns.reshape(tensor_count, padded_rows, -1)

    def by_group(values):
        return values.reshape(experts_own, dp_count, slots, values.shape[-1])

    far = tensor_count - 1
    sent = (
        lax.ppermute(packed[0][far], TENSOR, [(0, 1)]),
        lax.ppermute(packed[0][0], TENSOR, [(far, far - 1)]),
    )
    scale = muon_scale(width, hidden_cols * tensor_count)
    ahead_total, input_grad, sums, attn_new, _, product, made = run_back(
        packed, sent, places, by_group(back), by_group(gate_back), by_group(ahead), padded_cot,
        padded_images, first, normed_b, mixed, qkv, router_low, gains, weights_low,
        attn_momentum.reshape(attn_rows, TILE), attn_weights.reshape(attn_rows, TILE),
        directions[0], expert_weights, scale, flat.shape[0], 2,
    )
    expert_new = run_last(scale, made, product, directions[1], expert_weights)
    block_out = drop_padding(
        first + ahead_total.reshape(images, image_rows, width).astype(f32)
    )
    input_grad = drop_padding(input_grad)
    attn_sum = sums[:attn_rows].reshape(attn_weights.shape)
    router_sum = sums[attn_rows : attn_rows + EXPERTS, :small_lanes].T
    norm_sum = sums[attn_rows + EXPERTS : attn_rows + small_rows, :small_lanes]
    attn_mom = momentum_decay * attn_momentum + attn_sum
    attn_new = attn_new.reshape(attn_weights.shape)

    router_first_new, router_second_new, router_new = adamw_update(
        router_weight, router_first, router_second, router_sum, router_rate, router_decay
    )
    norm_first_new, norm_second_new, norm_new = adamw_update(
        norm_params, norm_first, norm_second, norm_sum, gains_rate, 0.0
    )
    return (
        block_out,
        input_grad,
        attn_mom,
        attn_new,
        router_first_new,
        router_second_new,
        router_new,
        expert_mom,
        expert_new,
        norm_first_new,
        norm_second_new,
        norm_new,
    )


def solution(mesh):
    in_specs = (
        P((DP, TENSOR), None),
        P(TENSOR, DP, HEADS),
        P(TENSOR, DP, HEADS),
        P((DP, TENSOR), None),
        P((DP, TENSOR), None),
        P((DP, TENSOR), None),
        P((HEADS, DP), None, TENSOR),
        P((HEADS, DP), None, TENSOR),
        P(None, (DP, TENSOR)),
        P(None, (DP, TENSOR)),
        P(None, (DP, TENSOR)),
        P(DP, None),
        P((DP, TENSOR), None),
    )
    out_specs = (
        P((DP, TENSOR), None),
        P((DP, TENSOR), None),
        P(TENSOR, DP, HEADS),
        P(TENSOR, DP, HEADS),
        P((DP, TENSOR), None),
        P((DP, TENSOR), None),
        P((DP, TENSOR), None),
        P((HEADS, DP), None, TENSOR),
        P((HEADS, DP), None, TENSOR),
        P(None, (DP, TENSOR)),
        P(None, (DP, TENSOR)),
        P(None, (DP, TENSOR)),
    )
    shape = dict(mesh.shape)
    step = EXPERTS * 2 // (shape[HEADS] * shape[DP])
    fits = shape[DP] == 2 and shape[HEADS] == 4 and step % (2 * shape[TENSOR]) == 0
    fits = fits and step == 2 * shape[TENSOR] and shape[TENSOR] % 2 == 0
    shards = shards_fast if fits else shards_general
    return jax.shard_map(shards, mesh=mesh, in_specs=in_specs, out_specs=out_specs, check_vma=False)
```

```python
import functools
import math

import jax
import jax.numpy as jnp
from jax import lax
from jax.experimental import pallas as pl
from jax.experimental.pallas import tpu as pltpu
from jax.sharding import PartitionSpec as P

EXPERTS = 32
SEQ = 197
TOP = 2
ITERS = 5
STEP = 5
HEAD_DIM = 64


norm_epsilon = 1e-06
coef_first = 3.4445
coef_second = -4.775
coef_third = 2.0315
momentum_decay = 0.95
muon_rate = 0.2
muon_decay = 0.1
adam_first = 0.9
adam_second = 0.999
adam_epsilon = 1e-08
router_rate = 0.03
router_decay = 0.01
gains_rate = 0.1
TILE = 128
DP, HEADS, TENSOR = "dp", "heads", "tensor"
TO_ALL, OWN_HEAD, TO_CORE = range(3)
VMEM_LIMIT = 56 * 1024 * 1024
VMEM_LARGE = 62 * 1024 * 1024


def norm_forward(values, gain, shift):
    center = jnp.mean(values, axis=-1, keepdims=True)
    centred = values - center
    inverse = lax.rsqrt(jnp.mean(centred * centred, axis=-1, keepdims=True) + norm_epsilon)
    scaled = centred * inverse
    return (scaled * gain + shift, scaled, inverse)


def norm_backward(grad_normed, scaled, inverse, gain):
    grad_scaled = grad_normed * gain
    inner = grad_scaled - jnp.mean(grad_scaled, axis=-1, keepdims=True)
    inner = inner - scaled * jnp.mean(grad_scaled * scaled, axis=-1, keepdims=True)
    return inner * inverse


def exact_gelu(values):
    return jax.nn.gelu(values, approximate=False)


def batch_gram(values):
    return jnp.einsum("mij,mkj->mik", values, values, precision=lax.Precision.HIGHEST)


def batch_product(left, right):
    return jnp.einsum("mij,mjk->mik", left, right, precision=lax.Precision.HIGHEST)


def polish_step(values, gram):
    poly = coef_second * gram + coef_third * batch_product(gram, gram)
    return coef_first * values + batch_product(poly, values)


def muon_scale(rows, cols):
    return muon_rate * 0.2 * math.sqrt(max(rows, cols))


def adamw_update(values, first, second, grad, rate, decay):
    first_new = adam_first * first + (1.0 - adam_first) * grad
    second_new = adam_second * second + (1.0 - adam_second) * grad * grad
    first_hat = first_new / (1.0 - adam_first**STEP)
    second_hat = second_new / (1.0 - adam_second**STEP)
    values_new = values * (1.0 - rate * decay) - rate * first_hat / (
        jnp.sqrt(second_hat) + adam_epsilon
    )
    return (first_new, second_new, values_new)


def shards_general(
    images_in,
    attn_weights,
    attn_momentum,
    router_weight,
    router_first,
    router_second,
    expert_weights,
    expert_momentum,
    norm_params,
    norm_first,
    norm_second,
    expert_ids,
    cotangent,
):
    local_rows, width = images_in.shape
    dp_count = lax.axis_size(DP)
    head_count = lax.axis_size(HEADS)
    tensor_count = lax.axis_size(TENSOR)
    mats_here = attn_weights.shape[0]
    row_shard = attn_weights.shape[1]
    head_cols = attn_weights.shape[2]
    hidden_cols = expert_weights.shape[2]
    group_rows = expert_ids.shape[0]
    capacity = 3 * TOP * group_rows // (2 * EXPERTS)
    experts_here = EXPERTS // head_count
    heads_here = head_cols // HEAD_DIM
    images = local_rows // SEQ
    score_scale = HEAD_DIM ** (-0.5)
    head_index = lax.axis_index(HEADS)
    tensor_index = lax.axis_index(TENSOR)
    dp_index = lax.axis_index(DP)
    attn_low, router_low, norms_low = (
        lax.all_gather(attn_weights.astype(jnp.bfloat16), (DP, TENSOR), axis=0, tiled=True),
        lax.all_gather(router_weight.astype(jnp.bfloat16), (DP, TENSOR), axis=0, tiled=True),
        lax.all_gather(norm_params.astype(jnp.bfloat16), (DP, TENSOR), axis=1, tiled=True),
    )
    attn_low = attn_low.reshape(dp_count, tensor_count * mats_here, row_shard, head_cols)
    attn_low = jnp.transpose(attn_low, (1, 0, 2, 3)).reshape(
        tensor_count * mats_here, width, head_cols
    )
    gains = norms_low.astype(jnp.float32)
    qkv_weight = jnp.transpose(attn_low[:3], (1, 0, 2)).reshape(width, 3 * head_cols)
    out_weight = attn_low[3]
    tokens = images_in.astype(jnp.float32)
    normed_a, scaled_a, inverse_a = norm_forward(tokens, gains[0], gains[1])
    normed_a = normed_a.astype(jnp.bfloat16)
    qkv = jnp.dot(normed_a, qkv_weight, preferred_element_type=jnp.float32).astype(jnp.bfloat16)
    split = qkv.reshape(images, SEQ, 3, heads_here, HEAD_DIM)
    query = split[:, :, 0]
    keys = split[:, :, 1]
    values = split[:, :, 2]
    scores = (
        jnp.einsum("ishd,ithd->ihst", query, keys, preferred_element_type=jnp.float32) * score_scale
    )
    peak = jnp.max(scores, axis=-1, keepdims=True)
    logsum = peak + jnp.log(jnp.sum(jnp.exp(scores - peak), axis=-1, keepdims=True))
    probs_low = jnp.exp(scores - logsum).astype(jnp.bfloat16)
    mixed = jnp.einsum("ihst,ithd->ishd", probs_low, values, preferred_element_type=jnp.float32)
    mixed = mixed.reshape(local_rows, head_cols).astype(jnp.bfloat16)
    partial_out = jnp.einsum("tc,dc->td", mixed, out_weight, preferred_element_type=jnp.float32)
    attended = lax.psum(partial_out, HEADS)
    first = tokens + attended
    normed_b, scaled_b, inverse_b = norm_forward(first, gains[2], gains[3])
    normed_b = normed_b.astype(jnp.bfloat16)
    group_in, group_cot = (
        lax.all_gather(normed_b, TENSOR, axis=0, tiled=True),
        lax.all_gather(cotangent, TENSOR, axis=0, tiled=True),
    )
    logits = jnp.dot(group_in, router_low, preferred_element_type=jnp.float32)
    chosen = jnp.take_along_axis(logits, expert_ids, axis=1)
    raised = jnp.exp(chosen - jnp.max(chosen, axis=1, keepdims=True))
    gates = raised / jnp.sum(raised, axis=1, keepdims=True)
    routes = expert_ids.reshape(-1)
    route_count = routes.shape[0]
    order = jnp.argsort(routes * route_count + jnp.arange(route_count, dtype=jnp.int32))
    labels = head_index * experts_here + jnp.arange(experts_here, dtype=jnp.int32)
    counts = jnp.sum((routes[None, :] == labels[:, None]).astype(jnp.int32), axis=1)
    starts = jnp.sum((routes[None, :] < labels[:, None]).astype(jnp.int32), axis=1)
    slot_index = jnp.arange(capacity, dtype=jnp.int32)
    picked = order[jnp.minimum(starts[:, None] + slot_index[None, :], route_count - 1)]
    filled = (slot_index[None, :] < counts[:, None]).astype(jnp.float32)
    token_rows = (picked // TOP).reshape(-1)
    pick_cols = (picked % TOP).reshape(-1)
    slot_gate = gates[token_rows, pick_cols].reshape(experts_here, capacity) * filled
    slot_in = group_in[token_rows].reshape(experts_here, capacity, width)
    pair = lax.all_gather(expert_weights.astype(jnp.bfloat16), DP, axis=0, tiled=True).reshape(
        experts_here, 2, width, hidden_cols
    )
    hidden = jnp.einsum("ecd,edf->ecf", slot_in, pair[:, 0], preferred_element_type=jnp.float32)
    active, gelu_pull = jax.vjp(exact_gelu, hidden)
    active = active.astype(jnp.bfloat16)
    expert_out = jnp.einsum("ecf,edf->ecd", active, pair[:, 1], preferred_element_type=jnp.float32)
    weighted = (expert_out * slot_gate[:, :, None]).reshape(-1, width)
    spread = jnp.zeros((group_rows, width), jnp.float32).at[token_rows].add(weighted)
    own_sum = lax.psum_scatter(spread, TENSOR, scatter_dimension=0, tiled=True)
    moe_out = lax.psum(own_sum, HEADS)
    block_out = first + moe_out
    grad_out = cotangent.astype(jnp.float32)
    slot_cot = group_cot[token_rows].reshape(experts_here, capacity, width).astype(jnp.float32)
    gate_grad = jnp.sum(slot_cot * expert_out, axis=-1) * filled
    out_grad = (slot_cot * slot_gate[:, :, None]).astype(jnp.bfloat16)
    pair_back = lax.all_gather(
        expert_weights.astype(jnp.bfloat16), DP, axis=0, tiled=True
    ).reshape(experts_here, 2, width, hidden_cols)
    active_grad = jnp.einsum(
        "ecd,edf->ecf", out_grad, pair_back[:, 1], preferred_element_type=jnp.float32
    )
    hidden_grad = gelu_pull(active_grad)[0].astype(jnp.bfloat16)
    down_grad = jnp.einsum("ecd,ecf->edf", out_grad, active, preferred_element_type=jnp.float32)
    up_grad = jnp.einsum("ecd,ecf->edf", slot_in, hidden_grad, preferred_element_type=jnp.float32)
    slot_in_grad = jnp.einsum(
        "ecf,edf->ecd", hidden_grad, pair_back[:, 0], preferred_element_type=jnp.float32
    ).reshape(-1, width)
    back_spread = jnp.zeros((group_rows, width), jnp.float32).at[token_rows].add(slot_in_grad)
    gate_spread = (
        jnp.zeros((group_rows, TOP), jnp.float32)
        .at[token_rows, pick_cols]
        .add(gate_grad.reshape(-1))
    )
    own_back, own_gate = (
        lax.psum_scatter(back_spread, TENSOR, scatter_dimension=0, tiled=True),
        lax.psum_scatter(gate_spread, TENSOR, scatter_dimension=0, tiled=True),
    )
    normed_b_grad, gate_total = lax.psum((own_back, own_gate), HEADS)
    matrix_grads = jnp.stack((up_grad, down_grad), axis=1).reshape(
        2 * experts_here, width, hidden_cols
    )
    expert_grad = lax.psum_scatter(matrix_grads, DP, scatter_dimension=0, tiled=True)
    own_ids = lax.dynamic_slice_in_dim(expert_ids, tensor_index * local_rows, local_rows, 0)
    own_gates = lax.dynamic_slice_in_dim(gates, tensor_index * local_rows, local_rows, 0)
    blend = jnp.sum(own_gates * gate_total, axis=1, keepdims=True)
    chosen_grad = own_gates * (gate_total - blend)
    expert_labels = jnp.arange(EXPERTS, dtype=jnp.int32)
    matches = (own_ids[:, :, None] == expert_labels[None, None, :]).astype(jnp.float32)
    logit_grad = jnp.sum(matches * chosen_grad[:, :, None], axis=1).astype(jnp.bfloat16)
    normed_b_grad = normed_b_grad + jnp.einsum(
        "te,de->td", logit_grad, router_low, preferred_element_type=jnp.float32
    )
    router_grad = jnp.einsum("td,te->de", normed_b, logit_grad, preferred_element_type=jnp.float32)
    gain_b_grad = jnp.sum(normed_b_grad * scaled_b, axis=0)
    shift_b_grad = jnp.sum(normed_b_grad, axis=0)
    first_grad = grad_out + norm_backward(normed_b_grad, scaled_b, inverse_b, gains[2])
    branch_grad = first_grad.astype(jnp.bfloat16)
    out_weight_grad = jnp.einsum(
        "td,tc->dc", branch_grad, mixed, preferred_element_type=jnp.float32
    )
    mixed_grad = jnp.einsum(
        "td,dc->tc", branch_grad, out_weight, preferred_element_type=jnp.float32
    ).astype(jnp.bfloat16)
    mixed_grad = mixed_grad.reshape(images, SEQ, heads_here, HEAD_DIM)
    scores_again = (
        jnp.einsum("ishd,ithd->ihst", query, keys, preferred_element_type=jnp.float32) * score_scale
    )
    probs_again = jnp.exp(scores_again - logsum)
    prob_grad = jnp.einsum(
        "ishd,ithd->ihst", mixed_grad, values, preferred_element_type=jnp.float32
    )
    value_grad = jnp.einsum(
        "ihst,ishd->ithd",
        probs_again.astype(jnp.bfloat16),
        mixed_grad,
        preferred_element_type=jnp.float32,
    )
    score_grad = (
        probs_again * (prob_grad - jnp.sum(probs_again * prob_grad, axis=-1, keepdims=True))
    ).astype(jnp.bfloat16)
    query_grad = (
        jnp.einsum("ihst,ithd->ishd", score_grad, keys, preferred_element_type=jnp.float32)
        * score_scale
    )
    key_grad = (
        jnp.einsum("ihst,ishd->ithd", score_grad, query, preferred_element_type=jnp.float32)
        * score_scale
    )
    qkv_grad = (
        jnp.stack((query_grad, key_grad, value_grad), axis=2)
        .reshape(local_rows, 3 * head_cols)
        .astype(jnp.bfloat16)
    )
    normed_a_part = jnp.einsum(
        "tc,dc->td", qkv_grad, qkv_weight, preferred_element_type=jnp.float32
    )
    qkv_weight_grad = jnp.einsum(
        "td,tc->dc", normed_a, qkv_grad, preferred_element_type=jnp.float32
    )
    normed_a_grad = lax.psum(normed_a_part, HEADS)
    gain_a_grad = jnp.sum(normed_a_grad * scaled_a, axis=0)
    shift_a_grad = jnp.sum(normed_a_grad, axis=0)
    input_grad = first_grad + norm_backward(normed_a_grad, scaled_a, inverse_a, gains[0])
    attn_grad = jnp.concatenate(
        (
            jnp.transpose(qkv_weight_grad.reshape(width, 3, head_cols), (1, 0, 2)),
            out_weight_grad[None],
        ),
        axis=0,
    )
    arranged = attn_grad.reshape(tensor_count, mats_here, dp_count, row_shard, head_cols)
    arranged = jnp.transpose(arranged, (2, 0, 1, 3, 4)).reshape(
        dp_count * tensor_count * mats_here, row_shard, head_cols
    )
    norm_grad = jnp.stack((gain_a_grad, shift_a_grad, gain_b_grad, shift_b_grad))
    attn_sum, router_sum, norm_sum = (
        lax.psum_scatter(arranged, (DP, TENSOR), scatter_dimension=0, tiled=True),
        lax.psum_scatter(router_grad, (DP, TENSOR), scatter_dimension=0, tiled=True),
        lax.psum_scatter(norm_grad, (DP, TENSOR), scatter_dimension=1, tiled=True),
    )
    attn_mom = momentum_decay * attn_momentum + attn_sum
    attn_dir = attn_sum + momentum_decay * attn_mom
    whole = lax.all_gather(attn_dir, (DP, HEADS), axis=1, tiled=True)
    whole = whole.reshape(mats_here, dp_count, head_count, row_shard, head_cols)
    whole = jnp.transpose(whole, (0, 1, 3, 2, 4)).reshape(mats_here, width, head_count * head_cols)
    whole = whole / (jnp.sqrt(jnp.sum(whole * whole, axis=(1, 2), keepdims=True)) + 1e-07)
    for iteration in range(ITERS):
        whole = polish_step(whole, batch_gram(whole))
    own_part = lax.dynamic_slice(
        whole, (0, dp_index * row_shard, head_index * head_cols), (mats_here, row_shard, head_cols)
    )
    attn_new = (
        attn_weights * (1.0 - muon_rate * muon_decay)
        - muon_scale(width, head_count * head_cols) * own_part
    )
    expert_mom = momentum_decay * expert_momentum + expert_grad
    current = expert_grad + momentum_decay * expert_mom
    for iteration in range(ITERS):
        gram = lax.psum(batch_gram(current), TENSOR)
        if iteration == 0:
            factor = 1.0 / (jnp.sqrt(jnp.trace(gram, axis1=1, axis2=2)) + 1e-07)
            factor = factor[:, None, None]
            current = current * factor
            gram = gram * (factor * factor)
        current = polish_step(current, gram)
    expert_new = (
        expert_weights * (1.0 - muon_rate * muon_decay)
        - muon_scale(width, hidden_cols * tensor_count) * current
    )
    router_first_new, router_second_new, router_new = adamw_update(
        router_weight, router_first, router_second, router_sum, router_rate, router_decay
    )
    norm_first_new, norm_second_new, norm_new = adamw_update(
        norm_params, norm_first, norm_second, norm_sum, gains_rate, 0.0
    )
    return (
        block_out,
        input_grad,
        attn_mom,
        attn_new,
        router_first_new,
        router_second_new,
        router_new,
        expert_mom,
        expert_new,
        norm_first_new,
        norm_second_new,
        norm_new,
    )


def ceil_to(value, step):
    return -(-value // step) * step


def dot_exact(left, right):
    return jnp.dot(
        left, right, precision=lax.Precision.HIGH, preferred_element_type=jnp.float32
    )


def dot_low(left, right, contract=((1,), (0,))):
    return lax.dot_general(
        left, right, (contract, ((), ())), preferred_element_type=jnp.float32
    )


def block_pairs(width):
    tiles = width // TILE
    return [(i, j) for i in range(tiles) for j in range(i + 1, tiles)]


def packed_rows(width):
    tiles = width // TILE
    return (len(block_pairs(width)) + tiles // 2) * TILE + ceil_to(tiles // 2, 8)


def tile_places():
    rows = lax.broadcasted_iota(jnp.int32, (TILE, TILE), 0)
    lanes = lax.broadcasted_iota(jnp.int32, (TILE, TILE), 1)
    return rows, lanes


def pack_upper(block, width, out_ref):
    rows, lanes = tile_places()
    start = 0
    for i, j in block_pairs(width):
        out_ref[start : start + TILE, :] = block(i, j)
        start += TILE
    diagonals = []
    for i in range(0, width // TILE, 2):
        second = block(i + 1, i + 1)
        out_ref[start : start + TILE, :] = jnp.where(rows <= lanes, block(i, i), second)
        diagonals.append(
            jnp.sum(jnp.where(rows == lanes, second, 0.0), axis=0, keepdims=True)
        )
        start += TILE
    rest = out_ref.shape[0] - start - len(diagonals)
    if rest:
        diagonals.append(jnp.zeros((rest, TILE), jnp.float32))
    out_ref[start:, :] = jnp.concatenate(diagonals, axis=0)


def packed_trace(packed_ref, width):
    rows, lanes = tile_places()
    start = len(block_pairs(width)) * TILE
    total = jnp.zeros((1, 1), jnp.float32)
    pairs = width // TILE // 2
    for pair in range(pairs):
        block = packed_ref[start + pair * TILE : start + (pair + 1) * TILE, :]
        total = total + jnp.sum(jnp.where(rows == lanes, block, 0.0), keepdims=True)
    return total + jnp.sum(packed_ref[start + pairs * TILE :, :], keepdims=True)


def unpack_upper(packed_ref, out_ref, factor=None):
    rows, lanes = tile_places()
    width = out_ref.shape[0]

    def load(start, count):
        values = packed_ref[start : start + count, :]
        return values if factor is None else values * factor

    start = 0
    for i, j in block_pairs(width):
        block = load(start, TILE)
        out_ref[i * TILE : (i + 1) * TILE, j * TILE : (j + 1) * TILE] = block
        out_ref[j * TILE : (j + 1) * TILE, i * TILE : (i + 1) * TILE] = block.T
        start += TILE
    diagonals = load(start + width // 2, 8)
    for i in range(0, width // TILE, 2):
        block = load(start, TILE)
        turned = block.T
        first = jnp.where(rows <= lanes, block, turned)
        second = jnp.where(rows > lanes, block, turned)
        second = jnp.where(rows == lanes, diagonals[i // 2 : i // 2 + 1], second)
        out_ref[i * TILE : (i + 1) * TILE, i * TILE : (i + 1) * TILE] = first
        i += 1
        out_ref[i * TILE : (i + 1) * TILE, i * TILE : (i + 1) * TILE] = second
        start += TILE


def gram_packed(values, out_ref):
    rows = values.shape[0]
    half = rows // 2
    contract = (((1,), (1,)), ((), ()))
    upper = lax.dot_general(
        values[:half], values, contract,
        precision=lax.Precision.HIGH, preferred_element_type=jnp.float32,
    )
    lower = lax.dot_general(
        values[half:], values[half:], contract,
        precision=lax.Precision.HIGH, preferred_element_type=jnp.float32,
    )

    def block(i, j):
        top, left = i * TILE, j * TILE
        if top < half:
            return upper[top : top + TILE, left : left + TILE]
        return lower[top - half : top - half + TILE, left - half : left - half + TILE]

    pack_upper(block, rows, out_ref)


def own_label(experts, number):
    shard = lax.axis_index(HEADS) * lax.axis_size(DP) + lax.axis_index(DP)
    return shard * experts + number


def expert_kernel(
    first, slot_in_ref, slot_cot_ref, member_ref, router_ref, weight_ref, momentum_ref,
    momentum_out, back_out, gate_out, ahead_out, dir_out, gram_out,
):
    experts = EXPERTS // (lax.axis_size(HEADS) * lax.axis_size(DP))
    label = own_label(experts, first + pl.program_id(0))
    rows = slot_in_ref.shape[1] * slot_in_ref.shape[2]
    slot_in = slot_in_ref[0].reshape(rows, -1)
    slot_cot = slot_cot_ref[0].reshape(rows, -1).astype(jnp.float32)
    member = member_ref[0].reshape(rows, EXPERTS)
    logits = dot_low(slot_in, router_ref[...], ((1,), (1,)))
    lanes = lax.broadcasted_iota(jnp.int32, logits.shape, 1)
    own = jnp.where(lanes == label, 1.0, 0.0)
    filled = jnp.sum(member * own, axis=1, keepdims=True)
    logit_own = jnp.sum(logits * own, axis=1, keepdims=True)
    logit_other = jnp.sum(logits * (member - own), axis=1, keepdims=True)
    peak = jnp.maximum(logit_own, logit_other)
    raised = jnp.exp(logit_own - peak)
    gate = filled * raised / (raised + jnp.exp(logit_other - peak))
    up = weight_ref[0].astype(jnp.bfloat16)
    down = weight_ref[1].astype(jnp.bfloat16)
    hidden = dot_low(slot_in, up)
    cdf = 0.5 * (1.0 + lax.erf(hidden * math.sqrt(0.5)))
    active = (hidden * cdf).astype(jnp.bfloat16)
    slope = cdf + hidden * jnp.exp(-0.5 * hidden * hidden) * (1.0 / math.sqrt(2.0 * math.pi))
    expert_out = dot_low(active, down, ((1,), (1,)))
    gate_grad = jnp.sum(slot_cot * expert_out, axis=1, keepdims=True) * filled
    ahead_out[0] = (expert_out * gate).astype(jnp.bfloat16)
    out_grad = (slot_cot * gate).astype(jnp.bfloat16)
    hidden_grad = (dot_low(out_grad, down) * slope).astype(jnp.bfloat16)
    back_out[0] = dot_low(hidden_grad, up, ((1,), (1,))).astype(jnp.bfloat16)
    wide = lax.broadcasted_iota(jnp.int32, (gate_grad.shape[0], TILE), 1)
    high = gate_grad.astype(jnp.bfloat16).astype(jnp.float32)
    spread = jnp.where(wide == label, high, 0.0)
    spread = jnp.where(wide == label + EXPERTS, gate_grad - high, spread)
    gate_out[0] = spread.astype(jnp.bfloat16)
    for which, grad in enumerate(
        (
            dot_low(slot_in, hidden_grad, ((0,), (0,))),
            dot_low(out_grad, active, ((0,), (0,))),
        )
    ):
        momentum = momentum_decay * momentum_ref[which] + grad
        momentum_out[which] = momentum
        direction = grad + momentum_decay * momentum
        dir_out[which] = direction
        gram_packed(direction, gram_out.at[which])


def run_experts(first, count, slot_in, slot_cot, member, router, weights, momentum, earlier):
    _, groups, slots, width = slot_in.shape
    mats, _, hidden = weights.shape
    packed = packed_rows(width)
    shape = jax.ShapeDtypeStruct
    whole = (
        shape((mats, width, hidden), jnp.float32),
        shape((mats // 2, groups * slots, width), jnp.bfloat16),
        shape((mats // 2, groups * slots, TILE), jnp.bfloat16),
        shape((mats // 2, groups * slots, width), jnp.bfloat16),
    )
    part = (
        shape((2 * count, width, hidden), jnp.float32),
        shape((2 * count, packed, TILE), jnp.float32),
    )

    def shifted(e):
        return (first + e, 0, 0)

    def here(e):
        return (e, 0, 0)

    def slotted(e):
        return (first + e, 0, 0, 0)

    def kernel(*refs):
        expert_kernel(first, *refs[:6], *refs[6 + len(earlier) :])

    return pl.pallas_call(
        kernel,
        grid=(count,),
        in_specs=[
            pl.BlockSpec((1, groups, slots, width), slotted),
            pl.BlockSpec((1, groups, slots, width), slotted),
            pl.BlockSpec((1, groups, slots, EXPERTS), slotted),
            pl.BlockSpec(router.shape, lambda e: (0, 0)),
            pl.BlockSpec((2, width, hidden), shifted),
            pl.BlockSpec((2, width, hidden), shifted),
        ]
        + [pl.BlockSpec(memory_space=pl.ANY)] * len(earlier),
        out_specs=[
            pl.BlockSpec((2, width, hidden), shifted),
            pl.BlockSpec((1, groups * slots, width), shifted),
            pl.BlockSpec((1, groups * slots, TILE), shifted),
            pl.BlockSpec((1, groups * slots, width), shifted),
            pl.BlockSpec((2, width, hidden), here),
            pl.BlockSpec((2, packed, TILE), here),
        ],
        out_shape=whole + part,
        input_output_aliases={6 + place: place for place in range(len(earlier))},
        compiler_params=pltpu.CompilerParams(vmem_limit_bytes=VMEM_LIMIT),
        name="experts",
    )(slot_in, slot_cot, member, router, weights, momentum, *earlier)


def polish(packed_ref, out_ref, gram, poly, product, between=()):
    width = gram.shape[0]
    half = width // 2
    factor = 1.0 / (jnp.sqrt(packed_trace(packed_ref, width)) + 1e-07)
    unpack_upper(packed_ref, gram, factor * factor)

    def symmetric(left, right):
        upper = dot_exact(left[:half, :], right[...])
        corner = dot_exact(left[half:, :], right[:, half:])
        return upper, corner

    def store(ref, upper, corner):
        ref[:half, :] = upper
        ref[half:, half:] = corner
        ref[half:, :half] = upper[:, half:].T

    def eye(count):
        here = lax.broadcasted_iota(jnp.int32, (half, count), 0)
        there = lax.broadcasted_iota(jnp.int32, (half, count), 1)
        return jnp.where(here == there, coef_first, 0.0)

    def polynomial():
        upper, corner = symmetric(gram, gram)
        upper = eye(width) + coef_second * gram[:half, :] + coef_third * upper
        corner = eye(half) + coef_second * gram[half:, half:] + coef_third * corner
        return upper, corner

    def next_gram():
        store(poly, *symmetric(poly, poly))
        store(gram, *symmetric(gram, poly))

    def step(_, carry):
        store(poly, *polynomial())
        store(product, *symmetric(poly, product))
        next_gram()
        return carry

    upper, corner = polynomial()
    store(poly, upper, corner)
    store(product, upper, corner)
    next_gram()
    middle = ITERS // 2
    lax.fori_loop(1, middle, step, 0)
    for work in between:
        work()
    lax.fori_loop(middle, ITERS - 1, step, 0)
    store(poly, *polynomial())
    store(product, *symmetric(poly, product))

    def block(i, j):
        return product[i * TILE : (i + 1) * TILE, j * TILE : (j + 1) * TILE] * factor

    pack_upper(block, width, out_ref)


def neighbours(index, count):
    return [lax.rem(index + step, count) for step in range(1, count)]


def square_peers(index):
    return [3 - index, index + 1 - 2 * lax.rem(index, 2), lax.rem(index + 2, 4)]


def enter(peers):
    barrier = pltpu.get_barrier_semaphore()
    for peer in peers:
        pl.semaphore_signal(barrier, inc=1, device_id=peer, device_id_type=pl.DeviceIdType.MESH)
    pl.semaphore_wait(barrier, len(peers))


def send(source, target, send_sem, recv_sem, peer):
    copy = pltpu.make_async_remote_copy(
        src_ref=source,
        dst_ref=target,
        send_sem=send_sem,
        recv_sem=recv_sem,
        device_id=peer,
        device_id_type=pl.DeviceIdType.MESH,
    )
    copy.start()
    return copy


class Sharing:
    def __init__(self, values, out, sems):
        self.values, self.out, self.sems = values, out, sems
        self.core, self.tensor = lax.axis_index(DP), lax.axis_index(TENSOR)
        self.head, self.places = lax.axis_index(HEADS), lax.axis_size(TENSOR)
        self.along = neighbours(self.tensor, self.places)
        self.diagonal, self.beside, self.above = square_peers(self.head)
        self.origins = [self.tensor] + [
            lax.rem(self.tensor + self.places - step, self.places)
            for step in range(1, self.places)
        ]
        self.here = out.at[self.core, self.tensor, self.head]
        self.started = []

    def start(self):
        self.home = pltpu.make_async_copy(self.values, self.here, self.sems[0])
        self.home.start()
        for step, peer in enumerate(self.along):
            self.started.append(
                send(
                    self.values, self.here, self.sems[1].at[step], self.sems[2].at[step],
                    {TENSOR: peer},
                )
            )

    def to_partner(self, block, source, number):
        self.started.append(
            send(
                source, block, self.sems[5].at[number], self.sems[6].at[number],
                {DP: 1 - self.core},
            )
        )

    def to_sides(self, block, source, place):
        for step, peer in enumerate((self.beside, self.above)):
            number = 4 * place + step
            self.started.append(
                send(
                    source, block, self.sems[3].at[number], self.sems[4].at[number],
                    {HEADS: peer},
                )
            )

    def cut(self, block):
        rows = block.shape[0]
        middle = ceil_to(rows // 2, 16)
        return block.at[pl.ds(0, middle)], block.at[pl.ds(middle, rows - middle)]

    def pass_to_sides(self):
        self.to_sides(self.here, self.values, 0)
        self.to_partner(self.here, self.values, 0)
        for place in range(1, self.places):
            block = self.out.at[self.core, self.origins[place], self.head]
            wait_for(block, self.sems[2].at[place - 1])
            self.to_sides(block, block, place)
            self.to_partner(block, block, 4 * place)

    def pass_round(self):
        ways = ((self.beside, self.above), (self.above, self.beside))
        for place in range(self.places):
            for step, (peer, other) in enumerate(ways):
                block = self.out.at[self.core, self.origins[place], peer]
                wait_for(block, self.sems[4].at[4 * place + step])
                half = self.cut(block)[step]
                number = 4 * place + 2 + step
                self.started.append(
                    send(
                        half, half, self.sems[3].at[number], self.sems[4].at[number],
                        {HEADS: other},
                    )
                )
                self.to_partner(block, block, 4 * place + 1 + step)

    def own_group(self):
        for place in range(self.places):
            block = self.out.at[self.core, self.origins[place], self.diagonal]
            for step, half in enumerate(self.cut(block)):
                wait_for(half, self.sems[4].at[4 * place + 2 + step])
            self.to_partner(block, block, 4 * place + 3)
        self.home.wait()

    def other_group(self):
        corners = (self.head, self.beside, self.above, self.diagonal)
        for place in range(self.places):
            for step, peer in enumerate(corners):
                block = self.out.at[1 - self.core, self.origins[place], peer]
                wait_for(block, self.sems[6].at[4 * place + step])

    def finish(self):
        for copy in self.started:
            copy.wait_send()


def sharing_sems(places, corners):
    dma = pltpu.SemaphoreType.DMA
    blocks = places * corners
    return [dma(()), dma((places - 1,)), dma((places - 1,))] + [dma((blocks,))] * 4


def wait_for(block, sem):
    pltpu.make_async_copy(block, block, sem).wait()


class LineReduce:
    def __init__(self, parts, received, total, sems, ahead=None):
        self.parts, self.received, self.total = parts, received, total
        self.ahead = ahead
        self.send_sem, self.recv_sem = sems
        self.place = lax.axis_index(TENSOR)
        self.far = lax.axis_size(TENSOR) - 1
        self.ways = ((self.place, self.place + 1), (self.far - self.place, self.place - 1))

    def copy(self, way, slot, source):
        return pltpu.make_async_remote_copy(
            src_ref=source,
            dst_ref=self.received.at[way, slot],
            send_sem=self.send_sem.at[way, slot],
            recv_sem=self.recv_sem.at[way, slot],
            device_id={TENSOR: self.ways[way][1]},
            device_id_type=pl.DeviceIdType.MESH,
        )

    def slot(self, slot):
        for way, (behind, _) in enumerate(self.ways):
            owner = self.far - slot + behind if way == 0 else slot - behind

            @pl.when(behind == 0)
            def _():
                self.copy(way, slot, self.parts.at[owner]).start()

            if slot:

                @pl.when((behind > 0) & (behind <= slot))
                def _():
                    block = self.received.at[way, slot - 1]
                    if slot == 1 and self.ahead is not None:
                        block[...] = self.ahead[way][...] + self.parts[owner]
                    else:
                        wait_for(block, self.recv_sem.at[way, slot - 1])
                        block[...] = block[...] + self.parts[owner]
                    self.copy(way, slot, block).start()

    def final(self):
        self.total[...] = self.parts[self.place]
        for way, (behind, _) in enumerate(self.ways):

            @pl.when(behind > 0)
            def _():
                block = self.received.at[way, self.far - 1]
                wait_for(block, self.recv_sem.at[way, self.far - 1])
                self.total[...] = self.total[...] + block[...]

    def finish(self):
        for way, (behind, _) in enumerate(self.ways):
            for slot in range(0 if self.ahead is None else 1, self.far):

                @pl.when(behind <= slot)
                def _():
                    self.copy(way, slot, self.parts.at[0]).wait_send()


class LineShare:
    def __init__(self, own, out, sems):
        self.own, self.out = own, out
        self.send_sem, self.recv_sem, home_sem = sems
        self.place = lax.axis_index(TENSOR)
        self.home = pltpu.make_async_copy(own, out.at[self.place], home_sem)
        self.far = lax.axis_size(TENSOR) - 1
        self.ways = (
            (self.place, self.place + 1, -1),
            (self.far - self.place, self.place - 1, 1),
        )

    def copy(self, way, slot):
        block = self.out.at[self.place + self.ways[way][2] * slot]
        return pltpu.make_async_remote_copy(
            src_ref=block if slot else self.own,
            dst_ref=block,
            send_sem=self.send_sem.at[way, slot],
            recv_sem=self.recv_sem.at[way, slot],
            device_id={TENSOR: self.ways[way][1]},
            device_id_type=pl.DeviceIdType.MESH,
        )

    def slot(self, slot):
        if slot == 0:
            self.home.start()
        for way, (behind, _, step) in enumerate(self.ways):
            if slot:

                @pl.when(behind >= slot)
                def _():
                    block = self.out.at[self.place + step * slot]
                    wait_for(block, self.recv_sem.at[way, slot - 1])

            if slot < self.far:

                @pl.when((behind >= slot) & (behind < self.far))
                def _():
                    self.copy(way, slot).start()

    def finish(self):
        self.slot(self.far)
        self.home.wait()
        for way, (behind, _, _) in enumerate(self.ways):
            for slot in range(self.far):

                @pl.when((behind >= slot) & (behind < self.far))
                def _():
                    self.copy(way, slot).wait_send()


def line_sems(places):
    dma = pltpu.SemaphoreType.DMA
    return [dma((2, places - 1)), dma((2, places - 1))]


class Exchange:
    def __init__(self, grads, momentum, sums, whole, scratch, sems):
        self.grads, self.momentum, self.sums, self.whole = grads, momentum, sums, whole
        (
            self.from_core, self.merged, self.low, self.from_z, self.from_z_small, self.direction,
        ) = scratch
        (
            self.own_sem, self.core_send, self.core_recv, self.z_send, self.z_recv,
            self.xy_send, self.xy_recv, self.pass_send, self.pass_recv,
        ) = sems
        self.core, self.tensor = lax.axis_index(DP), lax.axis_index(TENSOR)
        self.head, self.places = lax.axis_index(HEADS), lax.axis_size(TENSOR)
        self.along = neighbours(self.tensor, self.places)
        self.across = square_peers(self.head)
        self.rows = momentum.shape[0]
        self.started = []

    def send(self, *args):
        self.started.append(send(*args))

    def start(self):
        self.send(
            self.grads.at[1 - self.core], self.from_core, self.core_send, self.core_recv,
            {DP: 1 - self.core},
        )

    def along_tensor(self):
        rows = self.rows
        wait_for(self.from_core, self.core_recv)
        for place in range(self.places):
            both = self.grads[self.core, place] + self.from_core[place]
            self.merged[place] = both
            self.low[place] = both[:rows].astype(self.low.dtype)
        others = len(self.along)
        for step, peer in enumerate(self.along):
            self.send(
                self.low.at[peer], self.from_z.at[step], self.z_send.at[step],
                self.z_recv.at[step], {TENSOR: peer},
            )
            self.send(
                self.merged.at[peer, pl.ds(rows, self.from_z_small.shape[1])],
                self.from_z_small.at[step], self.z_send.at[others + step],
                self.z_recv.at[others + step], {TENSOR: peer},
            )

    def share(self):
        rows, others = self.rows, len(self.along)
        grad = self.merged[self.tensor, :rows, :]
        small = self.merged[self.tensor, rows:, :]
        for step in range(others):
            wait_for(self.from_z.at[step], self.z_recv.at[step])
            grad = grad + self.from_z[step].astype(jnp.float32)
            wait_for(self.from_z_small.at[step], self.z_recv.at[others + step])
            small = small + self.from_z_small[step]
        self.sums[:rows, :] = grad
        self.sums[rows:, :] = small
        momentum = momentum_decay * self.momentum[...] + grad
        self.direction[...] = grad + momentum_decay * momentum
        here = self.whole.at[self.core, self.head]
        self.home = pltpu.make_async_copy(self.direction, here, self.own_sem)
        self.home.start()
        for step, peer in enumerate(self.across):
            self.send(
                self.direction, here, self.xy_send.at[step], self.xy_recv.at[step],
                {HEADS: peer},
            )
        self.send(
            self.direction, here, self.pass_send.at[0], self.pass_recv.at[0],
            {DP: 1 - self.core},
        )

    def finish(self):
        for step, peer in enumerate(self.across):
            block = self.whole.at[self.core, peer]
            wait_for(block, self.xy_recv.at[step])
            self.send(
                block, block, self.pass_send.at[step + 1], self.pass_recv.at[step + 1],
                {DP: 1 - self.core},
            )
        for step, peer in enumerate([self.head] + self.across):
            wait_for(self.whole.at[1 - self.core, peer], self.pass_recv.at[step])
        self.home.wait()
        for copy in self.started:
            copy.wait_send()


def exchange_scratch(places, heads, rows, momentum):
    f32, bf16 = jnp.float32, jnp.bfloat16
    dma = pltpu.SemaphoreType.DMA
    scratch = [
        pltpu.VMEM((places, rows, TILE), f32),
        pltpu.VMEM((places, rows, TILE), f32),
        pltpu.VMEM((places,) + momentum, bf16),
        pltpu.VMEM((places - 1,) + momentum, bf16),
        pltpu.VMEM((places - 1, rows - momentum[0], TILE), f32),
        pltpu.VMEM(momentum, f32),
    ]
    sems = [
        dma(()),
        dma(()),
        dma(()),
        dma((2 * (places - 1),)),
        dma((2 * (places - 1),)),
        dma((heads - 1,)),
        dma((heads - 1,)),
        dma((heads,)),
        dma((heads,)),
    ]
    return scratch, sems


class Combining:
    def __init__(self, payloads, out, exact_out, scratch, sems):
        self.payloads, self.out, self.exact_out = payloads, out, exact_out
        self.widths = [payload.shape[3] for payload in payloads]
        (
            self.stage, self.own, self.from_core, self.from_side, self.relay,
            self.from_next, self.low, self.from_z, self.done, *self.exact,
        ) = scratch
        (
            self.home_sem, self.core_send, self.core_recv, self.xy_send, self.xy_recv,
            self.z_send, self.z_recv, self.back_send, self.back_recv,
        ) = sems
        self.core, self.tensor = lax.axis_index(DP), lax.axis_index(TENSOR)
        self.head, self.places = lax.axis_index(HEADS), lax.axis_size(TENSOR)
        self.across = square_peers(self.head)
        self.order = neighbours(self.tensor, self.places) + [self.tensor]
        self.quarter = self.done.shape[0]
        self.started, self.homes, self.to_core = [], [], []
        self.result = None

    def send(self, *args):
        self.started.append(send(*args))

    def write(self, ref, number, pick, group):
        start = 0
        rows = pick.shape[0]
        for payload, width in zip(self.payloads, self.widths):
            slots = payload[:, group].reshape(-1, width)
            ref[number, :rows, start : start + width] = dot_low(pick, slots).astype(ref.dtype)
            start += width

    def spread(self, number, picks):
        self.write(self.stage, number, picks[1], 1 - self.core)
        self.to_core.append(
            send(
                self.stage.at[number], self.from_core.at[number], self.core_send.at[number],
                self.core_recv.at[number], {DP: 1 - self.core},
            )
        )
        self.write(self.own, number, picks[0], self.core)

    def sides(self, number):
        _, beside, above = self.across
        return (beside, above) if number % 2 == 0 else (above, beside)

    def rows(self, corner):
        return pl.ds(pl.multiple_of(corner * self.quarter, 16), self.quarter)

    def exchange(self, number):
        wait_for(self.from_core.at[number], self.core_recv.at[number])
        rows = self.from_core.shape[1]
        both = self.own[number, :rows] + self.from_core[number].astype(jnp.float32)
        self.own[number, :rows] = both
        self.to_core[number].wait_send()
        self.stage[number] = both.astype(jnp.bfloat16)
        side = self.sides(number)[0]
        for step, corner in enumerate((self.across[0], side)):
            place = 3 * number + step
            self.send(
                self.stage.at[number, self.rows(corner)], self.from_side.at[number, step],
                self.xy_send.at[place], self.xy_recv.at[place], {HEADS: side},
            )

    def pass_on(self, number):
        following = self.sides(number)[1]
        place = 3 * number
        wait_for(self.from_side.at[number, 0], self.xy_recv.at[place])
        both = self.own[number, self.rows(following), :]
        both = both + self.from_side[number, 0].astype(jnp.float32)
        self.relay[number] = both.astype(jnp.bfloat16)
        self.send(
            self.relay.at[number], self.from_next.at[number], self.xy_send.at[place + 2],
            self.xy_recv.at[place + 2], {HEADS: following},
        )

    def reduce(self, number):
        wait_for(self.from_side.at[number, 1], self.xy_recv.at[3 * number + 1])
        wait_for(self.from_next.at[number], self.xy_recv.at[3 * number + 2])
        both = self.own[number, self.rows(self.head), :]
        both = both + self.from_side[number, 1].astype(jnp.float32)
        both = both + self.from_next[number].astype(jnp.float32)
        if number == self.places - 1:
            self.result = both
            return
        self.low[number] = both.astype(jnp.bfloat16)
        self.send(
            self.low.at[number], self.from_z.at[number], self.z_send.at[number],
            self.z_recv.at[number], {TENSOR: self.order[number]},
        )

    def share(self):
        result = self.result
        for number in range(self.places - 1):
            wait_for(self.from_z.at[number], self.z_recv.at[number])
            result = result + self.from_z[number].astype(jnp.float32)
        main = self.done.shape[1]
        self.done[...] = result[:, :main].astype(jnp.bfloat16)
        parts = [(self.done, self.out)]
        if self.exact:
            self.exact[0][...] = result[:, main:]
            parts.append((self.exact[0], self.exact_out))
        for which, (source, out) in enumerate(parts):
            here = out.at[self.head]
            home = pltpu.make_async_copy(source, here, self.home_sem.at[which])
            home.start()
            self.homes.append(home)
            for step, peer in enumerate(self.across):
                number = which * len(self.across) + step
                self.send(
                    source, here, self.back_send.at[number], self.back_recv.at[number],
                    {HEADS: peer},
                )

    def finish(self):
        outs = [self.out] + ([self.exact_out] if self.exact else [])
        for which, out in enumerate(outs):
            for step, peer in enumerate(self.across):
                number = which * len(self.across) + step
                wait_for(out.at[peer], self.back_recv.at[number])
        for home in self.homes:
            home.wait()
        for copy in self.started:
            copy.wait_send()


def combining_scratch(places, rows, quarter, widths, exact, room=0):
    wide = sum(widths)
    main = wide - (widths[-1] if exact else 0)
    f32, bf16 = jnp.float32, jnp.bfloat16
    dma = pltpu.SemaphoreType.DMA
    scratch = [
        pltpu.VMEM((places, rows, wide), bf16),
        pltpu.VMEM((places, max(rows, room), wide), f32),
        pltpu.VMEM((places, rows, wide), bf16),
        pltpu.VMEM((places, 2, quarter, wide), bf16),
        pltpu.VMEM((places, quarter, wide), bf16),
        pltpu.VMEM((places, quarter, wide), bf16),
        pltpu.VMEM((places - 1, quarter, wide), bf16),
        pltpu.VMEM((places - 1, quarter, wide), bf16),
        pltpu.VMEM((quarter, main), bf16),
    ]
    if exact:
        scratch.append(pltpu.VMEM((quarter, wide - main), f32))
    sems = [
        dma((2,)),
        dma((places,)),
        dma((places,)),
        dma((places * 3,)),
        dma((places * 3,)),
        dma((places - 1,)),
        dma((places - 1,)),
        dma((6,)),
        dma((6,)),
    ]
    return scratch, sems


def halves(values):
    lanes = lax.broadcasted_iota(jnp.int32, values.shape, 1)
    zero = jnp.zeros_like(values)
    return jnp.where(lanes < HEAD_DIM, values, zero), jnp.where(lanes < HEAD_DIM, zero, values)


def join_heads(first, second):
    lanes = lax.broadcasted_iota(jnp.int32, first.shape, 1)
    return jnp.where(lanes < HEAD_DIM, first, second)


def probabilities(query, keys):
    scores = dot_low(query, keys, ((1,), (1,))) * HEAD_DIM ** (-0.5)
    lanes = lax.broadcasted_iota(jnp.int32, scores.shape, 1)
    scores = jnp.where(lanes < SEQ, scores, -1e30)
    raised = jnp.exp(scores - jnp.max(scores, axis=1, keepdims=True))
    return raised / jnp.sum(raised, axis=1, keepdims=True)


def wide_rows(low_ref, first_row, rows):
    cores, places, _, _, tile = low_ref.shape
    shards = [low_ref[c, t, 0, first_row : first_row + rows, :] for c in range(cores) for t in range(places)]
    shards = [shard.astype(jnp.float32) for shard in shards]
    lanes = lax.broadcasted_iota(jnp.int32, (rows, tile), 1)
    tiles = []
    for left, right in zip(shards[::2], shards[1::2]):
        tiles.append(jnp.where(lanes < tile // 2, left, pltpu.roll(right, tile // 2, 1)))
    return jnp.concatenate(tiles, axis=1)


def front_kernel(slots, flat_ref, images_ref, cot_ref, ids_ref, *refs):
    outs, refs = refs[:11], refs[11:]
    results, refs = refs[:11], refs[11:]
    (
        qkv_out, mixed_out, first_out, normed_out, router_out, gains_out, weights_out,
        slot_in_out, slot_cot_out, member_out, column_out,
    ) = results
    low_ref, all_normed, all_cot, all_ids, ranks, picks, members, normed, mixed, *sems = refs
    leaving = []

    def leave(*numbers):
        for number in numbers:
            copy = pltpu.make_async_copy(results[number], outs[number], sems[22].at[number])
            copy.start()
            leaving.append(copy)

    images, padded, width = images_ref.shape
    cores, places, heads, _, tile = low_ref.shape
    f32, bf16 = jnp.float32, jnp.bfloat16
    core, head_index = lax.axis_index(DP), lax.axis_index(HEADS)
    block = width // cores
    quarter = cot_ref.shape[1]
    per = heads // images
    own_normed = normed_out.at[
        lax.div(head_index, per),
        pl.ds(pl.multiple_of(lax.rem(head_index, per) * quarter, 16), quarter),
    ]
    sharing_low = Sharing(flat_ref, low_ref, sems[:7])
    sharing_cot = Sharing(cot_ref.at[head_index], all_cot, sems[7:14])
    sharing_normed = Sharing(own_normed, all_normed, sems[14:21])
    ids_sems = sems[21]
    enter(
        [{TENSOR: peer} for peer in sharing_low.along]
        + [{HEADS: sharing_low.beside}, {HEADS: sharing_low.above}, {DP: 1 - core}]
    )
    sharing_low.start()
    ids_home = pltpu.make_async_copy(ids_ref, all_ids.at[core], ids_sems.at[0])
    ids_home.start()
    ids_copy = send(
        ids_ref, all_ids.at[core], ids_sems.at[1], ids_sems.at[2], {DP: 1 - core}
    )
    sharing_low.pass_to_sides()
    sharing_cot.start()
    ids_home.wait()
    wait_for(all_ids.at[1 - core], ids_sems.at[2])
    slot_places(slots, all_ids, ranks, column_out)
    sharing_low.pass_round()
    experts = slot_in_out.shape[0]
    groups = cores
    for group in range(groups):
        for e in range(experts):
            rank = ranks[e * groups + group : e * groups + group + 1, :]
            place = lax.broadcasted_iota(jnp.int32, (slots, rank.shape[1]), 0)
            picks[group, e * slots : (e + 1) * slots, :] = jnp.where(
                rank == place, 1.0, 0.0
            ).astype(bf16)
        lanes = lax.broadcasted_iota(jnp.int32, members.shape[1:], 1)
        start = (groups + group) * TOP
        hit = lanes == column_out[:, start : start + 1]
        for k in range(1, TOP):
            hit = hit | (lanes == column_out[:, start + k : start + k + 1])
        members[group] = jnp.where(hit, 1.0, 0.0).astype(bf16)
    for group in range(groups):
        part = dot_low(picks[group], members[group])
        for e in range(experts):
            member_out[e, group] = part[e * slots : (e + 1) * slots]
    leave(9, 10)
    sharing_cot.pass_to_sides()
    sharing_low.own_group()
    sharing_low.other_group()

    for matrix in range(4):
        for c in range(cores):
            for head in range(heads):
                start = matrix * width + head * tile
                weights_out[c * block : (c + 1) * block, start : start + tile] = low_ref[
                    c, matrix, head, :block, :
                ]
    small = wide_rows(low_ref, block, ceil_to(EXPERTS + 4, 16))
    router_out[...] = small[:EXPERTS].astype(bf16)
    gains = small[EXPERTS : EXPERTS + 8]
    gains_out[...] = gains
    leave(4, 5, 6)
    def attend(image):
        tokens = images_ref[image].astype(f32)
        here, _, _ = norm_forward(tokens, gains[0:1], gains[1:2])
        normed[...] = here.astype(bf16)
        for matrix in range(3):
            part = dot_low(normed[...], weights_out[:, matrix * width : (matrix + 1) * width])
            part = part.astype(bf16)
            for head in range(heads):
                qkv_out[matrix, head, image] = part[:, head * tile : (head + 1) * tile]
        for head in range(heads):
            keys = qkv_out[1, head, image]
            total = None
            for query, value in zip(
                halves(qkv_out[0, head, image]), halves(qkv_out[2, head, image])
            ):
                probs = probabilities(query, keys).astype(bf16)
                part = dot_low(probs, value)
                total = part if total is None else total + part
            mixed_out[head, image] = total.astype(bf16)
            mixed[:, head * tile : (head + 1) * tile] = total.astype(bf16)
        attended = dot_low(mixed[...], weights_out[:, 3 * width :], ((1,), (1,)))
        first = tokens + attended
        first_out[image] = first
        here, _, _ = norm_forward(first, gains[2:3], gains[3:4])
        normed_out[image] = here.astype(bf16)

    own_image = lax.div(head_index, per)
    attend(own_image)
    sharing_normed.start()
    sharing_cot.pass_round()
    for step in range(1, images):
        attend(lax.rem(own_image + step, images))

    def dispatch(source, out, group):
        rows = places * heads * quarter
        part = dot_low(picks[group], source[group].reshape(rows, width)).astype(bf16)
        for e in range(experts):
            out[e, group] = part[e * slots : (e + 1) * slots]

    sharing_normed.pass_to_sides()
    leave(0, 1, 2, 3)
    sharing_cot.own_group()
    sharing_normed.pass_round()
    dispatch(all_cot, slot_cot_out, core)
    sharing_cot.other_group()
    dispatch(all_cot, slot_cot_out, 1 - core)
    leave(8)
    sharing_normed.own_group()
    dispatch(all_normed, slot_in_out, core)
    sharing_normed.other_group()
    dispatch(all_normed, slot_in_out, 1 - core)
    leave(7)
    for copy in leaving:
        copy.wait()
    ids_copy.wait_send()
    for sharing in (sharing_low, sharing_cot, sharing_normed):
        sharing.finish()


def run_front(flat, images, cot, ids, experts, slots, number):
    count, padded, width = images.shape
    groups, heads = lax.axis_size(DP), lax.axis_size(HEADS)
    places, _, rows = ids.shape
    tokens = places * rows
    quarter = cot.shape[1]
    f32, bf16 = jnp.float32, jnp.bfloat16
    shape = jax.ShapeDtypeStruct
    dma = pltpu.SemaphoreType.DMA
    vmem, anywhere = pl.BlockSpec(memory_space=pltpu.VMEM), pl.BlockSpec(memory_space=pl.ANY)
    results = [
        shape((3, heads, count, padded, TILE), bf16),
        shape((heads, count, padded, TILE), bf16),
        shape((count, padded, width), f32),
        shape((count, padded, width), bf16),
        shape((EXPERTS, width), bf16),
        shape((8, width), f32),
        shape((width, 4 * width), bf16),
        shape((experts, groups, slots, width), bf16),
        shape((experts, groups, slots, width), bf16),
        shape((experts, groups, slots, EXPERTS), f32),
        shape((tokens, 2 * groups * TOP), jnp.int32),
    ]
    return pl.pallas_call(
        functools.partial(front_kernel, slots),
        in_specs=[anywhere, vmem, anywhere, anywhere],
        out_specs=[anywhere] * 11,
        out_shape=results,
        scratch_shapes=[pltpu.VMEM(result.shape, result.dtype) for result in results]
        + [
            pltpu.VMEM((groups, places, heads) + flat.shape, bf16),
            pltpu.VMEM((groups, places, heads, quarter, width), bf16),
            pltpu.VMEM((groups, places, heads, quarter, width), bf16),
            pltpu.VMEM((groups,) + ids.shape, jnp.int32),
            pltpu.VMEM((experts * groups, tokens), jnp.int32),
            pltpu.VMEM((groups, experts * slots, tokens), bf16),
            pltpu.VMEM((groups, tokens, EXPERTS), bf16),
            pltpu.VMEM((padded, width), bf16),
            pltpu.VMEM((padded, width), bf16),
        ]
        + sharing_sems(places, heads) * 3
        + [dma((3,)), dma((11,))],
        compiler_params=pltpu.CompilerParams(
            collective_id=number, has_side_effects=True, vmem_limit_bytes=VMEM_LIMIT
        ),
        name="front",
    )(flat, images, cot, ids)


def attend_back(
    back_ref, gate_ref, cot_ref, columns_ref, images_ref, first_ref, normed_b_ref, mixed_ref,
    qkv_ref, router_ref, gains_ref, weights_ref, input_out, grads_out,
    normed_a, branch, mixed_grad, qkv_grad, own_grad, between,
):
    images, padded, width = images_ref.shape
    heads, tile = mixed_ref.shape[0], mixed_ref.shape[3]
    cores = grads_out.shape[0]
    f32, bf16 = jnp.float32, jnp.bfloat16
    core = lax.axis_index(DP)
    head_index = lax.axis_index(HEADS)
    tensor = lax.axis_index(TENSOR)
    block = width // cores
    gains = gains_ref[...]
    router = router_ref[...]
    router_grad = jnp.zeros((EXPERTS, width), f32)
    sums = [jnp.zeros((1, width), f32) for _ in range(4)]
    for image in range(images):
        per = back_ref.shape[0] // images
        quarters = range(image * per, (image + 1) * per)
        back = jnp.concatenate([back_ref[q] for q in quarters], axis=0).astype(f32)
        parts = jnp.concatenate([gate_ref[q] for q in quarters], axis=0)
        columns = columns_ref[tensor, image * padded : (image + 1) * padded, :]
        ids = [
            jnp.where(core == 0, columns[:, 4 + k : 5 + k], columns[:, 6 + k : 7 + k])
            for k in range(TOP)
        ]
        lanes = lax.broadcasted_iota(jnp.int32, (padded, EXPERTS), 1)
        chosen = jnp.where((lanes == ids[0]) | (lanes == ids[1]), 1.0, 0.0)
        normed_b = normed_b_ref[image]
        logits = dot_low(normed_b, router, ((1,), (1,)))
        peak = jnp.max(jnp.where(chosen > 0, logits, -1e30), axis=1, keepdims=True)
        raised = jnp.exp(jnp.where(chosen > 0, logits - peak, -1e30))
        any_chosen = jnp.max(chosen, axis=1, keepdims=True)
        gates = raised / (jnp.sum(raised, axis=1, keepdims=True) + (1.0 - any_chosen))
        gate_grad = (parts + pltpu.roll(parts, tile - EXPERTS, 1))[:, :EXPERTS]
        blend = jnp.sum(gates * gate_grad, axis=1, keepdims=True)
        logit_grad = (gates * (gate_grad - blend)).astype(bf16)
        normed_grad = back + dot_low(logit_grad, router)
        router_grad = router_grad + dot_low(logit_grad, normed_b, ((0,), (0,)))
        _, scaled, inverse = norm_forward(first_ref[image], gains[2:3], gains[3:4])
        sums[2] = sums[2] + jnp.sum(normed_grad * scaled, axis=0, keepdims=True)
        sums[3] = sums[3] + jnp.sum(normed_grad, axis=0, keepdims=True)
        first_grad = cot_ref[image].astype(f32) + norm_backward(
            normed_grad, scaled, inverse, gains[2:3]
        )
        input_out[image] = first_grad
        branch[image] = first_grad.astype(bf16)
        mixed_grad[...] = dot_low(branch[image], weights_ref[:, 3 * width :]).astype(bf16)
        for head in range(heads):
            query, keys = qkv_ref[0, head, image], qkv_ref[1, head, image]
            values = qkv_ref[2, head, image]
            out_grad = mixed_grad[:, head * tile : (head + 1) * tile]
            query_grads, key_grads, value_grad = [], [], None
            for query_half, grad_half in zip(halves(query), halves(out_grad)):
                probs = probabilities(query_half, keys)
                prob_grad = dot_low(grad_half, values, ((1,), (1,)))
                part = dot_low(probs.astype(bf16), grad_half, ((0,), (0,)))
                value_grad = part if value_grad is None else value_grad + part
                score_grad = (
                    probs * (prob_grad - jnp.sum(probs * prob_grad, axis=1, keepdims=True))
                ).astype(bf16)
                query_grads.append(dot_low(score_grad, keys))
                key_grads.append(dot_low(score_grad, query, ((0,), (0,))))
            scale = HEAD_DIM ** (-0.5)
            for matrix, grad in enumerate(
                (join_heads(*query_grads) * scale, join_heads(*key_grads) * scale, value_grad)
            ):
                grad = grad.astype(bf16)
                start = matrix * width + head * tile
                qkv_grad[:, start : start + tile] = grad
                own_grad[matrix, head, image * padded : (image + 1) * padded, :] = grad
            for work in between.get((image, head), ()):
                work()
        normed_grad = dot_low(qkv_grad[...], weights_ref[:, : 3 * width], ((1,), (1,)))
        here, scaled, inverse = norm_forward(
            images_ref[image].astype(f32), gains[0:1], gains[1:2]
        )
        normed_a[image] = here.astype(bf16)
        sums[0] = sums[0] + jnp.sum(normed_grad * scaled, axis=0, keepdims=True)
        sums[1] = sums[1] + jnp.sum(normed_grad, axis=0, keepdims=True)
        input_out[image] = input_out[image] + norm_backward(
            normed_grad, scaled, inverse, gains[0:1]
        )
    rows = images * padded
    left = normed_a[...].reshape(rows, width)
    for matrix in range(4):
        if matrix < 3:
            grad = dot_low(left, own_grad[matrix, head_index], ((0,), (0,)))
        else:
            own_mixed = mixed_ref[head_index].reshape(rows, tile)
            grad = dot_low(branch[...].reshape(rows, width), own_mixed, ((0,), (0,)))
        for c in range(cores):
            grads_out[c, matrix, :block, :] = grad[c * block : (c + 1) * block]
    pad = grads_out.shape[2] - block - EXPERTS - 4
    small = jnp.concatenate([router_grad] + sums + [jnp.zeros((pad, width), f32)], axis=0)
    places = grads_out.shape[1]
    for c in range(cores):
        for t in range(places):
            shard = c * places + t
            piece = small[:, shard // 2 * tile : (shard // 2 + 1) * tile]
            if shard % 2:
                piece = pltpu.roll(piece, tile // 2, 1)
            grads_out[c, t, block:, :] = piece


def attn_polish(whole_ref, weights_ref, out_ref, values, gram, poly, between=()):
    cores, heads, block, tile = whole_ref.shape
    width = values.shape[0]
    half = width // 2
    core, head_index = lax.axis_index(DP), lax.axis_index(HEADS)
    squares = jnp.zeros((1, 1), jnp.float32)
    for c in range(cores):
        for h in range(heads):
            part = whole_ref[c, h]
            squares = squares + jnp.sum(part * part, keepdims=True)
    factor = 1.0 / (jnp.sqrt(squares) + 1e-07)
    for c in range(cores):
        for h in range(heads):
            values[c * block : (c + 1) * block, h * tile : (h + 1) * tile] = whole_ref[c, h] * factor

    def store(ref, upper, corner):
        ref[:half, :] = upper
        ref[half:, half:] = corner
        ref[half:, :half] = upper[:, half:].T

    def product(left, right, contract):
        return lax.dot_general(
            left, right, (contract, ((), ())),
            precision=lax.Precision.HIGH, preferred_element_type=jnp.float32,
        )

    for step in range(ITERS):
        across = ((1,), (1,))
        store(
            gram,
            product(values[:half, :], values[...], across),
            product(values[half:, :], values[half:, :], across),
        )
        along = ((1,), (0,))
        upper = product(gram[:half, :], gram[...], along)
        corner = product(gram[half:, :], gram[:, half:], along)
        store(
            poly,
            coef_second * gram[:half, :] + coef_third * upper,
            coef_second * gram[half:, half:] + coef_third * corner,
        )
        values[...] = coef_first * values[...] + product(poly[...], values[...], along)
        if step == ITERS // 2:
            for work in between:
                work()
    scale = muon_scale(width, heads * tile)
    for c in range(cores):
        for h in range(heads):

            @pl.when((core == c) & (head_index == h))
            def _():
                own = values[c * block : (c + 1) * block, h * tile : (h + 1) * tile]
                out_ref[...] = weights_ref[...] * (1.0 - muon_rate * muon_decay) - scale * own


def back_kernel(
    scale, gram_first, ahead_right, ahead_left, columns, back, gates, router, gains, momentum,
    attn_weights, *refs,
):
    late, refs = refs[:9], refs[9:]
    (
        directions, expert_weights, ahead_out, input_out, sums_out, attn_out, share_first,
        share_second, expert_out, *refs,
    ) = refs
    loaded, refs = refs[:9], refs[9:]
    ahead, gram_second, weights, qkv, first, cot, images, normed_b, mixed = loaded
    (
        back_total, gates_total, received_first, received_second, total_first, total_second,
        polish_gram, polish_poly, polish_product, grads, normed_a, branch, mixed_grad, qkv_grad,
        own_grad, whole, load_sem, apply_sem, *refs,
    ) = refs
    loading = [
        pltpu.make_async_copy(source, target, load_sem.at[number])
        for number, (source, target) in enumerate(zip(late, loaded))
    ]
    for copy in loading:
        copy.start()
    refs = list(refs)

    def take(count):
        taken = refs[:count]
        del refs[:count]
        return taken

    combine_back = Combining((back, gates), back_total, gates_total, take(10), take(9))
    combine_ahead = Combining((ahead,), ahead_out, None, take(9), take(9))
    reduce_first = LineReduce(
        gram_first, received_first, total_first, take(2), (ahead_right, ahead_left)
    )
    reduce_second = LineReduce(gram_second, received_second, total_second, take(2))
    line_first = LineShare(total_first, share_first, take(3))
    line_second = LineShare(total_second, share_second, take(3))
    exchange = Exchange(grads, momentum, sums_out, whole, take(6), take(9))
    core = lax.axis_index(DP)
    places, rows, _ = columns.shape
    experts, _, slots, _ = back.shape
    lanes_total = experts * slots
    enter(
        [{TENSOR: peer} for peer in combine_back.order[:-1]]
        + [{HEADS: peer} for peer in combine_back.across]
        + [{DP: 1 - core}]
    )

    def pick(group, place):
        table = columns[place]
        lanes = lax.broadcasted_iota(jnp.int32, (rows, lanes_total), 1)
        hit = None
        for k in range(TOP):
            code = jnp.where(group == 0, table[:, k : k + 1], table[:, TOP + k : TOP + k + 1])
            here = code == lanes
            hit = here if hit is None else hit | here
        return jnp.where(hit, 1.0, 0.0).astype(jnp.bfloat16)

    reduce_first.slot(1)
    last = places - 1
    for number, place in enumerate(combine_back.order):
        combine_back.spread(number, (pick(core, place), pick(1 - core, place)))
        if number > 0:
            combine_back.exchange(number - 1)
        if number > 1:
            combine_back.pass_on(number - 2)
    combine_back.exchange(last)
    reduce_first.slot(2)
    loading[0].wait()
    for number, place in enumerate(combine_back.order):
        combine_ahead.spread(number, (pick(core, place), pick(1 - core, place)))
        if number >= 2:
            combine_back.pass_on(last - 3 + number)
    for copy in loading[1:]:
        copy.wait()
    reduce_first.final()
    reduce_second.slot(0)
    polish_refs = (polish_gram, polish_poly, polish_product)
    polish(
        total_first, total_first, *polish_refs,
        between=(lambda: [combine_back.reduce(number) for number in range(places)],),
    )
    line_first.slot(0)
    combine_back.share()
    reduce_second.slot(1)
    combine_back.finish()
    between = {
        (0, 0): (lambda: [combine_ahead.exchange(number) for number in range(places)],),
        (0, 3): (lambda: line_first.slot(1),),
        (1, 0): (lambda: [combine_ahead.pass_on(number) for number in range(places)],),
        (1, 2): (lambda: reduce_second.slot(2),),
    }
    attend_back(
        back_total, gates_total, cot, columns, images, first, normed_b, mixed, qkv, router, gains,
        weights, input_out, grads, normed_a, branch, mixed_grad, qkv_grad, own_grad, between,
    )
    exchange.start()
    line_first.slot(2)
    for number in range(places):
        combine_ahead.reduce(number)
    exchange.along_tensor()
    reduce_second.final()
    packed_bufs = [received_first.at[0, 0], received_first.at[0, 1]]
    own = combine_back.own
    width = polish_gram.shape[0]
    views = [own.at[k, pl.ds(0, width), pl.ds(0, width)] for k in range(4)]
    fetched, stored = {}, {}

    def fetch(m):
        k = m % 2
        fetched[m] = [
            pltpu.make_async_copy(source, target, apply_sem.at[3 * k + which])
            for which, (source, target) in enumerate(
                (
                    (share_first.at[m], packed_bufs[k]),
                    (directions.at[m], views[k]),
                    (expert_weights.at[m], views[2 + k]),
                )
            )
        ]
        for copy in fetched[m]:
            copy.start()

    def new_matrix(m):
        k = m % 2
        for copy in fetched[m]:
            copy.wait()
        unpack_upper(packed_bufs[k], polish_poly)
        ortho = dot_exact(polish_poly[...], views[k][...])
        views[2 + k][...] = views[2 + k][...] * (1.0 - muon_rate * muon_decay) - scale * ortho
        stored[m] = pltpu.make_async_copy(views[2 + k], expert_out.at[m], apply_sem.at[6 + k])
        stored[m].start()

    def prepare():
        line_first.finish()
        reduce_first.finish()
        fetch(0)
        fetch(1)

    polish(total_second, total_second, *polish_refs, between=(prepare,))
    line_second.slot(0)
    for m in range(places):
        new_matrix(m)
        if m + 2 < places:
            stored[m].wait()
            fetch(m + 2)
    exchange.share()
    line_second.slot(1)
    combine_ahead.share()
    exchange.finish()
    attn_polish(
        whole, attn_weights, attn_out, *polish_refs, between=(lambda: line_second.slot(2),)
    )
    for m in range(places - 2, places):
        stored[m].wait()
    combine_ahead.finish()
    reduce_second.finish()
    line_second.finish()


def run_back(
    grams, sent, columns, back, gates, ahead, cot, images, first, normed_b, mixed, qkv, router,
    gains, weights, momentum, attn_weights, direction, expert_weights, scale, rows, number,
):
    places, block_rows, _ = columns.shape
    groups, heads = lax.axis_size(DP), lax.axis_size(HEADS)
    count, padded, width = images.shape
    quarter = block_rows // heads
    extra = gates.shape[3]
    f32, bf16 = jnp.float32, jnp.bfloat16
    shape = jax.ShapeDtypeStruct
    vmem, anywhere = pl.BlockSpec(memory_space=pltpu.VMEM), pl.BlockSpec(memory_space=pl.ANY)
    back_scratch, back_sems = combining_scratch(
        places, block_rows, quarter, (width, extra), True, width
    )
    ahead_scratch, ahead_sems = combining_scratch(places, block_rows, quarter, (width,), False)
    gram = grams[0].shape[1:]
    exchange_refs, exchange_sems = exchange_scratch(places, heads, rows, momentum.shape)
    early = (
        grams[0], *sent, columns, back, gates, router, gains, momentum, attn_weights,
    )
    late = (ahead, grams[1], weights, qkv, first, cot, images, normed_b, mixed)
    return pl.pallas_call(
        functools.partial(back_kernel, scale),
        in_specs=[vmem] * len(early) + [anywhere] * (len(late) + 2),
        out_specs=[anywhere] + [vmem] * 3 + [anywhere] * 3,
        out_shape=[
            shape((heads, quarter, width), bf16),
            shape((count, padded, width), f32),
            shape((rows, TILE), f32),
            shape(attn_weights.shape, f32),
            shape((places,) + gram, f32),
            shape((places,) + gram, f32),
            shape((places,) + expert_weights.shape[1:], f32),
        ],
        scratch_shapes=[pltpu.VMEM(values.shape, values.dtype) for values in late]
        + [
            pltpu.VMEM((heads, quarter, width), bf16),
            pltpu.VMEM((heads, quarter, extra), f32),
            pltpu.VMEM((2, places - 1) + gram, f32),
            pltpu.VMEM((2, places - 1) + gram, f32),
            pltpu.VMEM(gram, f32),
            pltpu.VMEM(gram, f32),
            pltpu.VMEM((width, width), f32),
            pltpu.VMEM((width, width), f32),
            pltpu.VMEM((width, width), f32),
            pltpu.VMEM((groups, places, rows, TILE), f32),
            pltpu.VMEM((count, padded, width), bf16),
            pltpu.VMEM((count, padded, width), bf16),
            pltpu.VMEM((padded, width), bf16),
            pltpu.VMEM((padded, 3 * width), bf16),
            pltpu.VMEM((3, heads, count * padded, TILE), bf16),
            pltpu.VMEM((groups, heads) + momentum.shape, f32),
            pltpu.SemaphoreType.DMA((len(late),)),
            pltpu.SemaphoreType.DMA((8,)),
        ]
        + back_scratch
        + back_sems
        + ahead_scratch
        + ahead_sems
        + line_sems(places) * 2
        + (line_sems(places) + [pltpu.SemaphoreType.DMA(())]) * 2
        + exchange_refs
        + exchange_sems,
        compiler_params=pltpu.CompilerParams(
            collective_id=number, has_side_effects=True, vmem_limit_bytes=VMEM_LARGE
        ),
        name="back",
    )(*early, *late, direction, expert_weights)


def slot_places(slots, ids_ref, rank_out, column_out):
    groups, places, _, rows = ids_ref.shape
    experts = rank_out.shape[0] // groups
    labels = [own_label(experts, e).astype(jnp.float32) for e in range(experts)]
    wide = ceil_to(rows, TILE)
    earlier = lax.broadcasted_iota(jnp.int32, (rows, rows), 0)
    later = lax.broadcasted_iota(jnp.int32, (rows, rows), 1)
    before = jnp.where(earlier < later, 1.0, 0.0).astype(jnp.bfloat16)
    running = jnp.zeros((groups * experts, 1), jnp.float32)
    ranks = []
    for place in range(places):
        ids = [
            ids_ref[g, place, k : k + 1, :].astype(jnp.float32)
            for g in range(groups)
            for k in range(TOP)
        ]
        marks = []
        for e in range(experts):
            for g in range(groups):
                hit = ids[TOP * g] == labels[e]
                for k in range(1, TOP):
                    hit = hit | (ids[TOP * g + k] == labels[e])
                marks.append(jnp.where(hit, 1.0, 0.0))
        marks = jnp.concatenate(marks, axis=0)
        rank = running + dot_low(marks.astype(jnp.bfloat16), before)
        running = running + jnp.sum(marks, axis=1, keepdims=True)
        rank = jnp.where(marks > 0, rank, -1.0)
        ranks.append(rank)
        codes = []
        for g in range(groups):
            for k in range(TOP):
                code = jnp.full((1, rows), -1.0, jnp.float32)
                for e in range(experts):
                    own = ids[TOP * g + k] == labels[e]
                    number = e * groups + g
                    code = jnp.where(own, rank[number : number + 1] + float(slots * e), code)
                codes.append(code)
        both = jnp.concatenate(codes + ids, axis=0)
        columns = both.shape[0]
        both = jnp.concatenate(
            [both, jnp.zeros((columns, wide - rows), jnp.float32)], axis=1
        )
        both = jnp.concatenate([both, jnp.zeros((TILE - columns, wide), jnp.float32)], axis=0)
        for start in range(0, rows, TILE):
            turned = both[:, start : start + TILE].T
            count = min(TILE, rows - start)
            column_out[place * rows + start : place * rows + start + count, :] = turned[
                :count, :columns
            ].astype(jnp.int32)
    rank_out[...] = jnp.concatenate(ranks, axis=1).astype(jnp.int32)


def last_kernel(scale, made_ref, packed_ref, dir_ref, weight_ref, out_ref, whole):
    out_ref[0, 0] = made_ref[0]
    unpack_upper(packed_ref.at[0], whole)
    ortho = dot_exact(whole[...], dir_ref[0])
    out_ref[1, 0] = weight_ref[0] * (1.0 - muon_rate * muon_decay) - scale * ortho


def run_last(scale, made, packed, direction, weights):
    mats, width, hidden = weights.shape
    count = mats // 2
    block = (1, width, hidden)

    def here(m):
        return (m, 0, 0)

    both = pl.pallas_call(
        functools.partial(last_kernel, scale),
        grid=(count,),
        in_specs=[
            pl.BlockSpec(block, here),
            pl.BlockSpec((1,) + packed.shape[1:], here),
            pl.BlockSpec(block, here),
            pl.BlockSpec(block, lambda m: (count + m, 0, 0)),
        ],
        out_specs=pl.BlockSpec((2,) + block, lambda m: (0, m, 0, 0)),
        out_shape=jax.ShapeDtypeStruct((2, count, width, hidden), jnp.float32),
        scratch_shapes=[pltpu.VMEM((width, width), jnp.float32)],
        compiler_params=pltpu.CompilerParams(vmem_limit_bytes=VMEM_LIMIT),
        name="last",
    )(made, packed, direction, weights)
    return both.reshape(weights.shape)


def shards_fast(
    images_in,
    attn_weights,
    attn_momentum,
    router_weight,
    router_first,
    router_second,
    expert_weights,
    expert_momentum,
    norm_params,
    norm_first,
    norm_second,
    expert_ids,
    cotangent,
):
    rows, width = images_in.shape
    dp_count = lax.axis_size(DP)
    head_count = lax.axis_size(HEADS)
    tensor_count = lax.axis_size(TENSOR)
    mats = expert_weights.shape[0]
    hidden_cols = expert_weights.shape[2]
    group_rows = expert_ids.shape[0]
    slots = ceil_to(3 * TOP * group_rows // (2 * EXPERTS), 16)
    images = rows // SEQ
    image_rows = ceil_to(SEQ, 16 * head_count // math.gcd(images, head_count))
    padded_rows = images * image_rows
    quarter = padded_rows // head_count
    bf16, f32 = jnp.bfloat16, jnp.float32

    def pad_images(values):
        values = values.reshape(-1, SEQ, values.shape[-1])
        return jnp.pad(values, ((0, 0), (0, image_rows - SEQ), (0, 0)))

    def drop_padding(values):
        return values.reshape(images, image_rows, -1)[:, :SEQ].reshape(rows, -1)

    attn_rows = attn_weights.size // TILE
    small = jnp.concatenate((router_weight.T, norm_params), axis=0).astype(bf16)
    small_rows, small_lanes = small.shape
    small = jnp.pad(
        small, ((0, ceil_to(small_rows, 16) - small_rows), (0, TILE - small_lanes))
    )
    flat = jnp.concatenate((attn_weights.astype(bf16).reshape(attn_rows, TILE), small), axis=0)
    padded_cot = pad_images(cotangent)
    padded_images = pad_images(images_in)
    own_ids = jnp.pad(
        expert_ids.reshape(-1, SEQ, TOP), ((0, 0), (0, image_rows - SEQ), (0, 0)), constant_values=-1
    )
    own_ids = jnp.transpose(own_ids.reshape(tensor_count, padded_rows, TOP), (0, 2, 1))
    experts_own = mats // 2

    (
        qkv, mixed, first, normed_b, router_low, gains, weights_low, slot_in, slot_cot, member, columns,
    ) = run_front(
        flat, padded_images, padded_cot.reshape(head_count, quarter, width), own_ids,
        experts_own, slots, 1,
    )

    step = tensor_count // 2
    earlier = ()
    directions, packed = [], []
    for start in range(0, experts_own, step):
        *earlier, direction, gram = run_experts(
            start, step, slot_in, slot_cot, member, router_low, expert_weights, expert_momentum,
            tuple(earlier),
        )
        directions.append(direction)
        packed.append(gram)
    expert_mom, back, gate_back, ahead = earlier
    places = columns.reshape(tensor_count, padded_rows, -1)

    def by_group(values):
        return values.reshape(experts_own, dp_count, slots, values.shape[-1])

    far = tensor_count - 1
    sent = (
        lax.ppermute(packed[0][far], TENSOR, [(0, 1)]),
        lax.ppermute(packed[0][0], TENSOR, [(far, far - 1)]),
    )
    scale = muon_scale(width, hidden_cols * tensor_count)
    ahead_total, input_grad, sums, attn_new, _, product, made = run_back(
        packed, sent, places, by_group(back), by_group(gate_back), by_group(ahead), padded_cot,
        padded_images, first, normed_b, mixed, qkv, router_low, gains, weights_low,
        attn_momentum.reshape(attn_rows, TILE), attn_weights.reshape(attn_rows, TILE),
        directions[0], expert_weights, scale, flat.shape[0], 2,
    )
    expert_new = run_last(scale, made, product, directions[1], expert_weights)
    block_out = drop_padding(
        first + ahead_total.reshape(images, image_rows, width).astype(f32)
    )
    input_grad = drop_padding(input_grad)
    attn_sum = sums[:attn_rows].reshape(attn_weights.shape)
    router_sum = sums[attn_rows : attn_rows + EXPERTS, :small_lanes].T
    norm_sum = sums[attn_rows + EXPERTS : attn_rows + small_rows, :small_lanes]
    attn_mom = momentum_decay * attn_momentum + attn_sum
    attn_new = attn_new.reshape(attn_weights.shape)

    router_first_new, router_second_new, router_new = adamw_update(
        router_weight, router_first, router_second, router_sum, router_rate, router_decay
    )
    norm_first_new, norm_second_new, norm_new = adamw_update(
        norm_params, norm_first, norm_second, norm_sum, gains_rate, 0.0
    )
    return (
        block_out,
        input_grad,
        attn_mom,
        attn_new,
        router_first_new,
        router_second_new,
        router_new,
        expert_mom,
        expert_new,
        norm_first_new,
        norm_second_new,
        norm_new,
    )


def solution(mesh):
    in_specs = (
        P((DP, TENSOR), None),
        P(TENSOR, DP, HEADS),
        P(TENSOR, DP, HEADS),
        P((DP, TENSOR), None),
        P((DP, TENSOR), None),
        P((DP, TENSOR), None),
        P((HEADS, DP), None, TENSOR),
        P((HEADS, DP), None, TENSOR),
        P(None, (DP, TENSOR)),
        P(None, (DP, TENSOR)),
        P(None, (DP, TENSOR)),
        P(DP, None),
        P((DP, TENSOR), None),
    )
    out_specs = (
        P((DP, TENSOR), None),
        P((DP, TENSOR), None),
        P(TENSOR, DP, HEADS),
        P(TENSOR, DP, HEADS),
        P((DP, TENSOR), None),
        P((DP, TENSOR), None),
        P((DP, TENSOR), None),
        P((HEADS, DP), None, TENSOR),
        P((HEADS, DP), None, TENSOR),
        P(None, (DP, TENSOR)),
        P(None, (DP, TENSOR)),
        P(None, (DP, TENSOR)),
    )
    shape = dict(mesh.shape)
    step = EXPERTS * 2 // (shape[HEADS] * shape[DP])
    fits = shape[DP] == 2 and shape[HEADS] == 4 and step % (2 * shape[TENSOR]) == 0
    fits = fits and step == 2 * shape[TENSOR] and shape[TENSOR] % 2 == 0
    shards = shards_fast if fits else shards_general
    return jax.shard_map(shards, mesh=mesh, in_specs=in_specs, out_specs=out_specs, check_vma=False)
```
